128 devices in a mesh: dp: 2 (over x_hi), seq: 8 (over x_lo, y), tensor: 8 (over z, core).
Axes of the slice: x: 4 (x_hi: 2, x_lo: 2; x = x_hi * 2 + x_lo), y: 4, z: 4, core: 2. Of those that a mesh axis runs over, the one named last changes fastest.
Arguments:
- inputs: bfloat16 [8, 2048, 1024], P('dp', 'seq'), may hold values from -6 to 6
- w_qkv: bfloat16 [2, 1024, 3, 1024], P(None, ('dp', 'seq'), None, 'tensor'), may hold values from -0.1875 to 0.1875
- w_dense: bfloat16 [2, 1024, 1024], P(None, ('dp', 'seq'), 'tensor'), may hold values from -0.75 to 0.75
- w_fc1: bfloat16 [2, 1024, 4096], P(None, ('dp', 'seq'), 'tensor'), may hold values from -0.1875 to 0.1875
- w_fc2: bfloat16 [2, 1024, 4096], P(None, ('dp', 'seq'), 'tensor'), may hold values from -0.09375 to 0.09375
- norm_gain: bfloat16 [2, 2048], P(None, ('dp', 'seq')), may hold values from 0.5 to 1.5
- biases: bfloat16 [2, 11264], P(None, ('dp', 'seq')), may hold values from -1.75 to 1.75
- segment_ids: int32 [8, 2048], P('dp'), may hold values from 0 to 4, as said below
- cotangent: bfloat16 [8, 2048, 1024], P('dp', 'seq', 'tensor'), may hold values from -6 to 6
Outputs:
- block_out: bfloat16 [8, 2048, 1024], P('dp', 'seq')
- grad_inputs: float32 [8, 2048, 1024], P('dp', 'seq', 'tensor')
- grad_w_qkv: float32 [2, 1024, 3, 1024], P(None, ('dp', 'seq'), None, 'tensor')
- grad_w_dense: float32 [2, 1024, 1024], P(None, ('dp', 'seq'), 'tensor')
- grad_w_fc1: float32 [2, 1024, 4096], P(None, ('dp', 'seq'), 'tensor')
- grad_w_fc2: float32 [2, 1024, 4096], P(None, ('dp', 'seq'), 'tensor')
- grad_norm_gain: float32 [2, 2048], P(None, ('dp', 'seq'))
- grad_biases: float32 [2, 11264], P(None, ('dp', 'seq'))
The draws below stay inside these ranges and needn't reach their ends.
Inputs may be any that keep to these rules, and one draw needn't show every extreme that they name: `segment_ids`: along each sequence the ids never fall, and the positions of one id are one document. Of each aligned block of 4 sequences exactly one is a single document; every other sequence ends with id 4.
All inputs are finite; a program needn't handle non-finite values.
Results may differ from the reference program's by a relative error of at most 0.025.
Values may be sent and summed in bfloat16 or wider, within the bound.
No kernel may reach another device: no remote copies, remote signals or barrier semaphores. Data moves between devices by JAX's collectives and lax.ppermute only.
A program may use at most 256 MiB of HBM per device.

```python
import jax
import jax.numpy as jnp
from jax import lax

D = 1024
FF = 4096
HEADS = 16
HEAD = 64
ROT = 16
LAYERS = 2
MICRO = 2
SEQ_LEN = 2048
CUTS = 4
SEQS_MB = 2
BATCH = 8


def draw_segment_ids(key, part):
    key = jax.random.fold_in(key, 7)
    cut_key, pick_key = jax.random.split(key)
    boundary = jax.random.randint(cut_key, (BATCH, CUTS), 1, SEQ_LEN)
    group_size = MICRO * SEQS_MB
    picked = jax.random.randint(pick_key, (BATCH // group_size,), 0, group_size)
    single_doc = jnp.arange(BATCH) % group_size == jnp.repeat(picked, group_size)
    positions = jnp.arange(SEQ_LEN)
    doc_ids = jnp.sum((boundary[:, :, None] <= positions[None, None, :]).astype(jnp.int32), axis=1)
    return jnp.where(single_doc[:, None], 0, doc_ids).astype(jnp.int32)


def block_levels(stream_key, dims, cuts, least, high):
    level = 1.0
    for position, blocks in cuts:
        draws = jax.random.uniform(jax.random.fold_in(jax.random.fold_in(stream_key, 6), position), (blocks,), jnp.float32, least / len(cuts), high / len(cuts))
        level = level * jnp.repeat(jnp.exp(draws), dims[position] // blocks).reshape((-1,) + (1,) * (len(dims) - 1 - position))
    return level


def bell_draw(stream_key, shape, spread, reach, cuts=(), held_as=jnp.bfloat16):
    factor_of = block_levels(stream_key, shape, cuts, -0.22, 0.18) if cuts else 1.0
    drawn = jax.random.normal(stream_key, shape, jnp.float32) * spread * factor_of
    return jnp.minimum(jnp.maximum(drawn, -reach), reach).astype(held_as)


def setup_inputs(seed: int = 0) -> dict:
    seeds = jax.random.split(jax.random.key(seed), 10)
    return {
        "inputs": bell_draw(seeds[0], (BATCH, SEQ_LEN, D), 1.0, 6.0, ((0, 2), (1, 8))),
        "w_qkv": bell_draw(seeds[1], (LAYERS, D, 3, D), D ** -0.5, 0.1875, ((1, 16), (3, 8))),
        "w_dense": bell_draw(seeds[2], (LAYERS, D, D), (D // 16) ** -0.5, 0.75, ((1, 16), (2, 8))),
        "w_fc1": bell_draw(seeds[3], (LAYERS, D, FF), D ** -0.5, 0.1875, ((1, 16), (2, 8))),
        "w_fc2": bell_draw(seeds[4], (LAYERS, D, FF), FF ** -0.5, 0.09375, ((1, 16), (2, 8))),
        "norm_gain": jnp.clip(1.0 + 0.1 * jax.random.normal(seeds[5], (LAYERS, 2 * D), jnp.float32), 0.5, 1.5).astype(jnp.bfloat16),
        "biases": bell_draw(seeds[6], (LAYERS, 7 * D + FF), 0.3, 1.75, ((1, 16),)),
        "segment_ids": draw_segment_ids(jax.random.fold_in(seeds[9], 71), 0),
        "cotangent": bell_draw(seeds[8], (BATCH, SEQ_LEN, D), 1.0, 6.0, ((0, 2), (1, 8), (2, 8))),
    }


epsilon = 1e-05
highest = lax.Precision.HIGHEST

@jax.custom_vjp
def low(v):
    return lax.optimization_barrier(v.astype(jnp.bfloat16)).astype(jnp.float32)

@jax.custom_vjp
def low_back(v):
    return v

def low_keep(v):
    return (low(v), None)

def low_pass(kept, grad):
    return (grad,)

def back_keep(v):
    return (v, None)

def back_low(kept, grad):
    return (low(grad),)
low.defvjp(low_keep, low_pass)
low_back.defvjp(back_keep, back_low)

def layer_norm(values, gain_vec, shift_vec):
    centred = values - lax.optimization_barrier(jnp.mean(values, axis=-1, keepdims=True))
    variance = lax.optimization_barrier(jnp.mean(centred * centred, axis=-1, keepdims=True))
    return centred * lax.rsqrt(variance + epsilon) * gain_vec + shift_vec

def rotate(values, places):
    half_rot = ROT // 2
    inverse = 10000.0 ** (-jnp.arange(half_rot, dtype=jnp.float32) * 2.0 / ROT)
    angles = places.astype(jnp.float32)[..., None] * inverse
    angles = jnp.concatenate([angles, angles], axis=-1)[..., None, :]
    cosine = jnp.cos(angles)
    sines = jnp.sin(angles)
    turned_part = values[..., :ROT]
    swapped = jnp.concatenate([-turned_part[..., half_rot:], turned_part[..., :half_rot]], axis=-1)
    return jnp.concatenate([turned_part * cosine + swapped * sines, values[..., ROT:]], axis=-1)

def token_places(segments):
    earlier = lax.optimization_barrier(jnp.sum((segments[:, None, :] < segments[:, :, None]).astype(jnp.int32), axis=-1))
    return jnp.arange(segments.shape[1], dtype=jnp.int32)[None, :] - earlier

def attend_one(packed):
    queries, keys, values, segments = packed
    scores = jnp.einsum('qhe,khe->hqk', queries, keys, precision=highest) * HEAD ** (-0.5)
    scores = low_back(scores)
    row_index = jnp.arange(segments.shape[0], dtype=jnp.int32)
    allowed = (segments[:, None] == segments[None, :]) & (row_index[None, :] <= row_index[:, None])
    scores = jnp.where(allowed[None], scores, -1e+30)
    largest = lax.optimization_barrier(jnp.max(scores, axis=-1, keepdims=True))
    exponent = jnp.exp(scores - largest)
    attn_probs = low(exponent / lax.optimization_barrier(jnp.sum(exponent, axis=-1, keepdims=True)))
    return jnp.einsum('hqk,khe->qhe', attn_probs, values, precision=highest)

def block(residual, qkv_weight, dense_weight, fc1_weight, fc2_weight, gain_vec, bias_vec, places, segments):
    normed_one = low(layer_norm(residual, gain_vec[:D], bias_vec[:D]))
    normed_two = low(layer_norm(residual, gain_vec[D:], bias_vec[D:2 * D]))
    qkv_bias = bias_vec[2 * D:5 * D].reshape(3, D)
    dense_bias = bias_vec[5 * D:6 * D]
    fc1_bias = bias_vec[6 * D:6 * D + FF]
    fc2_bias = bias_vec[6 * D + FF:]
    projected = low_back(jnp.einsum('bsd,dke->bske', normed_one, qkv_weight, precision=highest) + qkv_bias)
    head_shape = (residual.shape[0], residual.shape[1], HEADS, HEAD)
    queries = low(rotate(projected[:, :, 0].reshape(head_shape), places))
    keys = low(rotate(projected[:, :, 1].reshape(head_shape), places))
    values = low(projected[:, :, 2].reshape(head_shape))
    attended = lax.map(jax.checkpoint(attend_one), (queries, keys, values, segments))
    attended = low(low_back(attended.reshape(residual.shape)))
    pre_act = low_back(jnp.einsum('bsd,df->bsf', normed_two, fc1_weight, precision=highest) + fc1_bias)
    activated = low(jax.nn.gelu(pre_act, approximate=False))
    branch = jnp.einsum('bsi,oi->bso', attended, dense_weight, precision=highest) + dense_bias
    branch = branch + jnp.einsum('bsf,of->bso', activated, fc2_weight, precision=highest) + fc2_bias
    return residual + low_back(branch)

def reference(inputs, w_qkv, w_dense, w_fc1, w_fc2, norm_gain, biases, segment_ids, cotangent):
    places = token_places(segment_ids)

    def forward(residual, qkv_all, dense_all, fc1_all, fc2_all, gain_all, bias_all):
        for layer_id in range(LAYERS):
            residual = block(residual, qkv_all[layer_id], dense_all[layer_id], fc1_all[layer_id], fc2_all[layer_id], gain_all[layer_id], bias_all[layer_id], places, segment_ids)
        return residual
    result, backward = jax.vjp(forward, inputs.astype(jnp.float32), w_qkv.astype(jnp.float32), w_dense.astype(jnp.float32), w_fc1.astype(jnp.float32), w_fc2.astype(jnp.float32), norm_gain.astype(jnp.float32), biases.astype(jnp.float32))
    gradients = backward(cotangent.astype(jnp.float32))
    return (result.astype(jnp.bfloat16), gradients[0], gradients[1], gradients[2], gradients[3], gradients[4], gradients[5], gradients[6])
```

```python
import math

import jax
import jax.numpy as jnp
from jax import lax
from jax.experimental import pallas as pl
from jax.experimental.pallas import tpu as pltpu
from jax.sharding import PartitionSpec as P

D = 1024
FF = 4096
HEAD = 64
ROT = 16
LAYERS = 2
DOCUMENTS = 5
BLOCK = 256
VMEM_BYTES = 48 * 1024 * 1024
OWNERS = ("dp", "seq")
PLACES = ("seq", "tensor")
ALONG_Z = [[2 * z + core for z in range(4)] for core in range(2)]
ALONG_CORE = [[2 * z + core for core in range(2)] for z in range(4)]

epsilon = 1e-05


def dot(a, b, dims):
    return lax.dot_general(a, b, (dims, ((), ())), preferred_element_type=jnp.float32)


def turned(block, cosine, sines):
    half = ROT // 2
    low, high = (block[:half], block[half:ROT])
    return jnp.concatenate(
        [low * cosine - high * sines, high * cosine + low * sines, block[ROT:]], axis=0
    )


def prepare(packed, table, keys, keys_t, values, blocks):
    queries = []
    half = ROT // 2
    for i in range(blocks):
        cols = slice(i * BLOCK, (i + 1) * BLOCK)
        cosine, sines = (table[:half, cols], table[half:, cols])
        query = turned(packed[i, 0].astype(jnp.float32), cosine, sines).astype(jnp.bfloat16)
        queries.append(query * jnp.bfloat16(HEAD**-0.5))
        key = turned(packed[i, 1].astype(jnp.float32), cosine, sines).astype(jnp.bfloat16)
        keys[cols, :] = key.T
        if keys_t is not None:
            keys_t[:, cols] = key
        if values is not None:
            values[cols, :] = packed[i, 2].T
    return queries


def permitted(i, starts):
    length = (i + 1) * BLOCK
    row = lax.broadcasted_iota(jnp.int32, (length, BLOCK), 0)
    col = lax.broadcasted_iota(jnp.int32, (length, BLOCK), 1) + i * BLOCK
    return (row >= starts) & (row <= col)


def attend_kernel(packed, table, starts, out, wide, log_total, keys, values_t):
    blocks = packed.shape[0]
    queries = prepare(packed, table, keys, None, None, blocks)
    for i in range(blocks):
        values_t[:, i * BLOCK : (i + 1) * BLOCK] = packed[i, 2]
    for i in range(blocks):
        length = (i + 1) * BLOCK
        scores = dot(keys[:length], queries[i], ((1,), (0,)))
        allowed = permitted(i, starts[:, i * BLOCK : length])
        scores = jnp.where(allowed, scores, -1e30)
        largest = jnp.max(scores, axis=0, keepdims=True)
        exponent = jnp.exp(scores - largest)
        total = jnp.sum(exponent, axis=0, keepdims=True)
        result = dot(values_t[:, :length], exponent.astype(jnp.bfloat16), ((1,), (0,)))
        result = result / total
        wide[i] = result
        out[i] = result.astype(jnp.bfloat16)
        log_total[i] = largest + jnp.log(total)


def attend(packed, table, starts):
    blocks = packed.shape[0]
    full = blocks * BLOCK
    return pl.pallas_call(
        attend_kernel,
        out_shape=(
            jax.ShapeDtypeStruct((blocks, HEAD, BLOCK), jnp.bfloat16),
            jax.ShapeDtypeStruct((blocks, HEAD, BLOCK), jnp.float32),
            jax.ShapeDtypeStruct((blocks, 1, BLOCK), jnp.float32),
        ),
        scratch_shapes=[
            pltpu.VMEM((full, HEAD), jnp.bfloat16),
            pltpu.VMEM((HEAD, full), jnp.bfloat16),
        ],
        compiler_params=pltpu.CompilerParams(vmem_limit_bytes=VMEM_BYTES),
        cost_estimate=pl.CostEstimate(
            flops=4 * full * full * HEAD, bytes_accessed=2**21, transcendentals=full * full // 2
        ),
    )(packed, table, starts)


def attend_back_kernel(
    packed, table, starts, wide, log_total, upper, out, keys, keys_t, values, grad_k, grad_v
):
    blocks = packed.shape[0]
    half = ROT // 2
    queries = prepare(packed, table, keys, keys_t, values, blocks)
    for i in range(blocks):
        length = (i + 1) * BLOCK
        cols = slice(i * BLOCK, length)
        scores = dot(keys[:length], queries[i], ((1,), (0,)))
        allowed = permitted(i, starts[:, cols])
        probs = jnp.exp(jnp.where(allowed, scores, -1e30) - log_total[i])
        above = upper[i]
        grad_probs = dot(values[:length], above, ((1,), (0,)))
        row_dot = jnp.sum(above.astype(jnp.float32) * wide[i], axis=0, keepdims=True)
        grad_scores = (probs * (grad_probs - row_dot)).astype(jnp.bfloat16)
        grad_q = dot(keys_t[:, :length], grad_scores, ((1,), (0,))) * HEAD**-0.5
        cosine, sines = (table[:half, cols], table[half:, cols])
        out[i, 0] = turned(grad_q, cosine, -sines).astype(jnp.bfloat16)
        probs_low = probs.astype(jnp.bfloat16)
        part_v = dot(above, probs_low, ((1,), (1,)))
        part_k = dot(queries[i], grad_scores, ((1,), (1,)))
        if i > 0:
            grad_v[:, : i * BLOCK] += part_v[:, : i * BLOCK]
            grad_k[:, : i * BLOCK] += part_k[:, : i * BLOCK]
        grad_v[:, cols] = part_v[:, cols]
        grad_k[:, cols] = part_k[:, cols]
    for i in range(blocks):
        cols = slice(i * BLOCK, (i + 1) * BLOCK)
        cosine, sines = (table[:half, cols], table[half:, cols])
        out[i, 1] = turned(grad_k[:, cols], cosine, -sines).astype(jnp.bfloat16)
        out[i, 2] = grad_v[:, cols].astype(jnp.bfloat16)


def attend_back(packed, table, starts, wide, log_total, upper):
    blocks = packed.shape[0]
    full = blocks * BLOCK
    return pl.pallas_call(
        attend_back_kernel,
        out_shape=jax.ShapeDtypeStruct((blocks, 3, HEAD, BLOCK), jnp.bfloat16),
        scratch_shapes=[
            pltpu.VMEM((full, HEAD), jnp.bfloat16),
            pltpu.VMEM((HEAD, full), jnp.bfloat16),
            pltpu.VMEM((full, HEAD), jnp.bfloat16),
            pltpu.VMEM((HEAD, full), jnp.float32),
            pltpu.VMEM((HEAD, full), jnp.float32),
        ],
        compiler_params=pltpu.CompilerParams(vmem_limit_bytes=VMEM_BYTES),
        cost_estimate=pl.CostEstimate(
            flops=10 * full * full * HEAD, bytes_accessed=2**22, transcendentals=full * full // 2
        ),
    )(packed, table, starts, wide, log_total, upper)


def exchange(blocks, axis, groups=None):
    return lax.all_to_all(blocks, axis, 0, 0, tiled=True, axis_index_groups=groups)


def sent_to_all(shard, axis, groups=None):
    size = lax.axis_size(axis) if groups is None else len(groups[0])
    return exchange(jnp.broadcast_to(shard, (size, *shard.shape)), axis, groups)


def gathered(shard):
    return sent_to_all(sent_to_all(shard, "tensor", ALONG_Z), "tensor", ALONG_CORE)


def summed_share(blocks):
    halves = exchange(blocks.astype(jnp.bfloat16), "tensor", ALONG_CORE).astype(jnp.float32)
    half = (halves[0] + halves[1]).astype(jnp.bfloat16)
    return jnp.sum(exchange(half, "tensor", ALONG_Z).astype(jnp.float32), axis=0)


def gathered_tokens(own):
    every = gathered(own).reshape(2, 4, 4, 32, own.shape[-1])
    return every.transpose(2, 1, 0, 3, 4).reshape(-1, own.shape[-1])


def summed_tokens(partial):
    width = partial.shape[-1]
    blocks = partial.reshape(4, 4, 2, 32, width).transpose(2, 1, 0, 3, 4)
    return summed_share(blocks).reshape(-1, width)


def own_rows(tokens, rank):
    width = tokens.shape[-1]
    rows = lax.dynamic_index_in_dim(tokens.reshape(4, 8, 32, width), rank, 1, False)
    return rows.reshape(-1, width)


def normalised(values):
    centred = values - jnp.mean(values, axis=-1, keepdims=True)
    variance = jnp.mean(centred * centred, axis=-1, keepdims=True)
    scale = lax.rsqrt(variance + epsilon)
    return centred * scale, scale


def norm_back(grad, hat, scale):
    mean = jnp.mean(grad, axis=-1, keepdims=True)
    along = jnp.mean(grad * hat, axis=-1, keepdims=True)
    return scale * (grad - mean - hat * along)


def gelu_and_slope(values):
    share = 0.5 * (1.0 + lax.erf(values * math.sqrt(0.5)))
    slope = share + values * jnp.exp(-0.5 * values * values) * (1.0 / math.sqrt(2.0 * math.pi))
    return (values * share).astype(jnp.bfloat16), slope


def low(values):
    return values.astype(jnp.bfloat16)


def shards(inputs, w_qkv, w_dense, w_fc1, w_fc2, norm_gain, biases, segment_ids, cotangent):
    tensor_rank = lax.axis_index("tensor")
    seq_rank = lax.axis_index("seq")
    owners = 16
    full_len = segment_ids.shape[1]
    head_cols = w_qkv.shape[3]
    hidden_cols = w_fc1.shape[2]
    share = w_qkv.shape[1]
    gain_share = norm_gain.shape[1]
    bias_share = biases.shape[1]
    mine = jnp.arange(8) == tensor_rank

    qkv_flat = w_qkv.reshape(LAYERS, share, 3 * head_cols)
    vectors = jnp.concatenate([norm_gain, biases], axis=1).reshape(-1)
    rows = 16
    vectors = jnp.pad(vectors, (0, rows * 3 * head_cols - vectors.size)).reshape(rows, -1)
    first = sent_to_all(jnp.concatenate([qkv_flat[0], vectors], axis=0), OWNERS)
    qkv_zero = first[:, :share].reshape(D, 3 * head_cols)
    vectors = first[:, share:].reshape(owners, -1)[:, : LAYERS * (gain_share + bias_share)]
    vectors = vectors.reshape(owners, LAYERS, -1).astype(jnp.float32)
    gain_vecs = [vectors[:, l, :gain_share].reshape(-1) for l in range(LAYERS)]
    bias_vecs = [vectors[:, l, gain_share:].reshape(-1) for l in range(LAYERS)]

    both_fc = lax.all_gather(
        jnp.concatenate([w_fc1[0], w_fc2[0]], axis=1), OWNERS, axis=0, tiled=True
    )
    dense_whole = lax.all_gather(w_dense[0], (*OWNERS, "tensor"), axis=0, tiled=True)
    dense_whole = dense_whole.reshape(owners, 8, share, head_cols).transpose(0, 2, 1, 3)
    dense_whole = dense_whole.reshape(D, D)
    later = lax.all_gather(
        jnp.concatenate([qkv_flat[1], w_dense[1], w_fc1[1], w_fc2[1]], axis=1),
        OWNERS,
        axis=0,
        tiled=True,
    )
    ends = [3 * head_cols, 4 * head_cols, 4 * head_cols + hidden_cols]
    qkv_one, dense_one, fc1_one, fc2_one = jnp.split(later, ends, axis=1)
    qkv_weights = [qkv_zero, qkv_one]
    fc1_weights = [both_fc[:, :hidden_cols], fc1_one]
    fc2_weights = [both_fc[:, hidden_cols:], fc2_one]

    gains, shifts, qkv_biases, fc1_biases, outer_biases = ([], [], [], [], [])
    for l in range(LAYERS):
        vec = bias_vecs[l]
        gains.append((gain_vecs[l][:D], gain_vecs[l][D:]))
        shifts.append((vec[:D], vec[D : 2 * D]))
        qkv_biases.append(
            lax.dynamic_index_in_dim(vec[2 * D : 5 * D].reshape(3, 8, -1), tensor_rank, 1, False)
        )
        fc1_biases.append(
            lax.dynamic_index_in_dim(vec[6 * D : 6 * D + FF].reshape(8, -1), tensor_rank, 0, False)
        )
        outer_biases.append(vec[5 * D : 6 * D] + vec[6 * D + FF :])

    segments = lax.dynamic_index_in_dim(segment_ids, seq_rank // 2, 0, False)
    earlier = jnp.zeros_like(segments)
    for doc in range(1, DOCUMENTS):
        before = jnp.sum((segments < doc).astype(jnp.int32))
        earlier = jnp.where(segments == doc, before, earlier)
    places = jnp.arange(full_len, dtype=jnp.int32) - earlier
    half_rot = ROT // 2
    inverse = 10000.0 ** (-jnp.arange(half_rot, dtype=jnp.float32) * 2.0 / ROT)
    angles = inverse[:, None] * places.astype(jnp.float32)[None, :]
    table = jnp.concatenate([jnp.cos(angles), jnp.sin(angles)], axis=0)
    starts = earlier[None, :]

    def project(normed, l):
        weight = qkv_weights[l]
        flat = dot(weight, normed, ((0,), (1,)))
        flat = low(flat + qkv_biases[l].reshape(-1)[:, None])
        blocks = flat.reshape(3, 2, HEAD, 4, BLOCK).transpose(3, 1, 0, 2, 4)
        return exchange(blocks.reshape(8, 3, HEAD, BLOCK), "seq")

    def to_columns(blocks):
        back = exchange(blocks, "seq").reshape(4, 2, HEAD, BLOCK)
        return back.transpose(1, 2, 0, 3).reshape(2 * HEAD, 4 * BLOCK)

    start = inputs.reshape(-1, D)
    hat_zero, scale_zero = normalised(start.astype(jnp.float32))
    normed = [[low(hat_zero * gains[0][k] + shifts[0][k]) for k in range(2)]]
    attention, attended, hidden, slopes = ([], [], [], [])

    def hidden_of(l):
        pre_act = dot(normed[l][1], fc1_weights[l], ((1,), (0,))) + fc1_biases[l]
        activated, slope = gelu_and_slope(pre_act)
        hidden.append(activated)
        slopes.append(slope)

    packed = project(normed[0][0], 0)
    hidden_of(0)
    branch = summed_tokens(dot(hidden[0], fc2_weights[0], ((1,), (1,))))
    result, wide, log_total = attend(packed, table, starts)
    attention.append((packed, wide, log_total))
    sent = result.reshape(8, HEAD, 8, 32).transpose(0, 2, 3, 1).reshape(64, 16, 2 * HEAD)
    heads = exchange(sent, PLACES).reshape(4, 2, 8, 32, HEAD)
    heads = heads.transpose(0, 3, 2, 1, 4).reshape(-1, D)
    attended.append(to_columns(result))
    residual = own_rows(start, tensor_rank).astype(jnp.float32)
    residual = residual + (dot(heads, dense_whole, ((1,), (1,))) + branch + outer_biases[0])

    hat_one, scale_one = normalised(residual)
    hat_low = gathered_tokens(low(hat_one)).astype(jnp.float32)
    normed.append([low(hat_low * gains[1][k] + shifts[1][k]) for k in range(2)])
    packed = project(normed[1][0], 1)
    hidden_of(1)
    result, wide, log_total = attend(packed, table, starts)
    attention.append((packed, wide, log_total))
    attended.append(to_columns(result))
    partial = dot(attended[1], dense_one, ((0,), (1,)))
    partial = partial + dot(hidden[1], fc2_weights[1], ((1,), (1,)))
    final = residual + (summed_tokens(partial) + outer_biases[1])
    block_out = gathered_tokens(low(final)).reshape(inputs.shape)

    grad_low = gathered(cotangent.reshape(-1, cotangent.shape[-1]))
    grad_low = grad_low.transpose(2, 1, 0, 3).reshape(-1, D)
    grad_own = own_rows(grad_low, tensor_rank).astype(jnp.float32)
    flat_grads, small = ([None] * LAYERS, [None] * LAYERS)
    for l in reversed(range(LAYERS)):
        grad_own_low = low(grad_own)
        if l < LAYERS - 1:
            grad_low = gathered_tokens(grad_own_low)
            upper = low(dot(grad_own_low, dense_whole, ((1,), (0,))))
            upper = upper.reshape(4, 32, 8, 2, HEAD).transpose(0, 3, 2, 1, 4)
            upper = exchange(upper.reshape(64, 16, 2 * HEAD), PLACES)
            upper = upper.reshape(8, 8, 32, HEAD).transpose(0, 3, 1, 2)
            upper = upper.reshape(8, HEAD, BLOCK)
        else:
            upper = low(dot(dense_one, grad_low, ((0,), (1,))))
            upper = upper.reshape(2, HEAD, 4, BLOCK).transpose(2, 0, 1, 3)
            upper = exchange(upper.reshape(8, HEAD, BLOCK), "seq")
        grad_dense = dot(grad_low, attended[l], ((0,), (1,)))
        grad_fc2 = dot(grad_low, hidden[l], ((0,), (0,)))
        grad_pre = low(dot(grad_low, fc2_weights[l], ((1,), (0,))) * slopes[l])
        grad_fc1 = dot(normed[l][1], grad_pre, ((0,), (0,)))
        grad_two = dot(grad_pre, fc1_weights[l], ((1,), (1,)))
        packed, wide, log_total = attention[l]
        grad_heads = exchange(attend_back(packed, table, starts, wide, log_total, upper), "seq")
        grad_heads = grad_heads.reshape(4, 2, 3, HEAD, BLOCK).transpose(2, 1, 3, 0, 4)
        grad_heads = grad_heads.reshape(3 * head_cols, 4 * BLOCK)
        grad_qkv = dot(normed[l][0], grad_heads, ((0,), (1,)))
        grad_one = dot(grad_heads, qkv_weights[l], ((0,), (1,)))
        combined = grad_one * gains[l][0] + grad_two * gains[l][1]
        if l > 0:
            grad_own = grad_own + norm_back(summed_tokens(combined), hat_one, scale_one)
        else:
            change = norm_back(combined, hat_zero, scale_zero)
            blocks = change.reshape(-1, 4, 2, D // 8).transpose(2, 1, 0, 3)
            columns = lax.dynamic_slice_in_dim(grad_low, tensor_rank * (D // 8), D // 8, 1)
            grad_inputs = columns.astype(jnp.float32) + summed_share(blocks)
            grad_inputs = grad_inputs.reshape(cotangent.shape)
        if l > 0:
            both = jnp.concatenate(
                [low(grad_qkv), low(grad_dense), low(grad_fc1), low(grad_fc2)], axis=1
            )
            both = lax.psum_scatter(both, OWNERS, scatter_dimension=0, tiled=True)
            flat_grads[l] = jnp.split(both.astype(jnp.float32), ends, axis=1)
        else:
            both = jnp.concatenate([low(grad_dense), low(grad_fc1), low(grad_fc2)], axis=1)
            both = lax.psum_scatter(both, OWNERS, scatter_dimension=0, tiled=True)
            others = jnp.split(
                both.astype(jnp.float32), [head_cols, head_cols + hidden_cols], axis=1
            )
            tiles = exchange(low(grad_qkv).reshape(owners, share, -1), OWNERS)
            flat_grads[l] = [jnp.sum(tiles.astype(jnp.float32), axis=0), *others]
        head_sums = jnp.sum(grad_heads.astype(jnp.float32), axis=1)
        pre_sums = jnp.sum(grad_pre.astype(jnp.float32), axis=0)
        own_sums = jnp.sum(grad_own_low.astype(jnp.float32), axis=0)
        shift_grads, gain_grads = ([], [])
        for k, (weight, grad_weight, sums) in enumerate(
            ((qkv_weights[l], grad_qkv, head_sums), (fc1_weights[l], grad_fc1, pre_sums))
        ):
            wide_weight = weight.astype(jnp.float32)
            shift_grad = jnp.sum(wide_weight * sums, axis=1)
            product = jnp.sum(wide_weight * grad_weight, axis=1)
            shift_grads.append(shift_grad)
            gain_grads.append((product - shifts[l][k] * shift_grad) / gains[l][k])
        placed_heads = jnp.where(mine[:, None], head_sums.reshape(3, 1, head_cols), 0.0)
        placed_pre = jnp.where(mine[:, None], pre_sums[None, :], 0.0)
        bias_grad = jnp.concatenate(
            [*shift_grads, placed_heads.reshape(-1), own_sums, placed_pre.reshape(-1), own_sums]
        )
        small[l] = jnp.concatenate(
            [
                bias_grad.reshape(owners, bias_share),
                jnp.concatenate(gain_grads).reshape(owners, gain_share),
            ],
            axis=1,
        )
    small = jnp.sum(exchange(jnp.concatenate(small, axis=1), OWNERS), axis=0)
    small = jnp.sum(sent_to_all(small, "tensor"), axis=0).reshape(LAYERS, -1)
    stacked = [jnp.stack([flat_grads[l][k] for l in range(LAYERS)]) for k in range(4)]
    return (
        block_out,
        grad_inputs,
        stacked[0].reshape(w_qkv.shape),
        stacked[1],
        stacked[2],
        stacked[3],
        small[:, bias_share:],
        small[:, :bias_share],
    )


def solution(mesh):
    in_specs = (
        P("dp", "seq", None),
        P(None, ("dp", "seq"), None, "tensor"),
        P(None, ("dp", "seq"), "tensor"),
        P(None, ("dp", "seq"), "tensor"),
        P(None, ("dp", "seq"), "tensor"),
        P(None, ("dp", "seq")),
        P(None, ("dp", "seq")),
        P("dp", None),
        P("dp", "seq", "tensor"),
    )
    out_specs = (
        P("dp", "seq", None),
        P("dp", "seq", "tensor"),
        P(None, ("dp", "seq"), None, "tensor"),
        P(None, ("dp", "seq"), "tensor"),
        P(None, ("dp", "seq"), "tensor"),
        P(None, ("dp", "seq"), "tensor"),
        P(None, ("dp", "seq")),
        P(None, ("dp", "seq")),
    )
    return jax.shard_map(shards, mesh=mesh, in_specs=in_specs, out_specs=out_specs, check_vma=False)
```

```python
import math

import jax
import jax.numpy as jnp
from jax import lax
from jax.experimental import pallas as pl
from jax.experimental.pallas import tpu as pltpu
from jax.sharding import PartitionSpec as P

D = 1024
FF = 4096
HEAD = 64
ROT = 16
LAYERS = 2
DOCUMENTS = 5
BLOCK = 256
VMEM_BYTES = 48 * 1024 * 1024
OWNERS = ("dp", "seq")
ACROSS = [(2 * z + core, 2 * z + 1 - core) for z in range(4) for core in range(2)]

epsilon = 1e-05


def dot(a, b, dims):
    return lax.dot_general(a, b, (dims, ((), ())), preferred_element_type=jnp.float32)


def turned(block, cosine, sines):
    half = ROT // 2
    low, high = (block[:half], block[half:ROT])
    return jnp.concatenate(
        [low * cosine - high * sines, high * cosine + low * sines, block[ROT:]], axis=0
    )


def in_order(block, flip):
    half = block.shape[-1] // 2
    other = jnp.concatenate([block[..., half:], block[..., :half]], axis=-1)
    return jnp.where(flip, other, block)


def prepare(packed, table, keys, keys_t, values, values_t, blocks, flip):
    queries = []
    half = ROT // 2
    for i in range(blocks):
        cols = slice(i * BLOCK, (i + 1) * BLOCK)
        cosine, sines = (table[:half, cols], table[half:, cols])
        query = in_order(packed[i, 0].astype(jnp.float32), flip)
        query = turned(query, cosine, sines).astype(jnp.bfloat16)
        queries.append(query * jnp.bfloat16(HEAD**-0.5))
        key = in_order(packed[i, 1].astype(jnp.float32), flip)
        key = turned(key, cosine, sines).astype(jnp.bfloat16)
        keys[cols, :] = key.T
        value = in_order(packed[i, 2].astype(jnp.float32), flip).astype(jnp.bfloat16)
        if keys_t is not None:
            keys_t[:, cols] = key
        if values is not None:
            values[cols, :] = value.T
        if values_t is not None:
            values_t[:, cols] = value
    return queries


def permitted(i, starts):
    length = (i + 1) * BLOCK
    row = lax.broadcasted_iota(jnp.int32, (length, BLOCK), 0)
    col = lax.broadcasted_iota(jnp.int32, (length, BLOCK), 1) + i * BLOCK
    return (row >= starts) & (row <= col)


def attend_kernel(core, packed, table, starts, out, wide, log_total, keys, values_t):
    blocks = packed.shape[0]
    flip = core[0] == 1
    queries = prepare(packed, table, keys, None, None, values_t, blocks, flip)
    for i in range(blocks):
        length = (i + 1) * BLOCK
        scores = dot(keys[:length], queries[i], ((1,), (0,)))
        allowed = permitted(i, starts[:, i * BLOCK : length])
        scores = jnp.where(allowed, scores, -1e30)
        largest = jnp.max(scores, axis=0, keepdims=True)
        exponent = jnp.exp(scores - largest)
        total = jnp.sum(exponent, axis=0, keepdims=True)
        result = dot(values_t[:, :length], exponent.astype(jnp.bfloat16), ((1,), (0,)))
        result = result / total
        wide[i] = result
        out[i] = in_order(result, flip).astype(jnp.bfloat16)
        log_total[i] = largest + jnp.log(total)


SCALAR = pl.BlockSpec(memory_space=pltpu.SMEM)
WHOLE = pl.BlockSpec(memory_space=pltpu.VMEM)


def attend(core, packed, table, starts, work=()):
    blocks = packed.shape[0]
    full = blocks * BLOCK
    return pl.pallas_call(
        skipping(attend_kernel, 4, len(work)),
        out_shape=(
            jax.ShapeDtypeStruct((blocks, HEAD, BLOCK), jnp.bfloat16),
            jax.ShapeDtypeStruct((blocks, HEAD, BLOCK), jnp.float32),
            jax.ShapeDtypeStruct((blocks, 1, BLOCK), jnp.float32),
        ),
        in_specs=[SCALAR] + [WHOLE] * 3 + [UNREAD] * len(work),
        scratch_shapes=[
            pltpu.VMEM((full, HEAD), jnp.bfloat16),
            pltpu.VMEM((HEAD, full), jnp.bfloat16),
        ],
        compiler_params=pltpu.CompilerParams(vmem_limit_bytes=VMEM_BYTES),
        cost_estimate=pl.CostEstimate(
            flops=4 * full * full * HEAD, bytes_accessed=2**21, transcendentals=full * full // 2
        ),
    )(core, packed, table, starts, *work)


def attend_back_kernel(
    core, packed, table, starts, wide, log_total, upper, out, keys, keys_t, values, grad_k, grad_v
):
    blocks = packed.shape[0]
    half = ROT // 2
    flip = core[0] == 1
    queries = prepare(packed, table, keys, keys_t, values, None, blocks, flip)
    for i in range(blocks):
        length = (i + 1) * BLOCK
        cols = slice(i * BLOCK, length)
        scores = dot(keys[:length], queries[i], ((1,), (0,)))
        allowed = permitted(i, starts[:, cols])
        probs = jnp.exp(jnp.where(allowed, scores, -1e30) - log_total[i])
        above = in_order(upper[i].astype(jnp.float32), flip).astype(jnp.bfloat16)
        grad_probs = dot(values[:length], above, ((1,), (0,)))
        row_dot = jnp.sum(above.astype(jnp.float32) * wide[i], axis=0, keepdims=True)
        grad_scores = (probs * (grad_probs - row_dot)).astype(jnp.bfloat16)
        grad_q = dot(keys_t[:, :length], grad_scores, ((1,), (0,))) * HEAD**-0.5
        cosine, sines = (table[:half, cols], table[half:, cols])
        out[i, 0] = in_order(turned(grad_q, cosine, -sines), flip).astype(jnp.bfloat16)
        probs_low = probs.astype(jnp.bfloat16)
        part_v = dot(above, probs_low, ((1,), (1,)))
        part_k = dot(queries[i], grad_scores, ((1,), (1,)))
        if i > 0:
            grad_v[:, : i * BLOCK] += part_v[:, : i * BLOCK]
            grad_k[:, : i * BLOCK] += part_k[:, : i * BLOCK]
        grad_v[:, cols] = part_v[:, cols]
        grad_k[:, cols] = part_k[:, cols]
    for i in range(blocks):
        cols = slice(i * BLOCK, (i + 1) * BLOCK)
        cosine, sines = (table[:half, cols], table[half:, cols])
        out[i, 1] = in_order(turned(grad_k[:, cols], cosine, -sines), flip).astype(jnp.bfloat16)
        out[i, 2] = in_order(grad_v[:, cols], flip).astype(jnp.bfloat16)


def attend_back(core, packed, table, starts, wide, log_total, upper, work=()):
    blocks = packed.shape[0]
    full = blocks * BLOCK
    return pl.pallas_call(
        skipping(attend_back_kernel, 7, len(work)),
        out_shape=jax.ShapeDtypeStruct((blocks, 3, HEAD, BLOCK), jnp.bfloat16),
        in_specs=[SCALAR] + [WHOLE] * 6 + [UNREAD] * len(work),
        scratch_shapes=[
            pltpu.VMEM((full, HEAD), jnp.bfloat16),
            pltpu.VMEM((HEAD, full), jnp.bfloat16),
            pltpu.VMEM((full, HEAD), jnp.bfloat16),
            pltpu.VMEM((HEAD, full), jnp.float32),
            pltpu.VMEM((HEAD, full), jnp.float32),
        ],
        compiler_params=pltpu.CompilerParams(vmem_limit_bytes=VMEM_BYTES),
        cost_estimate=pl.CostEstimate(
            flops=10 * full * full * HEAD, bytes_accessed=2**22, transcendentals=full * full // 2
        ),
    )(core, packed, table, starts, wide, log_total, upper, *work)


def exchange(blocks, axis, groups=None):
    return lax.all_to_all(blocks, axis, 0, 0, tiled=True, axis_index_groups=groups)


def sent_to_all(shard, axis, groups=None):
    size = lax.axis_size(axis) if groups is None else len(groups[0])
    return exchange(jnp.broadcast_to(shard, (size, *shard.shape)), axis, groups)


UNREAD = pl.BlockSpec(memory_space=pl.ANY)


def skipping(kernel, first, count):
    return lambda *refs: kernel(*refs[:first], *refs[first + count :])


def after(value, *work):
    return pl.pallas_call(
        lambda *refs: None,
        out_shape=jax.ShapeDtypeStruct(value.shape, value.dtype),
        in_specs=[UNREAD] * (1 + len(work)),
        out_specs=UNREAD,
        input_output_aliases={0: 0},
        cost_estimate=pl.CostEstimate(flops=0, bytes_accessed=0, transcendentals=0),
    )(value, *work)


def along(distance):
    return [
        (2 * z + core, 2 * ((z + distance) % 4) + core) for z in range(4) for core in range(2)
    ]


def gathered(own):
    mine = jnp.stack([own] + [lax.ppermute(own, "tensor", along(-r)) for r in range(1, 4)])
    return mine, lax.ppermute(mine, "tensor", ACROSS)


def half_sum(halves):
    got = lax.ppermute(halves[1], "tensor", ACROSS)
    return low(halves[0].astype(jnp.float32) + got.astype(jnp.float32))


def z_sum(half):
    total = half[0].astype(jnp.float32)
    for r in range(1, 4):
        total = total + lax.ppermute(half[r], "tensor", along(r)).astype(jnp.float32)
    return total


def summed(halves):
    return z_sum(half_sum(halves))


def swapped(tokens, core):
    halves = tokens.reshape(4, 2, 128, tokens.shape[-1])
    return jnp.where(core == 0, halves, halves[:, ::-1]).reshape(tokens.shape)


def swapped_rows(block, flip):
    half = block.shape[0] // 2
    other = jnp.concatenate([block[half:], block[:half]], axis=0)
    return jnp.where(flip, other, block)


def own_rows(tokens, along_z, half):
    blocks = tokens.reshape(4, 2, 128, tokens.shape[-1])
    return lax.dynamic_index_in_dim(
        lax.dynamic_index_in_dim(blocks, along_z, 0, False), half, 0, False
    )


def in_steps(
    kernel, out_shape, in_specs, out_specs, operands, flops, work=(), scratch=(), alias=None
):
    return pl.pallas_call(
        skipping(kernel, len(operands), len(work)),
        out_shape=out_shape,
        grid_spec=pltpu.PrefetchScalarGridSpec(
            num_scalar_prefetch=1,
            grid=(4,),
            in_specs=[*in_specs, *([UNREAD] * len(work))],
            out_specs=out_specs,
            scratch_shapes=scratch,
        ),
        input_output_aliases={} if alias is None else alias,
        compiler_params=pltpu.CompilerParams(vmem_limit_bytes=VMEM_BYTES),
        cost_estimate=pl.CostEstimate(
            flops=flops, bytes_accessed=2**23 if flops else 2**10, transcendentals=0
        ),
    )(*operands, *work)


def distance_of(b, spot):
    return lax.rem(b - spot[0] + 4, 4)


def columns_of(weight, width, block):
    return pl.BlockSpec((weight.shape[0], width), lambda b, spot: (0, block))


def rows_of(weight, width, block):
    return pl.BlockSpec((BLOCK, width), lambda i, spot: (i, block))


def whole_of(array):
    return pl.BlockSpec(array.shape, lambda i, spot: (0,) * array.ndim)


PIECE = pl.BlockSpec((1, 128, D), lambda b, spot: (distance_of(b, spot), 0, 0))
TOKENS = pl.BlockSpec((BLOCK, D), lambda b, spot: (b, 0))
HALVES = pl.BlockSpec((2, 1, 128, D), lambda b, spot: (0, distance_of(b, spot), 0, 0))
ALL_TOKENS = jax.ShapeDtypeStruct((1024, D), jnp.bfloat16)
ALL_HALVES = jax.ShapeDtypeStruct((2, 4, 128, D), jnp.bfloat16)


def project_block(hat, gain, shift, qkv, bias, one, two, packed):
    first = (hat * gain[0:1] + shift[0:1]).astype(jnp.bfloat16)
    one[...] = first
    two[...] = (hat * gain[1:2] + shift[1:2]).astype(jnp.bfloat16)
    flat = (dot(first, qkv[...], ((1,), (0,))) + bias[...]).T.astype(jnp.bfloat16)
    for k in range(3):
        for j in range(2):
            at = (2 * k + j) * HEAD
            packed[j, k] = flat[at : at + HEAD]


def project_input_kernel(spot, start, gain, shift, qkv, bias, one, two, packed):
    block = swapped_rows(start[...].astype(jnp.float32), spot[1] == 1)
    hat, _ = normalised(block)
    project_block(hat, gain, shift, qkv, bias, one, two, packed)


def project_kernel(spot, mine, other, gain, shift, qkv, bias, one, two, packed):
    hat = jnp.concatenate([mine[0], other[0]], axis=0).astype(jnp.float32)
    project_block(hat, gain, shift, qkv, bias, one, two, packed)


def project(spot, tokens, pair, qkv, bias, work):
    qkv, block = qkv
    kernel = project_input_kernel if len(tokens) == 1 else project_kernel
    return in_steps(
        kernel,
        (ALL_TOKENS, ALL_TOKENS, jax.ShapeDtypeStruct((8, 3, HEAD, BLOCK), jnp.bfloat16)),
        [
            *([TOKENS] if len(tokens) == 1 else [PIECE, PIECE]),
            whole_of(pair[0]),
            whole_of(pair[1]),
            columns_of(qkv, 6 * HEAD, block),
            whole_of(bias),
        ],
        (TOKENS, TOKENS, pl.BlockSpec((2, 3, HEAD, BLOCK), lambda b, spot: (b, 0, 0, 0))),
        (spot, *tokens, *pair, qkv, bias),
        2 * 1024 * 384 * D,
        work,
    )


def out_kernel(spot, hidden, heads, fc2, dense, out):
    result = dot(hidden[...], fc2[...], ((1,), (1,)))
    block = jnp.concatenate([heads[0], heads[1]], axis=0).T
    result = result + dot(block, dense[...], ((1,), (1,)))
    out[0, 0] = result[:128].astype(jnp.bfloat16)
    out[1, 0] = result[128:].astype(jnp.bfloat16)


def branch_sums(spot, hidden, heads, fc2, dense, work=(), flops=2**31):
    (fc2, fc2_block), (dense, dense_block) = (fc2, dense)
    return in_steps(
        out_kernel,
        ALL_HALVES,
        [
            pl.BlockSpec((BLOCK, hidden.shape[1]), lambda b, spot: (b, 0)),
            pl.BlockSpec((2, HEAD, BLOCK), lambda b, spot: (b, 0, 0)),
            columns_of(fc2, hidden.shape[1], fc2_block),
            columns_of(dense, 2 * HEAD, dense_block),
        ],
        HALVES,
        (spot, hidden, heads, fc2, dense),
        flops,
        work,
    )


def to_norms(grad_heads, grad_pre, qkv, fc1, gain):
    block = jnp.concatenate([grad_heads[j, k] for k in range(3) for j in range(2)], axis=0)
    result = dot(block.T, qkv[...], ((1,), (1,))) * gain[0:1]
    return result + dot(grad_pre[...], fc1[...], ((1,), (1,))) * gain[1:2]


def back_kernel(spot, grad_heads, grad_pre, qkv, fc1, gain, out):
    result = to_norms(grad_heads, grad_pre, qkv, fc1, gain)
    out[0, 0] = result[:128].astype(jnp.bfloat16)
    out[1, 0] = result[128:].astype(jnp.bfloat16)


def back_input_kernel(spot, grad_heads, grad_pre, qkv, fc1, gain, start, out, change):
    result = to_norms(grad_heads, grad_pre, qkv, fc1, gain)
    z, core = (spot[0], spot[1])
    hat, scale = normalised(swapped_rows(start[...].astype(jnp.float32), core == 1))
    change[...] = swapped_rows(norm_back(result, hat, scale), core == 1)
    for r in range(4):
        for j in range(2):
            owner = 2 * lax.rem(z + r, 4) + lax.rem(core + j, 2)
            lanes = pl.ds(pl.multiple_of(owner * 128, 128), 128)
            out[j, r] = change[:, lanes].astype(jnp.bfloat16)


def norm_gradient(spot, grad_heads, grad_pre, qkv, fc1, gain, start=None, work=()):
    (qkv, qkv_block), (fc1, fc1_block) = (qkv, fc1)
    width = grad_pre.shape[1]
    in_specs = [
        pl.BlockSpec((2, 3, HEAD, BLOCK), lambda b, spot: (b, 0, 0, 0)),
        pl.BlockSpec((BLOCK, width), lambda b, spot: (b, 0)),
        columns_of(qkv, 6 * HEAD, qkv_block),
        columns_of(fc1, width, fc1_block),
        whole_of(gain),
    ]
    flops = 2 * 1024 * 896 * D
    operands = (spot, grad_heads, grad_pre, qkv, fc1, gain)
    if start is None:
        return in_steps(back_kernel, ALL_HALVES, in_specs, HALVES, operands, flops, work)
    flops = 0
    return in_steps(
        back_input_kernel,
        jax.ShapeDtypeStruct((2, 4, 1024, 128), jnp.bfloat16),
        [*in_specs, TOKENS],
        pl.BlockSpec((2, 4, BLOCK, 128), lambda b, spot: (0, 0, b, 0)),
        (*operands, start),
        flops,
        work,
        [pltpu.VMEM((BLOCK, D), jnp.float32)],
    )


def join_kernel(spot, mine, other, out):
    core = spot[1]
    out[pl.ds(pl.multiple_of(core * 128, 128), 128), :] = mine[0]
    out[pl.ds(pl.multiple_of((1 - core) * 128, 128), 128), :] = other[0]


def joined(spot, mine, other):
    return in_steps(join_kernel, ALL_TOKENS, [PIECE, PIECE], TOKENS, (spot, mine, other), 0)


def head_gradient(block, dense, upper):
    flat = dot(block, dense[...], ((1,), (0,))).T.astype(jnp.bfloat16)
    upper[0] = flat[:HEAD]
    upper[1] = flat[HEAD:]


def gradient_kernel(spot, mine, other, dense, out, upper):
    block = jnp.concatenate([mine[0], other[0]], axis=0)
    out[...] = block
    head_gradient(block, dense, upper)


def columns_kernel(spot, mine, other, dense, out, upper):
    z, core = (spot[0], spot[1])
    for r in range(4):
        for j, pieces in enumerate((mine, other)):
            owner = 2 * lax.rem(z + r, 4) + lax.rem(core + j, 2)
            piece = swapped_rows(pieces[r].astype(jnp.float32), core == 1)
            lanes = pl.ds(pl.multiple_of(owner * 128, 128), 128)
            out[:, lanes] = piece.astype(jnp.bfloat16)
    head_gradient(out[...], dense, upper)


def top_gradient(spot, pieces, dense, work=()):
    dense, block = dense
    kernel, specs = (gradient_kernel, [PIECE, PIECE])
    if pieces[0].shape[2] < D:
        kernel = columns_kernel
        specs = [pl.BlockSpec((4, BLOCK, 128), lambda b, spot: (0, b, 0))] * 2
    return in_steps(
        kernel,
        (ALL_TOKENS, jax.ShapeDtypeStruct((8, HEAD, BLOCK), jnp.bfloat16)),
        [*specs, columns_of(dense, 2 * HEAD, block)],
        (TOKENS, pl.BlockSpec((2, HEAD, BLOCK), lambda b, spot: (b, 0, 0))),
        (spot, *pieces, dense),
        2 * 1024 * 128 * D,
        work,
    )


def as_rows(column):
    return jnp.broadcast_to(column, (column.shape[0], 128)).T[:8]


def norm_sums(weight, grad_weight, sums, product, shift):
    wide = weight.astype(jnp.float32)
    product[...] = as_rows(jnp.sum(wide * grad_weight, axis=1, keepdims=True))
    shift[...] = as_rows(jnp.sum(wide * sums, axis=1, keepdims=True))


def feed_block(normed, grad_low, grad_pre, hidden, fc1, out, product, shift, sums):
    @pl.when(pl.program_id(0) == 0)
    def _():
        total = jnp.sum(grad_pre[...].astype(jnp.float32), axis=0, keepdims=True)
        sums[...] = jnp.broadcast_to(total, sums.shape)

    width = grad_pre.shape[1]
    grad_fc1 = dot(normed[...], grad_pre[...], ((0,), (0,)))
    out[:, :width] = grad_fc1.astype(jnp.bfloat16)
    grad_fc2 = dot(grad_low[...], hidden[...], ((0,), (0,)))
    out[:, width : 2 * width] = grad_fc2.astype(jnp.bfloat16)
    norm_sums(fc1[...], grad_fc1, sums[0:1], product, shift)


def dense_block(grad_low, heads):
    total = 0.0
    for b in range(4):
        block = jnp.concatenate([heads[2 * b], heads[2 * b + 1]], axis=0)
        total = total + dot(block, grad_low[b * BLOCK : (b + 1) * BLOCK], ((1,), (0,)))
    return total.T.astype(jnp.bfloat16)


def heads_block(normed, grad_heads, qkv, out, product, shift, sums, columns):
    @pl.when(pl.program_id(0) == 0)
    def _():
        for b in range(4):
            for k in range(3):
                for j in range(2):
                    at = (2 * k + j) * HEAD
                    columns[at : at + HEAD, b * BLOCK : (b + 1) * BLOCK] = grad_heads[2 * b + j, k]
        wide = columns[...].astype(jnp.float32)
        sums[...] = as_rows(jnp.sum(wide, axis=1, keepdims=True))

    grad_qkv = dot(columns[...], normed[...], ((1,), (0,))).T
    out[:, : 6 * HEAD] = grad_qkv.astype(jnp.bfloat16)
    norm_sums(qkv[...], grad_qkv, sums[0:1], product, shift)


def feed_kernel(spot, *refs):
    feed_block(*refs)


def feed_dense_kernel(
    spot, normed, grad_low, grad_pre, hidden, fc1, heads, more, out, product, shift, sums
):
    feed_block(normed, grad_low, grad_pre, hidden, fc1, out, product, shift, sums)
    at = 2 * grad_pre.shape[1]
    out[:, at : at + 2 * HEAD] = dense_block(grad_low, heads)
    out[:, at + 2 * HEAD :] = more[...]


def heads_kernel(spot, *refs):
    heads_block(*refs)


def heads_dense_kernel(
    spot, normed, grad_heads, qkv, grad_low, heads, out, product, shift, sums, columns
):
    heads_block(normed, grad_heads, qkv, out, product, shift, sums, columns)
    out[:, 6 * HEAD :] = dense_block(grad_low, heads)


FEATURES = pl.BlockSpec((1024, BLOCK), lambda i, spot: (0, i))
ROW = pl.BlockSpec((8, BLOCK), lambda i, spot: (0, i))
ROWS = jax.ShapeDtypeStruct((8, D), jnp.float32)


def weight_gradient(kernel, spot, operands, in_specs, width, summed_width, scratch, work):
    return in_steps(
        kernel,
        (
            jax.ShapeDtypeStruct((D, width), jnp.bfloat16),
            ROWS,
            ROWS,
            jax.ShapeDtypeStruct((8, summed_width), jnp.float32),
        ),
        in_specs,
        (
            pl.BlockSpec((BLOCK, width), lambda i, spot: (i, 0)),
            ROW,
            ROW,
            pl.BlockSpec((8, summed_width), lambda i, spot: (0, 0)),
        ),
        (spot, *operands),
        0,
        work,
        scratch,
    )


def feed_gradient(spot, normed, grad_low, grad_pre, hidden, fc1, heads=None, more=None, work=()):
    width = hidden.shape[1]
    operands = [normed, grad_low, grad_pre, hidden, fc1[0]]
    in_specs = [FEATURES, FEATURES, whole_of(grad_pre), whole_of(hidden)]
    in_specs += [rows_of(fc1[0], width, fc1[1])]
    kernel, total = (feed_kernel, 2 * width)
    if heads is not None:
        operands += [heads, more]
        in_specs += [whole_of(heads), rows_of(more, more.shape[1], 0)]
        kernel, total = (feed_dense_kernel, total + 2 * HEAD + more.shape[1])
    return weight_gradient(kernel, spot, operands, in_specs, total, width, (), work)


def heads_gradient(spot, normed, grad_heads, qkv, grad_low=None, heads=None, work=()):
    width = 6 * HEAD
    operands = [normed, grad_heads, qkv[0]]
    in_specs = [FEATURES, whole_of(grad_heads), rows_of(qkv[0], width, qkv[1])]
    kernel, total = (heads_kernel, width)
    if heads is not None:
        operands += [grad_low, heads]
        in_specs += [FEATURES, whole_of(heads)]
        kernel, total = (heads_dense_kernel, width + 2 * HEAD)
    scratch = [pltpu.VMEM((width, 1024), jnp.bfloat16)]
    return weight_gradient(kernel, spot, operands, in_specs, total, width, scratch, work)


def normalised(values):
    centred = values - jnp.mean(values, axis=-1, keepdims=True)
    variance = jnp.mean(centred * centred, axis=-1, keepdims=True)
    scale = lax.rsqrt(variance + epsilon)
    return centred * scale, scale


def norm_back(grad, hat, scale):
    mean = jnp.mean(grad, axis=-1, keepdims=True)
    along = jnp.mean(grad * hat, axis=-1, keepdims=True)
    return scale * (grad - mean - hat * along)


def gelu_and_slope(values):
    share = 0.5 * (1.0 + lax.erf(values * math.sqrt(0.5)))
    slope = share + values * jnp.exp(-0.5 * values * values) * (1.0 / math.sqrt(2.0 * math.pi))
    return (values * share).astype(jnp.bfloat16), slope


def low(values):
    return values.astype(jnp.bfloat16)


def shards(inputs, w_qkv, w_dense, w_fc1, w_fc2, norm_gain, biases, segment_ids, cotangent):
    tensor_rank = lax.axis_index("tensor")
    seq_rank = lax.axis_index("seq")
    along_z, core = (tensor_rank // 2, tensor_rank % 2)
    core_ref = core.astype(jnp.int32).reshape(1)
    spot = jnp.stack([along_z, core]).astype(jnp.int32)
    owners = 16
    full_len = segment_ids.shape[1]
    head_cols = w_qkv.shape[3]
    hidden_cols = w_fc1.shape[2]
    share = w_qkv.shape[1]
    gain_share = norm_gain.shape[1]
    bias_share = biases.shape[1]
    mine = jnp.arange(8) == tensor_rank

    qkv_flat = w_qkv.reshape(LAYERS, share, 3 * head_cols)
    vectors = jnp.concatenate([norm_gain.reshape(-1), biases.reshape(-1)])
    rows = 16
    vectors = jnp.pad(vectors, (0, rows * 3 * head_cols - vectors.size)).reshape(rows, -1)
    first = sent_to_all(jnp.concatenate([qkv_flat[0], vectors], axis=0), OWNERS)
    both_zero = lax.all_gather(
        jnp.concatenate([w_fc1[0], w_fc2[0], w_dense[0]], axis=1), OWNERS, axis=0, tiled=True
    )
    pieces = gathered(cotangent.reshape(-1, cotangent.shape[-1]))
    heads_one = lax.all_gather(
        jnp.concatenate([qkv_flat[1], w_dense[1]], axis=1), OWNERS, axis=0, tiled=True
    )
    feed_one = lax.all_gather(
        jnp.concatenate([w_fc1[1], w_fc2[1]], axis=1), OWNERS, axis=0, tiled=True
    )
    qkv_zero = first[:, :share].reshape(D, 3 * head_cols)
    vectors = first[:, share:].reshape(owners, -1)[:, : LAYERS * (gain_share + bias_share)]
    gain_vecs = vectors[:, : LAYERS * gain_share].reshape(owners, LAYERS, -1).astype(jnp.float32)
    bias_vecs = vectors[:, LAYERS * gain_share :].reshape(owners, LAYERS, -1).astype(jnp.float32)
    qkv_places = [(qkv_zero, 0), (heads_one, 0)]
    dense_places = [(both_zero, 8), (heads_one, 3)]
    fc1_places = [(both_zero, 0), (feed_one, 0)]
    fc2_places = [(both_zero, 1), (feed_one, 1)]
    fc1_weights = [both_zero[:, :hidden_cols], feed_one[:, :hidden_cols]]
    fc2_weights = [both_zero[:, hidden_cols : 2 * hidden_cols], feed_one[:, hidden_cols:]]

    pairs, qkv_biases, fc1_biases, outer_biases = ([], [], [], [])
    for l in range(LAYERS):
        vec = bias_vecs[:, l].reshape(-1)
        pairs.append((gain_vecs[:, l].reshape(2, D), vec[: 2 * D].reshape(2, D)))
        bias = vec[2 * D : 5 * D].reshape(3, 8, head_cols)
        bias = lax.dynamic_index_in_dim(bias, tensor_rank, 1, False)
        qkv_biases.append(bias.reshape(1, 3 * head_cols))
        bias = vec[6 * D : 6 * D + FF].reshape(8, hidden_cols)
        fc1_biases.append(lax.dynamic_index_in_dim(bias, tensor_rank, 0, True))
        outer_biases.append((vec[5 * D : 6 * D] + vec[6 * D + FF :]).reshape(1, D))

    segments = lax.dynamic_index_in_dim(segment_ids, seq_rank // 2, 0, False)
    earlier = jnp.zeros_like(segments)
    for doc in range(1, DOCUMENTS):
        before = jnp.sum((segments < doc).astype(jnp.int32))
        earlier = jnp.where(segments == doc, before, earlier)
    places = jnp.arange(full_len, dtype=jnp.int32) - earlier
    half_rot = ROT // 2
    inverse = 10000.0 ** (-jnp.arange(half_rot, dtype=jnp.float32) * 2.0 / ROT)
    angles = inverse[:, None] * places.astype(jnp.float32)[None, :]
    table = jnp.concatenate([jnp.cos(angles), jnp.sin(angles)], axis=0)
    starts = earlier[None, :]

    def feed_forward(normed_two, l):
        pre_act = dot(normed_two, fc1_weights[l], ((1,), (0,))) + fc1_biases[l]
        return gelu_and_slope(pre_act)

    def pre_gradient(grad_low, slope, l):
        return low(dot(grad_low, fc2_weights[l], ((1,), (0,))) * slope)

    tokens = inputs.reshape(-1, D)
    residual = own_rows(tokens, along_z, core).astype(jnp.float32)

    one_zero, two_zero, payload = project(
        spot, (tokens,), pairs[0], qkv_places[0], qkv_biases[0], (pieces[1],)
    )
    packed_zero = exchange(payload, "seq")
    prepared = (*pairs[1], qkv_biases[1], fc1_biases[1], outer_biases[0], outer_biases[1])
    result, *kept_zero = attend(core_ref, packed_zero, table, starts, prepared)
    heads_zero = exchange(result, "seq")
    hidden_zero, slope_zero = feed_forward(two_zero, 0)
    partial = branch_sums(spot, hidden_zero, heads_zero, fc2_places[0], dense_places[0])
    residual = residual + (summed(partial) + outer_biases[0])
    hat, scale = normalised(residual)
    hat_pieces = gathered(low(hat))
    grad_top, upper_payload = top_gradient(spot, pieces, dense_places[1])
    upper = exchange(upper_payload, "seq")

    one, two, payload = project(
        spot, hat_pieces, pairs[1], qkv_places[1], qkv_biases[1], ()
    )
    packed = exchange(payload, "seq")
    two = after(two, payload)
    hidden, slope = feed_forward(two, 1)
    grad_pre = pre_gradient(grad_top, slope, 1)
    result, *kept = attend(core_ref, packed, table, starts, (hidden, grad_pre))

    back = attend_back(core_ref, packed, table, starts, *kept, upper)
    grad_heads = exchange(back, "seq")
    heads = exchange(after(result, grad_heads), "seq")
    feed_grads, feed_product, feed_shift, feed_sums = feed_gradient(
        spot, two, grad_top, grad_pre, hidden, fc1_places[1], work=(back,)
    )
    shares_feed = lax.psum_scatter(feed_grads, OWNERS, scatter_dimension=0, tiled=True)
    change = half_sum(
        norm_gradient(
            spot,
            grad_heads,
            grad_pre,
            qkv_places[1],
            fc1_places[1],
            pairs[1][0],
            work=(feed_grads,),
        )
    )
    half = change
    change = z_sum(half)
    weight_grads, heads_product, heads_shift, heads_sums = heads_gradient(
        spot, one, grad_heads, qkv_places[1], grad_top, heads, (half,)
    )
    partial = branch_sums(spot, hidden, heads, fc2_places[1], dense_places[1], (half,), 0)
    own_top = own_rows(grad_top, along_z, 0).astype(jnp.float32)
    sums_one = (
        (heads_product, feed_product),
        (heads_shift, feed_shift),
        heads_sums,
        feed_sums,
        jnp.sum(own_top, axis=0),
    )
    grad_own = after(low(own_top + norm_back(change, hat, scale)), heads)
    grad_low, upper_payload = top_gradient(
        spot, gathered(grad_own), dense_places[0], (weight_grads, partial)
    )

    upper = exchange(upper_payload, "seq")
    grad_pre = pre_gradient(grad_low, slope_zero, 0)
    weight_grads, feed_product, feed_shift, feed_sums = feed_gradient(
        spot,
        two_zero,
        grad_low,
        grad_pre,
        hidden_zero,
        fc1_places[0],
        heads_zero,
        weight_grads,
        (upper_payload,),
    )
    shares_more = lax.psum_scatter(weight_grads, OWNERS, scatter_dimension=0, tiled=True)
    final = residual + (summed(partial) + outer_biases[1])
    back = attend_back(
        core_ref, packed_zero, table, starts, *kept_zero, upper, (weight_grads, final)
    )
    grad_heads = exchange(back, "seq")
    out_pieces = gathered(low(final))
    block_out = joined(spot, *out_pieces).reshape(inputs.shape)
    qkv_grads, heads_product, heads_shift, heads_sums = heads_gradient(
        spot, one_zero, grad_heads, qkv_places[0], work=(out_pieces[1],)
    )
    sums_zero = (
        (heads_product, feed_product),
        (heads_shift, feed_shift),
        heads_sums,
        feed_sums,
        jnp.sum(grad_own.astype(jnp.float32), axis=0),
    )

    def small_gradients(l, products, shift_grads, head_sums, pre_sums, own_sums):
        gain, shift = pairs[l]
        shift_grad = jnp.stack([s[0] for s in shift_grads])
        gain_grad = (jnp.stack([p[0] for p in products]) - shift * shift_grad) / gain
        placed_heads = jnp.where(mine[:, None], head_sums[0].reshape(3, 1, head_cols), 0.0)
        placed_pre = jnp.where(mine[:, None], pre_sums[0:1], 0.0)
        bias_grad = jnp.concatenate(
            [
                shift_grad.reshape(-1),
                placed_heads.reshape(-1),
                own_sums,
                placed_pre.reshape(-1),
                own_sums,
            ]
        )
        return [bias_grad.reshape(owners, bias_share), gain_grad.reshape(owners, gain_share)]

    small = jnp.concatenate(
        [*small_gradients(0, *sums_zero), *small_gradients(1, *sums_one)], axis=1
    )
    small = jnp.pad(small, ((0, 0), (0, rows * 3 * head_cols - small.shape[1])))
    tiles = jnp.concatenate(
        [qkv_grads.reshape(owners, share, -1), low(small).reshape(owners, rows, -1)], axis=1
    )
    change = summed(
        norm_gradient(
            spot,
            grad_heads,
            grad_pre,
            qkv_places[0],
            fc1_places[0],
            pairs[0][0],
            tokens,
            (tiles,),
        )
    )
    columns = lax.dynamic_slice_in_dim(grad_low, tensor_rank * (D // 8), D // 8, 1)
    grad_inputs = swapped(columns, core).astype(jnp.float32) + change
    grad_inputs = grad_inputs.reshape(cotangent.shape)
    tiles = jnp.sum(exchange(tiles, OWNERS).astype(jnp.float32), axis=0)
    small = tiles[share:].reshape(-1)[: LAYERS * (gain_share + bias_share)]
    small = jnp.sum(sent_to_all(small, "tensor"), axis=0).reshape(LAYERS, -1)
    feed = shares_feed.astype(jnp.float32)
    more = shares_more.astype(jnp.float32)
    grad_qkv = jnp.stack([tiles[:share], more[:, 1152:1536]])
    grad_dense = jnp.stack([more[:, 1024:1152], more[:, 1536:]])
    grad_fc1 = jnp.stack([more[:, :hidden_cols], feed[:, :hidden_cols]])
    grad_fc2 = jnp.stack([more[:, hidden_cols : 2 * hidden_cols], feed[:, hidden_cols:]])
    return (
        block_out,
        grad_inputs,
        grad_qkv.reshape(w_qkv.shape),
        grad_dense,
        grad_fc1,
        grad_fc2,
        small[:, bias_share:],
        small[:, :bias_share],
    )


def solution(mesh):
    in_specs = (
        P("dp", "seq", None),
        P(None, ("dp", "seq"), None, "tensor"),
        P(None, ("dp", "seq"), "tensor"),
        P(None, ("dp", "seq"), "tensor"),
        P(None, ("dp", "seq"), "tensor"),
        P(None, ("dp", "seq")),
        P(None, ("dp", "seq")),
        P("dp", None),
        P("dp", "seq", "tensor"),
    )
    out_specs = (
        P("dp", "seq", None),
        P("dp", "seq", "tensor"),
        P(None, ("dp", "seq"), None, "tensor"),
        P(None, ("dp", "seq"), "tensor"),
        P(None, ("dp", "seq"), "tensor"),
        P(None, ("dp", "seq"), "tensor"),
        P(None, ("dp", "seq")),
        P(None, ("dp", "seq")),
    )
    return jax.shard_map(shards, mesh=mesh, in_specs=in_specs, out_specs=out_specs, check_vma=False)
```

```python
import math

import jax
import jax.numpy as jnp
from jax import lax
from jax.experimental import pallas as pl
from jax.experimental.pallas import tpu as pltpu
from jax.sharding import PartitionSpec as P

D = 1024
FF = 4096
HEAD = 64
ROT = 16
LAYERS = 2
DOCUMENTS = 5
BLOCK = 256
VMEM_BYTES = 48 * 1024 * 1024
OWNERS = ("dp", "seq")
ACROSS = [(2 * z + core, 2 * z + 1 - core) for z in range(4) for core in range(2)]

epsilon = 1e-05


def dot(a, b, dims):
    return lax.dot_general(a, b, (dims, ((), ())), preferred_element_type=jnp.float32)


def turned(block, cosine, sines):
    half = ROT // 2
    low, high = (block[:half], block[half:ROT])
    return jnp.concatenate(
        [low * cosine - high * sines, high * cosine + low * sines, block[ROT:]], axis=0
    )


def in_order(block, flip):
    half = block.shape[-1] // 2
    other = jnp.concatenate([block[..., half:], block[..., :half]], axis=-1)
    return jnp.where(flip, other, block)


def prepare(packed, table, keys, keys_t, values, values_t, blocks, flip):
    queries = []
    half = ROT // 2
    for i in range(blocks):
        cols = slice(i * BLOCK, (i + 1) * BLOCK)
        cosine, sines = (table[:half, cols], table[half:, cols])
        query = in_order(packed[i, 0].astype(jnp.float32), flip)
        query = turned(query, cosine, sines).astype(jnp.bfloat16)
        queries.append(query * jnp.bfloat16(HEAD**-0.5))
        key = in_order(packed[i, 1].astype(jnp.float32), flip)
        key = turned(key, cosine, sines).astype(jnp.bfloat16)
        keys[cols, :] = key.T
        value = in_order(packed[i, 2].astype(jnp.float32), flip).astype(jnp.bfloat16)
        if keys_t is not None:
            keys_t[:, cols] = key
        if values is not None:
            values[cols, :] = value.T
        if values_t is not None:
            values_t[:, cols] = value
    return queries


def masked(scores, i, starts):
    row = lax.broadcasted_iota(jnp.int32, scores.shape, 0)
    in_document = jnp.where(row >= starts, scores, -1e30)
    last = in_document[i * BLOCK :]
    row = lax.broadcasted_iota(jnp.int32, last.shape, 0)
    col = lax.broadcasted_iota(jnp.int32, last.shape, 1)
    last = jnp.where(row <= col, last, -1e30)
    return jnp.concatenate([in_document[: i * BLOCK], last], axis=0) if i > 0 else last


def attend_kernel(core, packed, table, starts, out, wide, log_total, keys, values_t):
    blocks = packed.shape[0]
    flip = core[0] == 1
    queries = prepare(packed, table, keys, None, None, values_t, blocks, flip)
    for i in range(blocks):
        length = (i + 1) * BLOCK
        scores = dot(keys[:length], queries[i], ((1,), (0,)))
        scores = masked(scores, i, starts[:, i * BLOCK : length])
        largest = jnp.max(scores, axis=0, keepdims=True)
        exponent = jnp.exp(scores - largest)
        total = jnp.sum(exponent, axis=0, keepdims=True)
        result = dot(values_t[:, :length], exponent.astype(jnp.bfloat16), ((1,), (0,)))
        result = result / total
        wide[i] = result
        out[i] = in_order(result, flip).astype(jnp.bfloat16)
        log_total[i] = largest + jnp.log(total)


SCALAR = pl.BlockSpec(memory_space=pltpu.SMEM)
WHOLE = pl.BlockSpec(memory_space=pltpu.VMEM)


def attend(core, packed, table, starts, work=()):
    blocks = packed.shape[0]
    full = blocks * BLOCK
    return pl.pallas_call(
        skipping(attend_kernel, 4, len(work)),
        out_shape=(
            jax.ShapeDtypeStruct((blocks, HEAD, BLOCK), jnp.bfloat16),
            jax.ShapeDtypeStruct((blocks, HEAD, BLOCK), jnp.float32),
            jax.ShapeDtypeStruct((blocks, 1, BLOCK), jnp.float32),
        ),
        in_specs=[SCALAR] + [WHOLE] * 3 + [UNREAD] * len(work),
        scratch_shapes=[
            pltpu.VMEM((full, HEAD), jnp.bfloat16),
            pltpu.VMEM((HEAD, full), jnp.bfloat16),
        ],
        compiler_params=pltpu.CompilerParams(vmem_limit_bytes=VMEM_BYTES),
        cost_estimate=pl.CostEstimate(
            flops=4 * full * full * HEAD, bytes_accessed=2**21, transcendentals=full * full // 2
        ),
    )(core, packed, table, starts, *work)


def attend_back_kernel(
    core,
    packed,
    table,
    starts,
    wide,
    log_total,
    upper,
    result,
    out,
    keys,
    keys_t,
    values,
    grad_k,
    grad_v,
):
    blocks = packed.shape[0]
    half = ROT // 2
    flip = core[0] == 1
    queries = prepare(packed, table, keys, keys_t, values, None, blocks, flip)
    for i in range(blocks):
        length = (i + 1) * BLOCK
        cols = slice(i * BLOCK, length)
        scores = dot(keys[:length], queries[i], ((1,), (0,)))
        probs = jnp.exp(masked(scores, i, starts[:, cols]) - log_total[i])
        above = in_order(upper[i].astype(jnp.float32), flip).astype(jnp.bfloat16)
        grad_probs = dot(values[:length], above, ((1,), (0,)))
        row_dot = jnp.sum(above.astype(jnp.float32) * wide[i], axis=0, keepdims=True)
        grad_scores = (probs * (grad_probs - row_dot)).astype(jnp.bfloat16)
        grad_q = dot(keys_t[:, :length], grad_scores, ((1,), (0,))) * HEAD**-0.5
        cosine, sines = (table[:half, cols], table[half:, cols])
        out[i, 0] = in_order(turned(grad_q, cosine, -sines), flip).astype(jnp.bfloat16)
        probs_low = probs.astype(jnp.bfloat16)
        part_v = dot(above, probs_low, ((1,), (1,)))
        part_k = dot(queries[i], grad_scores, ((1,), (1,)))
        if i > 0:
            grad_v[:, : i * BLOCK] += part_v[:, : i * BLOCK]
            grad_k[:, : i * BLOCK] += part_k[:, : i * BLOCK]
        grad_v[:, cols] = part_v[:, cols]
        grad_k[:, cols] = part_k[:, cols]
    for i in range(blocks):
        cols = slice(i * BLOCK, (i + 1) * BLOCK)
        cosine, sines = (table[:half, cols], table[half:, cols])
        out[i, 1] = in_order(turned(grad_k[:, cols], cosine, -sines), flip).astype(jnp.bfloat16)
        out[i, 2] = in_order(grad_v[:, cols], flip).astype(jnp.bfloat16)
        if out.shape[1] > 3:
            out[i, 3] = result[i]


def attend_back(core, packed, table, starts, wide, log_total, upper, result, work=(), sent=3):
    blocks = packed.shape[0]
    full = blocks * BLOCK
    return pl.pallas_call(
        skipping(attend_back_kernel, 8, len(work)),
        out_shape=jax.ShapeDtypeStruct((blocks, sent, HEAD, BLOCK), jnp.bfloat16),
        in_specs=[SCALAR] + [WHOLE] * 7 + [UNREAD] * len(work),
        scratch_shapes=[
            pltpu.VMEM((full, HEAD), jnp.bfloat16),
            pltpu.VMEM((HEAD, full), jnp.bfloat16),
            pltpu.VMEM((full, HEAD), jnp.bfloat16),
            pltpu.VMEM((HEAD, full), jnp.float32),
            pltpu.VMEM((HEAD, full), jnp.float32),
        ],
        compiler_params=pltpu.CompilerParams(vmem_limit_bytes=VMEM_BYTES),
        cost_estimate=pl.CostEstimate(
            flops=10 * full * full * HEAD, bytes_accessed=2**22, transcendentals=full * full // 2
        ),
    )(core, packed, table, starts, wide, log_total, upper, result, *work)


def exchange(blocks, axis, groups=None):
    return lax.all_to_all(blocks, axis, 0, 0, tiled=True, axis_index_groups=groups)


def sent_to_all(shard, axis, groups=None):
    size = lax.axis_size(axis) if groups is None else len(groups[0])
    return exchange(jnp.broadcast_to(shard, (size, *shard.shape)), axis, groups)


UNREAD = pl.BlockSpec(memory_space=pl.ANY)


def skipping(kernel, first, count):
    return lambda *refs: kernel(*refs[:first], *refs[first + count :])


def after(value, *work):
    return pl.pallas_call(
        lambda *refs: None,
        out_shape=jax.ShapeDtypeStruct(value.shape, value.dtype),
        in_specs=[UNREAD] * (1 + len(work)),
        out_specs=UNREAD,
        input_output_aliases={0: 0},
        cost_estimate=pl.CostEstimate(flops=0, bytes_accessed=0, transcendentals=0),
    )(value, *work)


def along(distance):
    return [
        (2 * z + core, 2 * ((z + distance) % 4) + core) for z in range(4) for core in range(2)
    ]


def gathered(own, work=()):
    mine = jnp.stack([own] + [lax.ppermute(own, "tensor", along(-r)) for r in range(1, 4)])
    if work:
        mine = after(mine, *work)
    return mine, lax.ppermute(mine, "tensor", ACROSS)


def half_sum(halves):
    got = lax.ppermute(halves[1], "tensor", ACROSS)
    return low(halves[0].astype(jnp.float32) + got.astype(jnp.float32))


def z_sum(half):
    total = half[0].astype(jnp.float32)
    for r in range(1, 4):
        total = total + lax.ppermute(half[r], "tensor", along(r)).astype(jnp.float32)
    return total


def summed(halves):
    return z_sum(half_sum(halves))


def swapped(tokens, core):
    halves = tokens.reshape(4, 2, 128, tokens.shape[-1])
    return jnp.where(core == 0, halves, halves[:, ::-1]).reshape(tokens.shape)


def swapped_rows(block, flip):
    half = block.shape[0] // 2
    other = jnp.concatenate([block[half:], block[:half]], axis=0)
    return jnp.where(flip, other, block)


def own_rows(tokens, along_z, half):
    blocks = tokens.reshape(4, 2, 128, tokens.shape[-1])
    return lax.dynamic_index_in_dim(
        lax.dynamic_index_in_dim(blocks, along_z, 0, False), half, 0, False
    )


def in_steps(
    kernel, out_shape, in_specs, out_specs, operands, flops, work=(), scratch=(), alias=None
):
    return pl.pallas_call(
        skipping(kernel, len(operands), len(work)),
        out_shape=out_shape,
        grid_spec=pltpu.PrefetchScalarGridSpec(
            num_scalar_prefetch=1,
            grid=(4,),
            in_specs=[*in_specs, *([UNREAD] * len(work))],
            out_specs=out_specs,
            scratch_shapes=scratch,
        ),
        input_output_aliases={} if alias is None else alias,
        compiler_params=pltpu.CompilerParams(vmem_limit_bytes=VMEM_BYTES),
        cost_estimate=pl.CostEstimate(
            flops=flops, bytes_accessed=2**23 if flops else 2**10, transcendentals=0
        ),
    )(*operands, *work)


def distance_of(b, spot):
    return lax.rem(b - spot[0] + 4, 4)


def columns_of(weight, width, block):
    return pl.BlockSpec((weight.shape[0], width), lambda b, spot: (0, block))


def rows_of(weight, width, block):
    return pl.BlockSpec((BLOCK, width), lambda i, spot: (i, block))


def whole_of(array):
    return pl.BlockSpec(array.shape, lambda i, spot: (0,) * array.ndim)


PIECE = pl.BlockSpec((1, 128, D), lambda b, spot: (distance_of(b, spot), 0, 0))
TOKENS = pl.BlockSpec((BLOCK, D), lambda b, spot: (b, 0))
HALVES = pl.BlockSpec((2, 1, 128, D), lambda b, spot: (0, distance_of(b, spot), 0, 0))
ALL_TOKENS = jax.ShapeDtypeStruct((1024, D), jnp.bfloat16)
ALL_HALVES = jax.ShapeDtypeStruct((2, 4, 128, D), jnp.bfloat16)


def project_block(hat, gain, shift, qkv, bias, one, two, packed):
    first = (hat * gain[0:1] + shift[0:1]).astype(jnp.bfloat16)
    one[...] = first
    two[...] = (hat * gain[1:2] + shift[1:2]).astype(jnp.bfloat16)
    flat = (dot(first, qkv[...], ((1,), (0,))) + bias[...]).T.astype(jnp.bfloat16)
    for k in range(3):
        for j in range(2):
            at = (2 * k + j) * HEAD
            packed[j, k] = flat[at : at + HEAD]


def project_input_kernel(spot, start, gain, shift, qkv, bias, one, two, packed):
    block = swapped_rows(start[...].astype(jnp.float32), spot[1] == 1)
    hat, _ = normalised(block)
    project_block(hat, gain, shift, qkv, bias, one, two, packed)


def project_kernel(spot, mine, other, gain, shift, qkv, bias, one, two, packed):
    hat = jnp.concatenate([mine[0], other[0]], axis=0).astype(jnp.float32)
    project_block(hat, gain, shift, qkv, bias, one, two, packed)


def project(spot, tokens, pair, qkv, bias, work):
    qkv, block = qkv
    kernel = project_input_kernel if len(tokens) == 1 else project_kernel
    return in_steps(
        kernel,
        (ALL_TOKENS, ALL_TOKENS, jax.ShapeDtypeStruct((8, 3, HEAD, BLOCK), jnp.bfloat16)),
        [
            *([TOKENS] if len(tokens) == 1 else [PIECE, PIECE]),
            whole_of(pair[0]),
            whole_of(pair[1]),
            columns_of(qkv, 6 * HEAD, block),
            whole_of(bias),
        ],
        (TOKENS, TOKENS, pl.BlockSpec((2, 3, HEAD, BLOCK), lambda b, spot: (b, 0, 0, 0))),
        (spot, *tokens, *pair, qkv, bias),
        2 * 1024 * 384 * D,
        work,
    )


def last_of(blocks, count, place):
    if blocks.ndim == 3:
        return pl.BlockSpec((count, HEAD, BLOCK), lambda i, spot: (place(i), 0, 0))
    return pl.BlockSpec((count, None, HEAD, BLOCK), lambda i, spot: (place(i), 3, 0, 0))


def out_kernel(spot, hidden, heads, fc2, dense, out):
    result = dot(hidden[...], fc2[...], ((1,), (1,)))
    block = jnp.concatenate([heads[0], heads[1]], axis=0).T
    result = result + dot(block, dense[...], ((1,), (1,)))
    out[0, 0] = result[:128].astype(jnp.bfloat16)
    out[1, 0] = result[128:].astype(jnp.bfloat16)


def branch_sums(spot, hidden, heads, fc2, dense, work=(), flops=2**31):
    (fc2, fc2_block), (dense, dense_block) = (fc2, dense)
    return in_steps(
        out_kernel,
        ALL_HALVES,
        [
            pl.BlockSpec((BLOCK, hidden.shape[1]), lambda b, spot: (b, 0)),
            last_of(heads, 2, lambda b: b),
            columns_of(fc2, hidden.shape[1], fc2_block),
            columns_of(dense, 2 * HEAD, dense_block),
        ],
        HALVES,
        (spot, hidden, heads, fc2, dense),
        flops,
        work,
    )


def to_norms(grad_heads, grad_pre, qkv, fc1, gain):
    block = jnp.concatenate([grad_heads[j, k] for k in range(3) for j in range(2)], axis=0)
    result = dot(block.T, qkv[...], ((1,), (1,))) * gain[0:1]
    return result + dot(grad_pre[...], fc1[...], ((1,), (1,))) * gain[1:2]


def back_kernel(spot, grad_heads, grad_pre, qkv, fc1, gain, out):
    result = to_norms(grad_heads, grad_pre, qkv, fc1, gain)
    out[0, 0] = result[:128].astype(jnp.bfloat16)
    out[1, 0] = result[128:].astype(jnp.bfloat16)


def back_input_kernel(spot, grad_heads, grad_pre, qkv, fc1, gain, start, out, change):
    result = to_norms(grad_heads, grad_pre, qkv, fc1, gain)
    z, core = (spot[0], spot[1])
    hat, scale = normalised(swapped_rows(start[...].astype(jnp.float32), core == 1))
    change[...] = swapped_rows(norm_back(result, hat, scale), core == 1)
    for r in range(4):
        for j in range(2):
            owner = 2 * lax.rem(z + r, 4) + lax.rem(core + j, 2)
            lanes = pl.ds(pl.multiple_of(owner * 128, 128), 128)
            out[j, r] = change[:, lanes].astype(jnp.bfloat16)


def norm_gradient(spot, grad_heads, grad_pre, qkv, fc1, gain, start=None, work=()):
    (qkv, qkv_block), (fc1, fc1_block) = (qkv, fc1)
    width = grad_pre.shape[1]
    in_specs = [
        pl.BlockSpec((2, 3, HEAD, BLOCK), lambda b, spot: (b, 0, 0, 0)),
        pl.BlockSpec((BLOCK, width), lambda b, spot: (b, 0)),
        columns_of(qkv, 6 * HEAD, qkv_block),
        columns_of(fc1, width, fc1_block),
        whole_of(gain),
    ]
    flops = 2 * 1024 * 896 * D
    operands = (spot, grad_heads, grad_pre, qkv, fc1, gain)
    if start is None:
        return in_steps(back_kernel, ALL_HALVES, in_specs, HALVES, operands, flops, work)
    flops = 0
    return in_steps(
        back_input_kernel,
        jax.ShapeDtypeStruct((2, 4, 1024, 128), jnp.bfloat16),
        [*in_specs, TOKENS],
        pl.BlockSpec((2, 4, BLOCK, 128), lambda b, spot: (0, 0, b, 0)),
        (*operands, start),
        flops,
        work,
        [pltpu.VMEM((BLOCK, D), jnp.float32)],
    )


def join_kernel(spot, mine, other, out):
    core = spot[1]
    out[pl.ds(pl.multiple_of(core * 128, 128), 128), :] = mine[0]
    out[pl.ds(pl.multiple_of((1 - core) * 128, 128), 128), :] = other[0]


def joined(spot, mine, other):
    return in_steps(join_kernel, ALL_TOKENS, [PIECE, PIECE], TOKENS, (spot, mine, other), 0)


def head_gradient(block, dense, upper):
    flat = dot(block, dense[...], ((1,), (0,))).T.astype(jnp.bfloat16)
    upper[0] = flat[:HEAD]
    upper[1] = flat[HEAD:]


def gradient_kernel(spot, mine, other, dense, out, upper):
    block = jnp.concatenate([mine[0], other[0]], axis=0)
    out[...] = block
    head_gradient(block, dense, upper)


def columns_kernel(spot, mine, other, dense, out, upper):
    z, core = (spot[0], spot[1])
    for r in range(4):
        for j, pieces in enumerate((mine, other)):
            owner = 2 * lax.rem(z + r, 4) + lax.rem(core + j, 2)
            piece = swapped_rows(pieces[r].astype(jnp.float32), core == 1)
            lanes = pl.ds(pl.multiple_of(owner * 128, 128), 128)
            out[:, lanes] = piece.astype(jnp.bfloat16)
    head_gradient(out[...], dense, upper)


def top_gradient(spot, pieces, dense, work=()):
    dense, block = dense
    kernel, specs = (gradient_kernel, [PIECE, PIECE])
    if pieces[0].shape[2] < D:
        kernel = columns_kernel
        specs = [pl.BlockSpec((4, BLOCK, 128), lambda b, spot: (0, b, 0))] * 2
    return in_steps(
        kernel,
        (ALL_TOKENS, jax.ShapeDtypeStruct((8, HEAD, BLOCK), jnp.bfloat16)),
        [*specs, columns_of(dense, 2 * HEAD, block)],
        (TOKENS, pl.BlockSpec((2, HEAD, BLOCK), lambda b, spot: (b, 0, 0))),
        (spot, *pieces, dense),
        2 * 1024 * 128 * D,
        work,
    )


def as_row(column):
    return jnp.broadcast_to(column, (column.shape[0], 128)).T[:1]


def norm_sums(weight, grad_weight, sums, product, shift):
    wide = weight.astype(jnp.float32)
    product[...] = as_row(jnp.sum(wide * grad_weight, axis=1, keepdims=True))
    shift[...] = as_row(jnp.sum(wide * sums, axis=1, keepdims=True))


def feed_block(normed, grad_low, grad_pre, hidden, fc1, out, product, shift, sums):
    @pl.when(pl.program_id(0) == 0)
    def _():
        total = jnp.sum(grad_pre[...].astype(jnp.float32), axis=0, keepdims=True)
        sums[...] = total

    width = grad_pre.shape[1]
    grad_fc1 = dot(normed[...], grad_pre[...], ((0,), (0,)))
    out[:, :width] = grad_fc1.astype(jnp.bfloat16)
    grad_fc2 = dot(grad_low[...], hidden[...], ((0,), (0,)))
    out[:, width : 2 * width] = grad_fc2.astype(jnp.bfloat16)
    norm_sums(fc1[...], grad_fc1, sums[...], product, shift)


def dense_block(grad_low, heads):
    total = 0.0
    for b in range(4):
        block = jnp.concatenate([heads[2 * b], heads[2 * b + 1]], axis=0)
        total = total + dot(block, grad_low[b * BLOCK : (b + 1) * BLOCK], ((1,), (0,)))
    return total.T.astype(jnp.bfloat16)


def heads_block(normed, grad_heads, qkv, out, product, shift, sums, columns):
    @pl.when(pl.program_id(0) == 0)
    def _():
        for b in range(4):
            for k in range(3):
                for j in range(2):
                    at = (2 * k + j) * HEAD
                    columns[at : at + HEAD, b * BLOCK : (b + 1) * BLOCK] = grad_heads[2 * b + j, k]
        wide = columns[...].astype(jnp.float32)
        sums[...] = as_row(jnp.sum(wide, axis=1, keepdims=True))

    grad_qkv = dot(columns[...], normed[...], ((1,), (0,))).T
    if len(out.shape) == 2:
        out[:, : 6 * HEAD] = grad_qkv.astype(jnp.bfloat16)
    else:
        out[...] = grad_qkv.astype(jnp.bfloat16).reshape(out.shape)
    norm_sums(qkv[...], grad_qkv, sums[...], product, shift)


def feed_kernel(spot, *refs):
    feed_block(*refs)


def feed_dense_kernel(
    spot, normed, grad_low, grad_pre, hidden, fc1, heads, more, out, product, shift, sums
):
    feed_block(normed, grad_low, grad_pre, hidden, fc1, out, product, shift, sums)
    at = 2 * grad_pre.shape[1]
    out[:, at : at + 2 * HEAD] = dense_block(grad_low, heads)
    out[:, at + 2 * HEAD :] = more[...]


def heads_kernel(spot, *refs):
    heads_block(*refs)


def heads_dense_kernel(
    spot, normed, grad_heads, qkv, grad_low, heads, out, product, shift, sums, columns
):
    heads_block(normed, grad_heads, qkv, out, product, shift, sums, columns)
    out[:, 6 * HEAD :] = dense_block(grad_low, heads)


FEATURES = pl.BlockSpec((1024, BLOCK), lambda i, spot: (0, i))
ROW = pl.BlockSpec((1, BLOCK), lambda i, spot: (0, i))
ROWS = jax.ShapeDtypeStruct((1, D), jnp.float32)


def weight_gradient(
    kernel, spot, operands, in_specs, width, summed_width, scratch, work, tiled=None
):
    shape, block = ((D, width), pl.BlockSpec((BLOCK, width), lambda i, spot: (i, 0)))
    if tiled is not None:
        shape = (16, tiled, width)
        block = pl.BlockSpec((4, 64, width), lambda i, spot: (i, 0, 0))
    return in_steps(
        kernel,
        (
            jax.ShapeDtypeStruct(shape, jnp.bfloat16),
            ROWS,
            ROWS,
            jax.ShapeDtypeStruct((1, summed_width), jnp.float32),
        ),
        in_specs,
        (
            block,
            ROW,
            ROW,
            pl.BlockSpec((1, summed_width), lambda i, spot: (0, 0)),
        ),
        (spot, *operands),
        0,
        work,
        scratch,
    )


def feed_gradient(spot, normed, grad_low, grad_pre, hidden, fc1, heads=None, more=None, work=()):
    width = hidden.shape[1]
    operands = [normed, grad_low, grad_pre, hidden, fc1[0]]
    in_specs = [FEATURES, FEATURES, whole_of(grad_pre), whole_of(hidden)]
    in_specs += [rows_of(fc1[0], width, fc1[1])]
    kernel, total = (feed_kernel, 2 * width)
    if heads is not None:
        operands += [heads, more]
        in_specs += [last_of(heads, 8, lambda i: 0), rows_of(more, more.shape[1], 0)]
        kernel, total = (feed_dense_kernel, total + 2 * HEAD + more.shape[1])
    return weight_gradient(kernel, spot, operands, in_specs, total, width, (), work)


def heads_gradient(
    spot, normed, grad_heads, qkv, grad_low=None, heads=None, work=(), tiled=None
):
    width = 6 * HEAD
    operands = [normed, grad_heads, qkv[0]]
    in_specs = [
        FEATURES,
        pl.BlockSpec((8, 3, HEAD, BLOCK), lambda i, spot: (0, 0, 0, 0)),
        rows_of(qkv[0], width, qkv[1]),
    ]
    kernel, total = (heads_kernel, width)
    if heads is not None:
        operands += [grad_low, heads]
        in_specs += [FEATURES, last_of(heads, 8, lambda i: 0)]
        kernel, total = (heads_dense_kernel, width + 2 * HEAD)
    scratch = [pltpu.VMEM((width, 1024), jnp.bfloat16)]
    return weight_gradient(
        kernel, spot, operands, in_specs, total, width, scratch, work, tiled
    )


def normalised(values):
    centred = values - jnp.mean(values, axis=-1, keepdims=True)
    variance = jnp.mean(centred * centred, axis=-1, keepdims=True)
    scale = lax.rsqrt(variance + epsilon)
    return centred * scale, scale


def norm_back(grad, hat, scale):
    mean = jnp.mean(grad, axis=-1, keepdims=True)
    along = jnp.mean(grad * hat, axis=-1, keepdims=True)
    return scale * (grad - mean - hat * along)


def gelu_and_slope(values):
    share = 0.5 * (1.0 + lax.erf(values * math.sqrt(0.5)))
    slope = share + values * jnp.exp(-0.5 * values * values) * (1.0 / math.sqrt(2.0 * math.pi))
    return (values * share).astype(jnp.bfloat16), slope


def low(values):
    return values.astype(jnp.bfloat16)


def shards(inputs, w_qkv, w_dense, w_fc1, w_fc2, norm_gain, biases, segment_ids, cotangent):
    tensor_rank = lax.axis_index("tensor")
    seq_rank = lax.axis_index("seq")
    along_z, core = (tensor_rank // 2, tensor_rank % 2)
    core_ref = core.astype(jnp.int32).reshape(1)
    spot = jnp.stack([along_z, core]).astype(jnp.int32)
    owners = 16
    full_len = segment_ids.shape[1]
    head_cols = w_qkv.shape[3]
    hidden_cols = w_fc1.shape[2]
    share = w_qkv.shape[1]
    gain_share = norm_gain.shape[1]
    bias_share = biases.shape[1]
    mine = jnp.arange(8) == tensor_rank

    qkv_flat = w_qkv.reshape(LAYERS, share, 3 * head_cols)
    vectors = jnp.concatenate([norm_gain.reshape(-1), biases.reshape(-1)])
    rows = 16
    vectors = jnp.pad(vectors, (0, rows * 3 * head_cols - vectors.size)).reshape(rows, -1)
    first = jnp.concatenate([qkv_flat[0], vectors], axis=0)
    first = jnp.broadcast_to(first, (owners, *first.shape))
    columns = after(cotangent.reshape(-1, cotangent.shape[-1]), first)
    first = exchange(first, OWNERS)
    both_zero = lax.all_gather(
        jnp.concatenate([w_fc1[0], w_fc2[0], w_dense[0]], axis=1), OWNERS, axis=0, tiled=True
    )
    pieces = gathered(columns)
    heads_one = lax.all_gather(
        jnp.concatenate([qkv_flat[1], w_dense[1]], axis=1), OWNERS, axis=0, tiled=True
    )
    feed_one = lax.all_gather(
        jnp.concatenate([w_fc1[1], w_fc2[1]], axis=1), OWNERS, axis=0, tiled=True
    )
    qkv_zero = first[:, :share].reshape(D, 3 * head_cols)
    vectors = first[:, share:].reshape(owners, -1)[:, : LAYERS * (gain_share + bias_share)]
    gain_vecs = vectors[:, : LAYERS * gain_share].reshape(owners, LAYERS, -1).astype(jnp.float32)
    bias_vecs = vectors[:, LAYERS * gain_share :].reshape(owners, LAYERS, -1).astype(jnp.float32)
    qkv_places = [(qkv_zero, 0), (heads_one, 0)]
    dense_places = [(both_zero, 8), (heads_one, 3)]
    fc1_places = [(both_zero, 0), (feed_one, 0)]
    fc2_places = [(both_zero, 1), (feed_one, 1)]
    fc1_weights = [both_zero[:, :hidden_cols], feed_one[:, :hidden_cols]]
    fc2_weights = [both_zero[:, hidden_cols : 2 * hidden_cols], feed_one[:, hidden_cols:]]

    pairs, qkv_biases, fc1_biases, outer_biases = ([], [], [], [])
    for l in range(LAYERS):
        vec = bias_vecs[:, l].reshape(-1)
        pairs.append((gain_vecs[:, l].reshape(2, D), vec[: 2 * D].reshape(2, D)))
        bias = vec[2 * D : 5 * D].reshape(3, 8, head_cols)
        bias = lax.dynamic_index_in_dim(bias, tensor_rank, 1, False)
        qkv_biases.append(bias.reshape(1, 3 * head_cols))
        bias = vec[6 * D : 6 * D + FF].reshape(8, hidden_cols)
        fc1_biases.append(lax.dynamic_index_in_dim(bias, tensor_rank, 0, True))
        outer_biases.append((vec[5 * D : 6 * D] + vec[6 * D + FF :]).reshape(1, D))

    segments = lax.dynamic_index_in_dim(segment_ids, seq_rank // 2, 0, False)
    earlier = jnp.zeros_like(segments)
    for doc in range(1, DOCUMENTS):
        before = jnp.sum((segments < doc).astype(jnp.int32))
        earlier = jnp.where(segments == doc, before, earlier)
    places = jnp.arange(full_len, dtype=jnp.int32) - earlier
    half_rot = ROT // 2
    inverse = 10000.0 ** (-jnp.arange(half_rot, dtype=jnp.float32) * 2.0 / ROT)
    angles = inverse[:, None] * places.astype(jnp.float32)[None, :]
    table = jnp.concatenate([jnp.cos(angles), jnp.sin(angles)], axis=0)
    starts = earlier[None, :]

    def feed_forward(normed_two, l):
        pre_act = dot(normed_two, fc1_weights[l], ((1,), (0,))) + fc1_biases[l]
        return gelu_and_slope(pre_act)

    def pre_gradient(grad_low, slope, l):
        return low(dot(grad_low, fc2_weights[l], ((1,), (0,))) * slope)

    tokens = inputs.reshape(-1, D)
    residual = own_rows(tokens, along_z, core).astype(jnp.float32)

    one_zero, two_zero, payload = project(
        spot, (tokens,), pairs[0], qkv_places[0], qkv_biases[0], (pieces[1],)
    )
    packed_zero = exchange(payload, "seq")
    prepared = (*pairs[1], qkv_biases[1], fc1_biases[1], outer_biases[0], outer_biases[1])
    result, *kept_zero = attend(core_ref, packed_zero, table, starts, prepared)
    heads_zero = exchange(result, "seq")
    hidden_zero, slope_zero = feed_forward(two_zero, 0)
    partial = branch_sums(spot, hidden_zero, heads_zero, fc2_places[0], dense_places[0])
    residual = residual + (summed(partial) + outer_biases[0])
    hat, scale = normalised(residual)
    grad_top, upper_payload = top_gradient(spot, pieces, dense_places[1], (partial,))
    upper = exchange(upper_payload, "seq")
    hat_pieces = gathered(after(low(hat), upper_payload), (upper,))

    one, two, payload = project(
        spot, hat_pieces, pairs[1], qkv_places[1], qkv_biases[1], ()
    )
    packed = exchange(payload, "seq")
    result, *kept = attend(core_ref, packed, table, starts)

    back = attend_back(core_ref, packed, table, starts, *kept, upper, result, sent=4)
    grad_heads = exchange(back, "seq")
    two = after(two, back)
    hidden, slope = feed_forward(two, 1)
    grad_pre = pre_gradient(grad_top, slope, 1)
    feed_grads, feed_product, feed_shift, feed_sums = feed_gradient(
        spot, two, grad_top, grad_pre, hidden, fc1_places[1], work=(back,)
    )
    shares_feed = lax.psum_scatter(feed_grads, OWNERS, scatter_dimension=0, tiled=True)
    change = half_sum(
        norm_gradient(
            spot,
            grad_heads,
            grad_pre,
            qkv_places[1],
            fc1_places[1],
            pairs[1][0],
            work=(feed_grads,),
        )
    )
    half = change
    change = z_sum(half)
    weight_grads, heads_product, heads_shift, heads_sums = heads_gradient(
        spot, one, grad_heads, qkv_places[1], grad_top, grad_heads, (half,)
    )
    partial = branch_sums(
        spot, hidden, grad_heads, fc2_places[1], dense_places[1], (change,), 0
    )
    own_top = own_rows(grad_top, along_z, 0).astype(jnp.float32)
    sums_one = (
        (heads_product, feed_product),
        (heads_shift, feed_shift),
        heads_sums,
        feed_sums,
        jnp.sum(own_top, axis=0),
    )
    grad_own = low(own_top + norm_back(change, hat, scale))
    grad_low, upper_payload = top_gradient(
        spot, gathered(after(grad_own, weight_grads), (partial,)), dense_places[0]
    )

    upper = exchange(upper_payload, "seq")
    grad_pre = pre_gradient(grad_low, slope_zero, 0)
    weight_grads, feed_product, feed_shift, feed_sums = feed_gradient(
        spot,
        two_zero,
        grad_low,
        grad_pre,
        hidden_zero,
        fc1_places[0],
        heads_zero,
        weight_grads,
        (upper_payload,),
    )
    shares_more = lax.psum_scatter(weight_grads, OWNERS, scatter_dimension=0, tiled=True)
    half = half_sum(after(partial, weight_grads))
    back = attend_back(
        core_ref, packed_zero, table, starts, *kept_zero, upper, result, (weight_grads, half)
    )
    grad_heads = exchange(back, "seq")
    final = residual + (z_sum(half) + outer_biases[1])
    out_pieces = gathered(low(final))
    block_out = joined(spot, *out_pieces).reshape(inputs.shape)
    blocks = norm_gradient(
        spot,
        grad_heads,
        grad_pre,
        qkv_places[0],
        fc1_places[0],
        pairs[0][0],
        tokens,
        (final,),
    )
    qkv_grads, heads_product, heads_shift, heads_sums = heads_gradient(
        spot, one_zero, grad_heads, qkv_places[0], work=(blocks,), tiled=share + rows
    )
    sums_zero = (
        (heads_product, feed_product),
        (heads_shift, feed_shift),
        heads_sums,
        feed_sums,
        jnp.sum(grad_own.astype(jnp.float32), axis=0),
    )

    def small_gradients(l, products, shift_grads, head_sums, pre_sums, own_sums):
        gain, shift = pairs[l]
        shift_grad = jnp.concatenate(shift_grads, axis=1)
        product = jnp.concatenate(products, axis=1)
        gain_grad = (product - shift.reshape(1, -1) * shift_grad) / gain.reshape(1, -1)
        placed_heads = jnp.where(mine[:, None], head_sums.reshape(3, 1, head_cols), 0.0)
        placed_pre = jnp.where(mine[:, None], pre_sums, 0.0)
        own_sums = own_sums.reshape(1, -1)
        bias_grad = jnp.concatenate(
            [
                shift_grad,
                placed_heads.reshape(1, -1),
                own_sums,
                placed_pre.reshape(1, -1),
                own_sums,
            ],
            axis=1,
        )
        return [bias_grad.reshape(owners, bias_share), gain_grad.reshape(owners, gain_share)]

    small = jnp.concatenate(
        [*small_gradients(0, *sums_zero), *small_gradients(1, *sums_one)], axis=1
    )
    small = jnp.pad(small, ((0, 0), (0, rows * 3 * head_cols - small.shape[1])))
    small = low(small).reshape(owners, rows, -1)
    tiles = lax.dynamic_update_slice(qkv_grads, small, (0, share, 0))
    change = z_sum(after(half_sum(blocks), block_out))
    columns = lax.dynamic_slice_in_dim(grad_low, tensor_rank * (D // 8), D // 8, 1)
    grad_inputs = swapped(columns, core).astype(jnp.float32) + change
    grad_inputs = grad_inputs.reshape(cotangent.shape)
    tiles = jnp.sum(exchange(tiles, OWNERS).astype(jnp.float32), axis=0)
    small = tiles[share:].reshape(-1)[: LAYERS * (gain_share + bias_share)]
    small = jnp.sum(sent_to_all(small, "tensor"), axis=0).reshape(LAYERS, -1)
    feed = shares_feed.astype(jnp.float32)
    more = shares_more.astype(jnp.float32)
    grad_qkv = jnp.stack([tiles[:share], more[:, 1152:1536]])
    grad_dense = jnp.stack([more[:, 1024:1152], more[:, 1536:]])
    grad_fc1 = jnp.stack([more[:, :hidden_cols], feed[:, :hidden_cols]])
    grad_fc2 = jnp.stack([more[:, hidden_cols : 2 * hidden_cols], feed[:, hidden_cols:]])
    return (
        block_out,
        grad_inputs,
        grad_qkv.reshape(w_qkv.shape),
        grad_dense,
        grad_fc1,
        grad_fc2,
        small[:, bias_share:],
        small[:, :bias_share],
    )


def solution(mesh):
    in_specs = (
        P("dp", "seq", None),
        P(None, ("dp", "seq"), None, "tensor"),
        P(None, ("dp", "seq"), "tensor"),
        P(None, ("dp", "seq"), "tensor"),
        P(None, ("dp", "seq"), "tensor"),
        P(None, ("dp", "seq")),
        P(None, ("dp", "seq")),
        P("dp", None),
        P("dp", "seq", "tensor"),
    )
    out_specs = (
        P("dp", "seq", None),
        P("dp", "seq", "tensor"),
        P(None, ("dp", "seq"), None, "tensor"),
        P(None, ("dp", "seq"), "tensor"),
        P(None, ("dp", "seq"), "tensor"),
        P(None, ("dp", "seq"), "tensor"),
        P(None, ("dp", "seq")),
        P(None, ("dp", "seq")),
    )
    return jax.shard_map(shards, mesh=mesh, in_specs=in_specs, out_specs=out_specs, check_vma=False)
```

```python
import math

import jax
import jax.numpy as jnp
from jax import lax
from jax.experimental import pallas as pl
from jax.experimental.pallas import tpu as pltpu
from jax.sharding import PartitionSpec as P

D = 1024
FF = 4096
HEAD = 64
ROT = 16
LAYERS = 2
DOCUMENTS = 5
BLOCK = 256
VMEM_BYTES = 48 * 1024 * 1024
OWNERS = ("dp", "seq")
ACROSS = [(2 * z + core, 2 * z + 1 - core) for z in range(4) for core in range(2)]

epsilon = 1e-05


def dot(a, b, dims):
    return lax.dot_general(a, b, (dims, ((), ())), preferred_element_type=jnp.float32)


def turned(block, cosine, sines):
    half = ROT // 2
    low, high = (block[:half], block[half:ROT])
    return jnp.concatenate(
        [low * cosine - high * sines, high * cosine + low * sines, block[ROT:]], axis=0
    )


def in_order(block, flip):
    half = block.shape[-1] // 2
    other = jnp.concatenate([block[..., half:], block[..., :half]], axis=-1)
    return jnp.where(flip, other, block)


def prepare(packed, table, keys, keys_t, values, values_t, blocks, flip):
    queries = []
    half = ROT // 2
    for i in range(blocks):
        cols = slice(i * BLOCK, (i + 1) * BLOCK)
        cosine, sines = (table[:half, cols], table[half:, cols])
        query = in_order(packed[i, 0].astype(jnp.float32), flip)
        query = turned(query, cosine, sines).astype(jnp.bfloat16)
        queries.append(query * jnp.bfloat16(HEAD**-0.5))
        key = in_order(packed[i, 1].astype(jnp.float32), flip)
        key = turned(key, cosine, sines).astype(jnp.bfloat16)
        keys[cols, :] = key.T
        value = in_order(packed[i, 2].astype(jnp.float32), flip).astype(jnp.bfloat16)
        if keys_t is not None:
            keys_t[:, cols] = key
        if values is not None:
            values[cols, :] = value.T
        if values_t is not None:
            values_t[:, cols] = value
    return queries


def masked(scores, i, starts):
    row = lax.broadcasted_iota(jnp.int32, scores.shape, 0)
    in_document = jnp.where(row >= starts, scores, -1e30)
    last = in_document[i * BLOCK :]
    row = lax.broadcasted_iota(jnp.int32, last.shape, 0)
    col = lax.broadcasted_iota(jnp.int32, last.shape, 1)
    last = jnp.where(row <= col, last, -1e30)
    return jnp.concatenate([in_document[: i * BLOCK], last], axis=0) if i > 0 else last


def attend_kernel(core, packed, table, starts, out, wide, log_total, keys, values_t):
    blocks = packed.shape[0]
    flip = core[0] == 1
    queries = prepare(packed, table, keys, None, None, values_t, blocks, flip)
    for i in range(blocks):
        length = (i + 1) * BLOCK
        scores = dot(keys[:length], queries[i], ((1,), (0,)))
        scores = masked(scores, i, starts[:, i * BLOCK : length])
        largest = jnp.max(scores, axis=0, keepdims=True)
        exponent = jnp.exp(scores - largest)
        total = jnp.sum(exponent, axis=0, keepdims=True)
        result = dot(values_t[:, :length], exponent.astype(jnp.bfloat16), ((1,), (0,)))
        result = result / total
        wide[i] = result
        out[i] = in_order(result, flip).astype(jnp.bfloat16)
        log_total[i] = largest + jnp.log(total)


SCALAR = pl.BlockSpec(memory_space=pltpu.SMEM)
WHOLE = pl.BlockSpec(memory_space=pltpu.VMEM)


def attend(core, packed, table, starts, work=()):
    blocks = packed.shape[0]
    full = blocks * BLOCK
    return pl.pallas_call(
        skipping(attend_kernel, 4, len(work)),
        out_shape=(
            jax.ShapeDtypeStruct((blocks, HEAD, BLOCK), jnp.bfloat16),
            jax.ShapeDtypeStruct((blocks, HEAD, BLOCK), jnp.float32),
            jax.ShapeDtypeStruct((blocks, 1, BLOCK), jnp.float32),
        ),
        in_specs=[SCALAR] + [WHOLE] * 3 + [UNREAD] * len(work),
        scratch_shapes=[
            pltpu.VMEM((full, HEAD), jnp.bfloat16),
            pltpu.VMEM((HEAD, full), jnp.bfloat16),
        ],
        compiler_params=pltpu.CompilerParams(vmem_limit_bytes=VMEM_BYTES),
        cost_estimate=pl.CostEstimate(
            flops=4 * full * full * HEAD, bytes_accessed=2**21, transcendentals=full * full // 2
        ),
    )(core, packed, table, starts, *work)


def attend_back_kernel(
    core,
    packed,
    table,
    starts,
    wide,
    log_total,
    upper,
    out,
    keys,
    keys_t,
    values,
    grad_k,
    grad_v,
):
    blocks = packed.shape[0]
    half = ROT // 2
    flip = core[0] == 1
    queries = prepare(packed, table, keys, keys_t, values, None, blocks, flip)
    for i in range(blocks):
        length = (i + 1) * BLOCK
        cols = slice(i * BLOCK, length)
        scores = dot(keys[:length], queries[i], ((1,), (0,)))
        probs = jnp.exp(masked(scores, i, starts[:, cols]) - log_total[i])
        above = in_order(upper[i].astype(jnp.float32), flip).astype(jnp.bfloat16)
        grad_probs = dot(values[:length], above, ((1,), (0,)))
        row_dot = jnp.sum(above.astype(jnp.float32) * wide[i], axis=0, keepdims=True)
        grad_scores = (probs * (grad_probs - row_dot)).astype(jnp.bfloat16)
        grad_q = dot(keys_t[:, :length], grad_scores, ((1,), (0,))) * HEAD**-0.5
        cosine, sines = (table[:half, cols], table[half:, cols])
        out[i, 0] = in_order(turned(grad_q, cosine, -sines), flip).astype(jnp.bfloat16)
        probs_low = probs.astype(jnp.bfloat16)
        part_v = dot(above, probs_low, ((1,), (1,)))
        part_k = dot(queries[i], grad_scores, ((1,), (1,)))
        if i > 0:
            grad_v[:, : i * BLOCK] += part_v[:, : i * BLOCK]
            grad_k[:, : i * BLOCK] += part_k[:, : i * BLOCK]
        grad_v[:, cols] = part_v[:, cols]
        grad_k[:, cols] = part_k[:, cols]
    for i in range(blocks):
        cols = slice(i * BLOCK, (i + 1) * BLOCK)
        cosine, sines = (table[:half, cols], table[half:, cols])
        out[i, 1] = in_order(turned(grad_k[:, cols], cosine, -sines), flip).astype(jnp.bfloat16)
        out[i, 2] = in_order(grad_v[:, cols], flip).astype(jnp.bfloat16)


def attend_both_kernel(
    core, packed, table, starts, upper, out, keys, keys_t, values, values_t, grad_k, grad_v
):
    blocks = packed.shape[0]
    half = ROT // 2
    flip = core[0] == 1
    queries = prepare(packed, table, keys, keys_t, values, values_t, blocks, flip)
    for i in range(blocks):
        length = (i + 1) * BLOCK
        cols = slice(i * BLOCK, length)
        scores = dot(keys[:length], queries[i], ((1,), (0,)))
        scores = masked(scores, i, starts[:, cols])
        exponent = jnp.exp(scores - jnp.max(scores, axis=0, keepdims=True))
        share = 1.0 / jnp.sum(exponent, axis=0, keepdims=True)
        probs = exponent * share
        probs_low = probs.astype(jnp.bfloat16)
        result = dot(values_t[:, :length], probs_low, ((1,), (0,)))
        out[i, 3] = in_order(result, flip).astype(jnp.bfloat16)
        above = in_order(upper[i].astype(jnp.float32), flip)
        row_dot = jnp.sum(above * result, axis=0, keepdims=True)
        above = above.astype(jnp.bfloat16)
        grad_probs = dot(values[:length], above, ((1,), (0,)))
        grad_scores = (probs * (grad_probs - row_dot)).astype(jnp.bfloat16)
        grad_q = dot(keys_t[:, :length], grad_scores, ((1,), (0,))) * HEAD**-0.5
        cosine, sines = (table[:half, cols], table[half:, cols])
        out[i, 0] = in_order(turned(grad_q, cosine, -sines), flip).astype(jnp.bfloat16)
        part_v = dot(above, probs_low, ((1,), (1,)))
        part_k = dot(queries[i], grad_scores, ((1,), (1,)))
        if i > 0:
            grad_v[:, : i * BLOCK] += part_v[:, : i * BLOCK]
            grad_k[:, : i * BLOCK] += part_k[:, : i * BLOCK]
        grad_v[:, cols] = part_v[:, cols]
        grad_k[:, cols] = part_k[:, cols]
    for i in range(blocks):
        cols = slice(i * BLOCK, (i + 1) * BLOCK)
        cosine, sines = (table[:half, cols], table[half:, cols])
        out[i, 1] = in_order(turned(grad_k[:, cols], cosine, -sines), flip).astype(jnp.bfloat16)
        out[i, 2] = in_order(grad_v[:, cols], flip).astype(jnp.bfloat16)


def attend_both(core, packed, table, starts, upper):
    blocks = packed.shape[0]
    full = blocks * BLOCK
    return pl.pallas_call(
        attend_both_kernel,
        out_shape=jax.ShapeDtypeStruct((blocks, 4, HEAD, BLOCK), jnp.bfloat16),
        in_specs=[SCALAR] + [WHOLE] * 4,
        scratch_shapes=[
            pltpu.VMEM((full, HEAD), jnp.bfloat16),
            pltpu.VMEM((HEAD, full), jnp.bfloat16),
            pltpu.VMEM((full, HEAD), jnp.bfloat16),
            pltpu.VMEM((HEAD, full), jnp.bfloat16),
            pltpu.VMEM((HEAD, full), jnp.float32),
            pltpu.VMEM((HEAD, full), jnp.float32),
        ],
        compiler_params=pltpu.CompilerParams(vmem_limit_bytes=VMEM_BYTES),
        cost_estimate=pl.CostEstimate(
            flops=12 * full * full * HEAD, bytes_accessed=2**22, transcendentals=full * full // 2
        ),
    )(core, packed, table, starts, upper)


def attend_back(core, packed, table, starts, wide, log_total, upper, work=()):
    blocks = packed.shape[0]
    full = blocks * BLOCK
    return pl.pallas_call(
        skipping(attend_back_kernel, 7, len(work)),
        out_shape=jax.ShapeDtypeStruct((blocks, 3, HEAD, BLOCK), jnp.bfloat16),
        in_specs=[SCALAR] + [WHOLE] * 6 + [UNREAD] * len(work),
        scratch_shapes=[
            pltpu.VMEM((full, HEAD), jnp.bfloat16),
            pltpu.VMEM((HEAD, full), jnp.bfloat16),
            pltpu.VMEM((full, HEAD), jnp.bfloat16),
            pltpu.VMEM((HEAD, full), jnp.float32),
            pltpu.VMEM((HEAD, full), jnp.float32),
        ],
        compiler_params=pltpu.CompilerParams(vmem_limit_bytes=VMEM_BYTES),
        cost_estimate=pl.CostEstimate(
            flops=10 * full * full * HEAD, bytes_accessed=2**22, transcendentals=full * full // 2
        ),
    )(core, packed, table, starts, wide, log_total, upper, *work)


def exchange(blocks, axis, groups=None):
    return lax.all_to_all(blocks, axis, 0, 0, tiled=True, axis_index_groups=groups)


def sent_to_all(shard, axis, groups=None):
    size = lax.axis_size(axis) if groups is None else len(groups[0])
    return exchange(jnp.broadcast_to(shard, (size, *shard.shape)), axis, groups)


UNREAD = pl.BlockSpec(memory_space=pl.ANY)


def skipping(kernel, first, count):
    return lambda *refs: kernel(*refs[:first], *refs[first + count :])


def after(value, *work):
    return pl.pallas_call(
        lambda *refs: None,
        out_shape=jax.ShapeDtypeStruct(value.shape, value.dtype),
        in_specs=[UNREAD] * (1 + len(work)),
        out_specs=UNREAD,
        input_output_aliases={0: 0},
        cost_estimate=pl.CostEstimate(flops=0, bytes_accessed=0, transcendentals=0),
    )(value, *work)


def along(distance):
    return [
        (2 * z + core, 2 * ((z + distance) % 4) + core) for z in range(4) for core in range(2)
    ]


def gathered(own, work=(), late=()):
    pieces = [lax.ppermute(own, "tensor", along(-r)) for r in range(1, 4)]
    if late:
        pieces = [after(piece, *late) for piece in pieces]
    mine = jnp.stack([own, *pieces])
    if work:
        mine = after(mine, *work)
    return mine, lax.ppermute(mine, "tensor", ACROSS)


def half_kernel(mine, got, *outs):
    for r, out in enumerate(outs):
        out[...] = (mine[r].astype(jnp.float32) + got[r].astype(jnp.float32)).astype(jnp.bfloat16)


def half_sum(mine, other):
    got = lax.ppermute(other, "tensor", ACROSS)
    return pl.pallas_call(
        half_kernel,
        out_shape=(jax.ShapeDtypeStruct(mine.shape[1:], jnp.bfloat16),) * 4,
        in_specs=[WHOLE] * 2,
        compiler_params=pltpu.CompilerParams(vmem_limit_bytes=VMEM_BYTES),
        cost_estimate=pl.CostEstimate(flops=2**20, bytes_accessed=2**22, transcendentals=0),
    )(mine, got)


def z_terms(half):
    return [half[0]] + [lax.ppermute(half[r], "tensor", along(r)) for r in range(1, 4)]


def z_sum(half):
    total = 0.0
    for term in z_terms(half):
        total = total + term.astype(jnp.float32)
    return total


def settle_kernel(one, two, three, four, residual, bias, out, hat, scale, hat_low):
    total = one[...].astype(jnp.float32) + two[...].astype(jnp.float32)
    total = total + three[...].astype(jnp.float32) + four[...].astype(jnp.float32)
    total = residual[...] + (total + bias[...])
    out[...] = total
    hat[...], scale[...] = normalised(total)
    hat_low[...] = hat[...].astype(jnp.bfloat16)


def settled(terms, residual, bias):
    wide = jax.ShapeDtypeStruct(residual.shape, jnp.float32)
    return pl.pallas_call(
        settle_kernel,
        out_shape=(
            wide,
            wide,
            jax.ShapeDtypeStruct((residual.shape[0], 1), jnp.float32),
            jax.ShapeDtypeStruct(residual.shape, jnp.bfloat16),
        ),
        in_specs=[WHOLE] * 6,
        compiler_params=pltpu.CompilerParams(vmem_limit_bytes=VMEM_BYTES),
        cost_estimate=pl.CostEstimate(flops=2**21, bytes_accessed=2**22, transcendentals=0),
    )(*terms, residual, bias)


def through_norm_kernel(one, two, three, four, grad, hat, scale, out):
    total = one[...].astype(jnp.float32) + two[...].astype(jnp.float32)
    total = total + three[...].astype(jnp.float32) + four[...].astype(jnp.float32)
    total = grad[...].astype(jnp.float32) + norm_back(total, hat[...], scale[...])
    out[...] = total.astype(jnp.bfloat16)


def through_norm(terms, grad, hat, scale):
    return pl.pallas_call(
        through_norm_kernel,
        out_shape=jax.ShapeDtypeStruct(grad.shape, jnp.bfloat16),
        in_specs=[WHOLE] * 7,
        compiler_params=pltpu.CompilerParams(vmem_limit_bytes=VMEM_BYTES),
        cost_estimate=pl.CostEstimate(flops=2**21, bytes_accessed=2**22, transcendentals=0),
    )(*terms, grad, hat, scale)


def swapped(tokens, core):
    halves = tokens.reshape(4, 2, 128, tokens.shape[-1])
    return jnp.where(core == 0, halves, halves[:, ::-1]).reshape(tokens.shape)


def swapped_rows(block, flip):
    half = block.shape[0] // 2
    other = jnp.concatenate([block[half:], block[:half]], axis=0)
    return jnp.where(flip, other, block)


def own_rows(tokens, along_z, half):
    blocks = tokens.reshape(4, 2, 128, tokens.shape[-1])
    return lax.dynamic_index_in_dim(
        lax.dynamic_index_in_dim(blocks, along_z, 0, False), half, 0, False
    )


def in_steps(
    kernel, out_shape, in_specs, out_specs, operands, flops, work=(), scratch=(), alias=None
):
    return pl.pallas_call(
        skipping(kernel, len(operands), len(work)),
        out_shape=out_shape,
        grid_spec=pltpu.PrefetchScalarGridSpec(
            num_scalar_prefetch=1,
            grid=(4,),
            in_specs=[*in_specs, *([UNREAD] * len(work))],
            out_specs=out_specs,
            scratch_shapes=scratch,
        ),
        input_output_aliases={} if alias is None else alias,
        compiler_params=pltpu.CompilerParams(vmem_limit_bytes=VMEM_BYTES),
        cost_estimate=pl.CostEstimate(
            flops=flops, bytes_accessed=2**23 if flops else 2**10, transcendentals=0
        ),
    )(*operands, *work)


def distance_of(b, spot):
    return lax.rem(b - spot[0] + 4, 4)


def columns_of(weight, width, block):
    return pl.BlockSpec((weight.shape[0], width), lambda b, spot: (0, block))


def rows_of(weight, width, block):
    return pl.BlockSpec((BLOCK, width), lambda i, spot: (i, block))


def whole_of(array):
    return pl.BlockSpec(array.shape, lambda i, spot: (0,) * array.ndim)


PIECE = pl.BlockSpec((1, 128, D), lambda b, spot: (distance_of(b, spot), 0, 0))
TOKENS = pl.BlockSpec((BLOCK, D), lambda b, spot: (b, 0))
ALL_TOKENS = jax.ShapeDtypeStruct((1024, D), jnp.bfloat16)
HALVES = (PIECE, PIECE)
ALL_HALVES = (jax.ShapeDtypeStruct((4, 128, D), jnp.bfloat16),) * 2


def project_block(hat, gain, shift, qkv, bias, one, two, packed):
    first = (hat * gain[0:1] + shift[0:1]).astype(jnp.bfloat16)
    one[...] = first
    two[...] = (hat * gain[1:2] + shift[1:2]).astype(jnp.bfloat16)
    flat = (dot(first, qkv[...], ((1,), (0,))) + bias[...]).T.astype(jnp.bfloat16)
    for k in range(3):
        for j in range(2):
            at = (2 * k + j) * HEAD
            packed[j, k] = flat[at : at + HEAD]


def project_input_kernel(spot, start, gain, shift, qkv, bias, one, two, packed):
    block = swapped_rows(start[...].astype(jnp.float32), spot[1] == 1)
    hat, _ = normalised(block)
    project_block(hat, gain, shift, qkv, bias, one, two, packed)


def project_kernel(spot, mine, other, gain, shift, qkv, bias, one, two, packed):
    hat = jnp.concatenate([mine[0], other[0]], axis=0).astype(jnp.float32)
    project_block(hat, gain, shift, qkv, bias, one, two, packed)


def project(spot, tokens, pair, qkv, bias, work):
    qkv, block = qkv
    kernel = project_input_kernel if len(tokens) == 1 else project_kernel
    return in_steps(
        kernel,
        (ALL_TOKENS, ALL_TOKENS, jax.ShapeDtypeStruct((8, 3, HEAD, BLOCK), jnp.bfloat16)),
        [
            *([TOKENS] if len(tokens) == 1 else [PIECE, PIECE]),
            whole_of(pair[0]),
            whole_of(pair[1]),
            columns_of(qkv, 6 * HEAD, block),
            whole_of(bias),
        ],
        (TOKENS, TOKENS, pl.BlockSpec((2, 3, HEAD, BLOCK), lambda b, spot: (b, 0, 0, 0))),
        (spot, *tokens, *pair, qkv, bias),
        2 * 1024 * 384 * D,
        work,
    )


def last_of(blocks, count, place):
    if blocks.ndim == 3:
        return pl.BlockSpec((count, HEAD, BLOCK), lambda i, spot: (place(i), 0, 0))
    return pl.BlockSpec((count, None, HEAD, BLOCK), lambda i, spot: (place(i), 3, 0, 0))


def out_kernel(spot, hidden, heads, fc2, dense, mine, other):
    result = dot(hidden[...], fc2[...], ((1,), (1,)))
    block = jnp.concatenate([heads[0], heads[1]], axis=0).T
    result = result + dot(block, dense[...], ((1,), (1,)))
    mine[0] = result[:128].astype(jnp.bfloat16)
    other[0] = result[128:].astype(jnp.bfloat16)


def branch_sums(spot, hidden, heads, fc2, dense, work=(), flops=2**31):
    (fc2, fc2_block), (dense, dense_block) = (fc2, dense)
    return in_steps(
        out_kernel,
        ALL_HALVES,
        [
            pl.BlockSpec((BLOCK, hidden.shape[1]), lambda b, spot: (b, 0)),
            last_of(heads, 2, lambda b: b),
            columns_of(fc2, hidden.shape[1], fc2_block),
            columns_of(dense, 2 * HEAD, dense_block),
        ],
        HALVES,
        (spot, hidden, heads, fc2, dense),
        flops,
        work,
    )


def to_norms(grad_heads, grad_pre, qkv, fc1, gain):
    block = jnp.concatenate([grad_heads[j, k] for k in range(3) for j in range(2)], axis=0)
    result = dot(block.T, qkv[...], ((1,), (1,))) * gain[0:1]
    return result + dot(grad_pre[...], fc1[...], ((1,), (1,))) * gain[1:2]


def back_kernel(spot, grad_heads, grad_pre, qkv, fc1, gain, mine, other):
    result = to_norms(grad_heads, grad_pre, qkv, fc1, gain)
    mine[0] = result[:128].astype(jnp.bfloat16)
    other[0] = result[128:].astype(jnp.bfloat16)


def back_input_kernel(
    spot, grad_heads, grad_pre, qkv, fc1, gain, start, out_mine, out_other, change
):
    result = to_norms(grad_heads, grad_pre, qkv, fc1, gain)
    z, core = (spot[0], spot[1])
    hat, scale = normalised(swapped_rows(start[...].astype(jnp.float32), core == 1))
    change[...] = swapped_rows(norm_back(result, hat, scale), core == 1)
    for r in range(4):
        for j, out in enumerate((out_mine, out_other)):
            owner = 2 * lax.rem(z + r, 4) + lax.rem(core + j, 2)
            lanes = pl.ds(pl.multiple_of(owner * 128, 128), 128)
            out[r] = change[:, lanes].astype(jnp.bfloat16)


def norm_gradient(spot, grad_heads, grad_pre, qkv, fc1, gain, start=None, work=()):
    (qkv, qkv_block), (fc1, fc1_block) = (qkv, fc1)
    width = grad_pre.shape[1]
    in_specs = [
        pl.BlockSpec((2, 3, HEAD, BLOCK), lambda b, spot: (b, 0, 0, 0)),
        pl.BlockSpec((BLOCK, width), lambda b, spot: (b, 0)),
        columns_of(qkv, 6 * HEAD, qkv_block),
        columns_of(fc1, width, fc1_block),
        whole_of(gain),
    ]
    flops = 2 * 1024 * 896 * D
    operands = (spot, grad_heads, grad_pre, qkv, fc1, gain)
    if start is None:
        return in_steps(back_kernel, ALL_HALVES, in_specs, HALVES, operands, flops, work)
    flops = 0
    return in_steps(
        back_input_kernel,
        (jax.ShapeDtypeStruct((4, 1024, 128), jnp.bfloat16),) * 2,
        [*in_specs, TOKENS],
        (pl.BlockSpec((4, BLOCK, 128), lambda b, spot: (0, b, 0)),) * 2,
        (*operands, start),
        flops,
        work,
        [pltpu.VMEM((BLOCK, D), jnp.float32)],
    )


def join_kernel(spot, mine, other, out):
    core = spot[1]
    out[pl.ds(pl.multiple_of(core * 128, 128), 128), :] = mine[0]
    out[pl.ds(pl.multiple_of((1 - core) * 128, 128), 128), :] = other[0]


def joined(spot, mine, other):
    return in_steps(join_kernel, ALL_TOKENS, [PIECE, PIECE], TOKENS, (spot, mine, other), 0)


def head_gradient(block, dense, upper):
    flat = dot(block, dense[...], ((1,), (0,))).T.astype(jnp.bfloat16)
    upper[0] = flat[:HEAD]
    upper[1] = flat[HEAD:]


def gradient_kernel(spot, mine, other, dense, out, upper):
    block = jnp.concatenate([mine[0], other[0]], axis=0)
    out[...] = block
    head_gradient(block, dense, upper)


def columns_kernel(spot, mine, other, dense, out, upper):
    z, core = (spot[0], spot[1])
    for r in range(4):
        for j, pieces in enumerate((mine, other)):
            owner = 2 * lax.rem(z + r, 4) + lax.rem(core + j, 2)
            piece = swapped_rows(pieces[r].astype(jnp.float32), core == 1)
            lanes = pl.ds(pl.multiple_of(owner * 128, 128), 128)
            out[:, lanes] = piece.astype(jnp.bfloat16)
    head_gradient(out[...], dense, upper)


def top_gradient(spot, pieces, dense, work=()):
    dense, block = dense
    kernel, specs = (gradient_kernel, [PIECE, PIECE])
    if pieces[0].shape[2] < D:
        kernel = columns_kernel
        specs = [pl.BlockSpec((4, BLOCK, 128), lambda b, spot: (0, b, 0))] * 2
    return in_steps(
        kernel,
        (ALL_TOKENS, jax.ShapeDtypeStruct((8, HEAD, BLOCK), jnp.bfloat16)),
        [*specs, columns_of(dense, 2 * HEAD, block)],
        (TOKENS, pl.BlockSpec((2, HEAD, BLOCK), lambda b, spot: (b, 0, 0))),
        (spot, *pieces, dense),
        2 * 1024 * 128 * D,
        work,
    )


def as_row(column):
    return jnp.broadcast_to(column, (column.shape[0], 128)).T[:1]


def norm_sums(weight, grad_weight, sums, product, shift):
    wide = weight.astype(jnp.float32)
    product[...] = as_row(jnp.sum(wide * grad_weight, axis=1, keepdims=True))
    shift[...] = as_row(jnp.sum(wide * sums, axis=1, keepdims=True))


def feed_block(normed, grad_low, grad_pre, hidden, fc1, out, product, shift, sums):
    @pl.when(pl.program_id(0) == 0)
    def _():
        total = jnp.sum(grad_pre[...].astype(jnp.float32), axis=0, keepdims=True)
        sums[...] = total

    width = grad_pre.shape[1]
    grad_fc1 = dot(normed[...], grad_pre[...], ((0,), (0,)))
    out[:, :width] = grad_fc1.astype(jnp.bfloat16)
    grad_fc2 = dot(grad_low[...], hidden[...], ((0,), (0,)))
    out[:, width : 2 * width] = grad_fc2.astype(jnp.bfloat16)
    norm_sums(fc1[...], grad_fc1, sums[...], product, shift)


def dense_block(grad_low, heads):
    total = 0.0
    for b in range(4):
        block = jnp.concatenate([heads[2 * b], heads[2 * b + 1]], axis=0)
        total = total + dot(block, grad_low[b * BLOCK : (b + 1) * BLOCK], ((1,), (0,)))
    return total.T.astype(jnp.bfloat16)


def heads_block(normed, grad_heads, qkv, out, product, shift, sums, columns):
    @pl.when(pl.program_id(0) == 0)
    def _():
        for b in range(4):
            for k in range(3):
                for j in range(2):
                    at = (2 * k + j) * HEAD
                    columns[at : at + HEAD, b * BLOCK : (b + 1) * BLOCK] = grad_heads[2 * b + j, k]
        wide = columns[...].astype(jnp.float32)
        sums[...] = as_row(jnp.sum(wide, axis=1, keepdims=True))

    grad_qkv = dot(columns[...], normed[...], ((1,), (0,))).T
    if len(out.shape) == 2:
        out[:, : 6 * HEAD] = grad_qkv.astype(jnp.bfloat16)
    else:
        out[...] = grad_qkv.astype(jnp.bfloat16).reshape(out.shape)
    norm_sums(qkv[...], grad_qkv, sums[...], product, shift)


def feed_kernel(spot, *refs):
    feed_block(*refs)


def feed_dense_kernel(
    spot, normed, grad_low, grad_pre, hidden, fc1, heads, more, out, product, shift, sums
):
    feed_block(normed, grad_low, grad_pre, hidden, fc1, out, product, shift, sums)
    at = 2 * grad_pre.shape[1]
    out[:, at : at + 2 * HEAD] = dense_block(grad_low, heads)
    out[:, at + 2 * HEAD :] = more[...]


def heads_kernel(spot, *refs):
    heads_block(*refs)


def heads_dense_kernel(
    spot, normed, grad_heads, qkv, grad_low, heads, out, product, shift, sums, columns
):
    heads_block(normed, grad_heads, qkv, out, product, shift, sums, columns)
    out[:, 6 * HEAD :] = dense_block(grad_low, heads)


FEATURES = pl.BlockSpec((1024, BLOCK), lambda i, spot: (0, i))
ROW = pl.BlockSpec((1, BLOCK), lambda i, spot: (0, i))
ROWS = jax.ShapeDtypeStruct((1, D), jnp.float32)


def weight_gradient(
    kernel, spot, operands, in_specs, width, summed_width, scratch, work, tiled=None
):
    shape, block = ((D, width), pl.BlockSpec((BLOCK, width), lambda i, spot: (i, 0)))
    if tiled is not None:
        shape = (16, tiled, width)
        block = pl.BlockSpec((4, 64, width), lambda i, spot: (i, 0, 0))
    return in_steps(
        kernel,
        (
            jax.ShapeDtypeStruct(shape, jnp.bfloat16),
            ROWS,
            ROWS,
            jax.ShapeDtypeStruct((1, summed_width), jnp.float32),
        ),
        in_specs,
        (
            block,
            ROW,
            ROW,
            pl.BlockSpec((1, summed_width), lambda i, spot: (0, 0)),
        ),
        (spot, *operands),
        0,
        work,
        scratch,
    )


def feed_gradient(spot, normed, grad_low, grad_pre, hidden, fc1, heads=None, more=None, work=()):
    width = hidden.shape[1]
    operands = [normed, grad_low, grad_pre, hidden, fc1[0]]
    in_specs = [FEATURES, FEATURES, whole_of(grad_pre), whole_of(hidden)]
    in_specs += [rows_of(fc1[0], width, fc1[1])]
    kernel, total = (feed_kernel, 2 * width)
    if heads is not None:
        operands += [heads, more]
        in_specs += [last_of(heads, 8, lambda i: 0), rows_of(more, more.shape[1], 0)]
        kernel, total = (feed_dense_kernel, total + 2 * HEAD + more.shape[1])
    return weight_gradient(kernel, spot, operands, in_specs, total, width, (), work)


def heads_gradient(
    spot, normed, grad_heads, qkv, grad_low=None, heads=None, work=(), tiled=None
):
    width = 6 * HEAD
    operands = [normed, grad_heads, qkv[0]]
    in_specs = [
        FEATURES,
        pl.BlockSpec((8, 3, HEAD, BLOCK), lambda i, spot: (0, 0, 0, 0)),
        rows_of(qkv[0], width, qkv[1]),
    ]
    kernel, total = (heads_kernel, width)
    if heads is not None:
        operands += [grad_low, heads]
        in_specs += [FEATURES, last_of(heads, 8, lambda i: 0)]
        kernel, total = (heads_dense_kernel, width + 2 * HEAD)
    scratch = [pltpu.VMEM((width, 1024), jnp.bfloat16)]
    return weight_gradient(
        kernel, spot, operands, in_specs, total, width, scratch, work, tiled
    )


def normalised(values):
    centred = values - jnp.mean(values, axis=-1, keepdims=True)
    variance = jnp.mean(centred * centred, axis=-1, keepdims=True)
    scale = lax.rsqrt(variance + epsilon)
    return centred * scale, scale


def norm_back(grad, hat, scale):
    mean = jnp.mean(grad, axis=-1, keepdims=True)
    along = jnp.mean(grad * hat, axis=-1, keepdims=True)
    return scale * (grad - mean - hat * along)


def gelu_and_slope(values):
    share = 0.5 * (1.0 + lax.erf(values * math.sqrt(0.5)))
    slope = share + values * jnp.exp(-0.5 * values * values) * (1.0 / math.sqrt(2.0 * math.pi))
    return (values * share).astype(jnp.bfloat16), slope


def low(values):
    return values.astype(jnp.bfloat16)


def shards(inputs, w_qkv, w_dense, w_fc1, w_fc2, norm_gain, biases, segment_ids, cotangent):
    tensor_rank = lax.axis_index("tensor")
    seq_rank = lax.axis_index("seq")
    along_z, core = (tensor_rank // 2, tensor_rank % 2)
    core_ref = core.astype(jnp.int32).reshape(1)
    spot = jnp.stack([along_z, core]).astype(jnp.int32)
    owners = 16
    full_len = segment_ids.shape[1]
    head_cols = w_qkv.shape[3]
    hidden_cols = w_fc1.shape[2]
    share = w_qkv.shape[1]
    gain_share = norm_gain.shape[1]
    bias_share = biases.shape[1]
    mine = jnp.arange(8) == tensor_rank

    qkv_flat = w_qkv.reshape(LAYERS, share, 3 * head_cols)
    vectors = jnp.concatenate([norm_gain.reshape(-1), biases.reshape(-1)])
    rows = 16
    vectors = jnp.pad(vectors, (0, rows * 3 * head_cols - vectors.size)).reshape(rows, -1)
    first = jnp.concatenate([qkv_flat[0], vectors], axis=0)
    first = jnp.broadcast_to(first, (owners, *first.shape))
    columns = after(cotangent.reshape(-1, cotangent.shape[-1]), first)
    first = exchange(first, OWNERS)
    both_zero = lax.all_gather(
        jnp.concatenate([w_fc1[0], w_fc2[0], w_dense[0]], axis=1), OWNERS, axis=0, tiled=True
    )
    pieces = gathered(columns)
    heads_one = lax.all_gather(
        jnp.concatenate([qkv_flat[1], w_dense[1]], axis=1), OWNERS, axis=0, tiled=True
    )
    feed_one = lax.all_gather(
        jnp.concatenate([w_fc1[1], w_fc2[1]], axis=1), OWNERS, axis=0, tiled=True
    )
    qkv_zero = first[:, :share].reshape(D, 3 * head_cols)
    vectors = first[:, share:].reshape(owners, -1)[:, : LAYERS * (gain_share + bias_share)]
    gain_vecs = vectors[:, : LAYERS * gain_share].reshape(owners, LAYERS, -1).astype(jnp.float32)
    bias_vecs = vectors[:, LAYERS * gain_share :].reshape(owners, LAYERS, -1).astype(jnp.float32)
    qkv_places = [(qkv_zero, 0), (heads_one, 0)]
    dense_places = [(both_zero, 8), (heads_one, 3)]
    fc1_places = [(both_zero, 0), (feed_one, 0)]
    fc2_places = [(both_zero, 1), (feed_one, 1)]
    fc1_weights = [both_zero[:, :hidden_cols], feed_one[:, :hidden_cols]]
    fc2_weights = [both_zero[:, hidden_cols : 2 * hidden_cols], feed_one[:, hidden_cols:]]

    pairs, qkv_biases, fc1_biases, outer_biases = ([], [], [], [])
    for l in range(LAYERS):
        vec = bias_vecs[:, l].reshape(-1)
        pairs.append((gain_vecs[:, l].reshape(2, D), vec[: 2 * D].reshape(2, D)))
        bias = vec[2 * D : 5 * D].reshape(3, 8, head_cols)
        bias = lax.dynamic_index_in_dim(bias, tensor_rank, 1, False)
        qkv_biases.append(bias.reshape(1, 3 * head_cols))
        bias = vec[6 * D : 6 * D + FF].reshape(8, hidden_cols)
        fc1_biases.append(lax.dynamic_index_in_dim(bias, tensor_rank, 0, True))
        outer_biases.append((vec[5 * D : 6 * D] + vec[6 * D + FF :]).reshape(1, D))

    segments = lax.dynamic_index_in_dim(segment_ids, seq_rank // 2, 0, False)
    earlier = jnp.zeros_like(segments)
    for doc in range(1, DOCUMENTS):
        before = jnp.sum((segments < doc).astype(jnp.int32))
        earlier = jnp.where(segments == doc, before, earlier)
    places = jnp.arange(full_len, dtype=jnp.int32) - earlier
    half_rot = ROT // 2
    inverse = 10000.0 ** (-jnp.arange(half_rot, dtype=jnp.float32) * 2.0 / ROT)
    angles = inverse[:, None] * places.astype(jnp.float32)[None, :]
    table = jnp.concatenate([jnp.cos(angles), jnp.sin(angles)], axis=0)
    starts = earlier[None, :]

    def feed_forward(normed_two, l):
        pre_act = dot(normed_two, fc1_weights[l], ((1,), (0,))) + fc1_biases[l]
        return gelu_and_slope(pre_act)

    def pre_gradient(grad_low, slope, l):
        return low(dot(grad_low, fc2_weights[l], ((1,), (0,))) * slope)

    tokens = inputs.reshape(-1, D)
    residual = own_rows(tokens, along_z, core).astype(jnp.float32)

    one_zero, two_zero, payload = project(
        spot, (tokens,), pairs[0], qkv_places[0], qkv_biases[0], (pieces[1],)
    )
    packed_zero = exchange(payload, "seq")
    prepared = (*pairs[1], qkv_biases[1], fc1_biases[1], outer_biases[0], outer_biases[1])
    result, *kept_zero = attend(core_ref, packed_zero, table, starts, prepared)
    heads_zero = exchange(result, "seq")
    hidden_zero, slope_zero = feed_forward(two_zero, 0)
    partial = branch_sums(spot, hidden_zero, heads_zero, fc2_places[0], dense_places[0])
    terms = z_terms(half_sum(*partial))
    residual, hat, scale, hat_low = settled(terms, residual, outer_biases[0])
    grad_top, upper_payload = top_gradient(spot, pieces, dense_places[1], (partial[0],))
    upper = exchange(upper_payload, "seq")
    hat_pieces = gathered(after(hat_low, upper_payload), (upper,))

    one, two, payload = project(
        spot, hat_pieces, pairs[1], qkv_places[1], qkv_biases[1], ()
    )
    packed = exchange(payload, "seq")

    back = attend_both(core_ref, packed, table, starts, upper)
    grad_heads = exchange(back, "seq")
    two = after(two, back)
    hidden, slope = feed_forward(two, 1)
    grad_pre = pre_gradient(grad_top, slope, 1)
    feed_grads, feed_product, feed_shift, feed_sums = feed_gradient(
        spot, two, grad_top, grad_pre, hidden, fc1_places[1], work=(back,)
    )
    shares_feed = lax.psum_scatter(feed_grads, OWNERS, scatter_dimension=0, tiled=True)
    half = half_sum(
        *norm_gradient(
            spot,
            grad_heads,
            grad_pre,
            qkv_places[1],
            fc1_places[1],
            pairs[1][0],
            work=(feed_grads,),
        )
    )
    terms = z_terms(half)
    weight_grads, heads_product, heads_shift, heads_sums = heads_gradient(
        spot, one, grad_heads, qkv_places[1], grad_top, grad_heads, (half[0],)
    )
    partial = branch_sums(
        spot, hidden, grad_heads, fc2_places[1], dense_places[1], (half[0],), 0
    )
    own_top = own_rows(grad_top, along_z, 0)
    grad_own = through_norm(terms, own_top, hat, scale)
    sums_one = (
        (heads_product, feed_product),
        (heads_shift, feed_shift),
        heads_sums,
        feed_sums,
        jnp.sum(own_top.astype(jnp.float32), axis=0),
    )
    grad_low, upper_payload = top_gradient(
        spot, gathered(after(grad_own, weight_grads, partial[0])), dense_places[0]
    )

    upper = exchange(upper_payload, "seq")
    grad_pre = pre_gradient(grad_low, slope_zero, 0)
    weight_grads, feed_product, feed_shift, feed_sums = feed_gradient(
        spot,
        two_zero,
        grad_low,
        grad_pre,
        hidden_zero,
        fc1_places[0],
        heads_zero,
        weight_grads,
        (upper_payload,),
    )
    shares_more = lax.psum_scatter(weight_grads, OWNERS, scatter_dimension=0, tiled=True)
    back = attend_back(
        core_ref, packed_zero, table, starts, *kept_zero, upper, (weight_grads,)
    )
    grad_heads = exchange(back, "seq")
    half = half_sum(partial[0], after(partial[1], back))
    final = residual + (z_sum(half) + outer_biases[1])
    blocks = norm_gradient(
        spot,
        grad_heads,
        grad_pre,
        qkv_places[0],
        fc1_places[0],
        pairs[0][0],
        tokens,
        (final,),
    )
    out_pieces = gathered(low(final), late=(blocks[0],))
    block_out = joined(spot, *out_pieces).reshape(inputs.shape)
    qkv_grads, heads_product, heads_shift, heads_sums = heads_gradient(
        spot, one_zero, grad_heads, qkv_places[0], work=(blocks[0],), tiled=share + rows
    )
    sums_zero = (
        (heads_product, feed_product),
        (heads_shift, feed_shift),
        heads_sums,
        feed_sums,
        jnp.sum(grad_own.astype(jnp.float32), axis=0),
    )

    def small_gradients(l, products, shift_grads, head_sums, pre_sums, own_sums):
        gain, shift = pairs[l]
        shift_grad = jnp.concatenate(shift_grads, axis=1)
        product = jnp.concatenate(products, axis=1)
        gain_grad = (product - shift.reshape(1, -1) * shift_grad) / gain.reshape(1, -1)
        placed_heads = jnp.where(mine[:, None], head_sums.reshape(3, 1, head_cols), 0.0)
        placed_pre = jnp.where(mine[:, None], pre_sums, 0.0)
        own_sums = own_sums.reshape(1, -1)
        bias_grad = jnp.concatenate(
            [
                shift_grad,
                placed_heads.reshape(1, -1),
                own_sums,
                placed_pre.reshape(1, -1),
                own_sums,
            ],
            axis=1,
        )
        return [bias_grad.reshape(owners, bias_share), gain_grad.reshape(owners, gain_share)]

    small = jnp.concatenate(
        [*small_gradients(0, *sums_zero), *small_gradients(1, *sums_one)], axis=1
    )
    small = jnp.pad(small, ((0, 0), (0, rows * 3 * head_cols - small.shape[1])))
    small = low(small).reshape(owners, rows, -1)
    tiles = lax.dynamic_update_slice(qkv_grads, small, (0, share, 0))
    half = half_sum(*blocks)
    change = z_sum((half[0], after(half[1], block_out), *half[2:]))
    columns = lax.dynamic_slice_in_dim(grad_low, tensor_rank * (D // 8), D // 8, 1)
    grad_inputs = swapped(columns, core).astype(jnp.float32) + change
    grad_inputs = grad_inputs.reshape(cotangent.shape)
    tiles = jnp.sum(exchange(tiles, OWNERS).astype(jnp.float32), axis=0)
    small = tiles[share:].reshape(-1)[: LAYERS * (gain_share + bias_share)]
    small = jnp.sum(sent_to_all(small, "tensor"), axis=0).reshape(LAYERS, -1)
    feed = shares_feed.astype(jnp.float32)
    more = shares_more.astype(jnp.float32)
    grad_qkv = jnp.stack([tiles[:share], more[:, 1152:1536]])
    grad_dense = jnp.stack([more[:, 1024:1152], more[:, 1536:]])
    grad_fc1 = jnp.stack([more[:, :hidden_cols], feed[:, :hidden_cols]])
    grad_fc2 = jnp.stack([more[:, hidden_cols : 2 * hidden_cols], feed[:, hidden_cols:]])
    return (
        block_out,
        grad_inputs,
        grad_qkv.reshape(w_qkv.shape),
        grad_dense,
        grad_fc1,
        grad_fc2,
        small[:, bias_share:],
        small[:, :bias_share],
    )


def solution(mesh):
    in_specs = (
        P("dp", "seq", None),
        P(None, ("dp", "seq"), None, "tensor"),
        P(None, ("dp", "seq"), "tensor"),
        P(None, ("dp", "seq"), "tensor"),
        P(None, ("dp", "seq"), "tensor"),
        P(None, ("dp", "seq")),
        P(None, ("dp", "seq")),
        P("dp", None),
        P("dp", "seq", "tensor"),
    )
    out_specs = (
        P("dp", "seq", None),
        P("dp", "seq", "tensor"),
        P(None, ("dp", "seq"), None, "tensor"),
        P(None, ("dp", "seq"), "tensor"),
        P(None, ("dp", "seq"), "tensor"),
        P(None, ("dp", "seq"), "tensor"),
        P(None, ("dp", "seq")),
        P(None, ("dp", "seq")),
    )
    return jax.shard_map(shards, mesh=mesh, in_specs=in_specs, out_specs=out_specs, check_vma=False)
```

```python
import math

import jax
import jax.numpy as jnp
from jax import lax
from jax.experimental import pallas as pl
from jax.experimental.pallas import tpu as pltpu
from jax.sharding import PartitionSpec as P

D = 1024
FF = 4096
HEAD = 64
ROT = 16
LAYERS = 2
DOCUMENTS = 5
BLOCK = 256
VMEM_BYTES = 48 * 1024 * 1024
OWNERS = ("dp", "seq")
ACROSS = [(2 * z + core, 2 * z + 1 - core) for z in range(4) for core in range(2)]

epsilon = 1e-05


def dot(a, b, dims):
    return lax.dot_general(a, b, (dims, ((), ())), preferred_element_type=jnp.float32)


def turned(block, cosine, sines):
    half = ROT // 2
    low, high = (block[:half], block[half:ROT])
    return jnp.concatenate(
        [low * cosine - high * sines, high * cosine + low * sines, block[ROT:]], axis=0
    )


def in_order(block, flip):
    half = block.shape[-1] // 2
    other = jnp.concatenate([block[..., half:], block[..., :half]], axis=-1)
    return jnp.where(flip, other, block)


def prepare(packed, table, keys, keys_t, values, values_t, blocks, flip):
    queries = []
    half = ROT // 2
    for i in range(blocks):
        cols = slice(i * BLOCK, (i + 1) * BLOCK)
        cosine, sines = (table[:half, cols], table[half:, cols])
        query = in_order(packed[i, 0].astype(jnp.float32), flip)
        query = turned(query, cosine, sines).astype(jnp.bfloat16)
        queries.append(query * jnp.bfloat16(HEAD**-0.5))
        key = in_order(packed[i, 1].astype(jnp.float32), flip)
        key = turned(key, cosine, sines).astype(jnp.bfloat16)
        keys[cols, :] = key.T
        value = in_order(packed[i, 2].astype(jnp.float32), flip).astype(jnp.bfloat16)
        if keys_t is not None:
            keys_t[:, cols] = key
        if values is not None:
            values[cols, :] = value.T
        if values_t is not None:
            values_t[:, cols] = value
    return queries


def masked(scores, i, starts):
    row = lax.broadcasted_iota(jnp.int32, scores.shape, 0)
    in_document = jnp.where(row >= starts, scores, -1e30)
    last = in_document[i * BLOCK :]
    row = lax.broadcasted_iota(jnp.int32, last.shape, 0)
    col = lax.broadcasted_iota(jnp.int32, last.shape, 1)
    last = jnp.where(row <= col, last, -1e30)
    return jnp.concatenate([in_document[: i * BLOCK], last], axis=0) if i > 0 else last


def attend_kernel(core, packed, table, starts, out, wide, log_total, keys, values_t):
    blocks = packed.shape[0]
    flip = core[0] == 1
    queries = prepare(packed, table, keys, None, None, values_t, blocks, flip)
    for i in range(blocks):
        length = (i + 1) * BLOCK
        scores = dot(keys[:length], queries[i], ((1,), (0,)))
        scores = masked(scores, i, starts[:, i * BLOCK : length])
        largest = jnp.max(scores, axis=0, keepdims=True)
        exponent = jnp.exp(scores - largest)
        total = jnp.sum(exponent, axis=0, keepdims=True)
        result = dot(values_t[:, :length], exponent.astype(jnp.bfloat16), ((1,), (0,)))
        result = result / total
        wide[i] = result
        out[i] = in_order(result, flip).astype(jnp.bfloat16)
        log_total[i] = largest + jnp.log(total)


SCALAR = pl.BlockSpec(memory_space=pltpu.SMEM)
WHOLE = pl.BlockSpec(memory_space=pltpu.VMEM)


def attend(core, packed, table, starts, work=()):
    blocks = packed.shape[0]
    full = blocks * BLOCK
    return pl.pallas_call(
        skipping(attend_kernel, 4, len(work)),
        out_shape=(
            jax.ShapeDtypeStruct((blocks, HEAD, BLOCK), jnp.bfloat16),
            jax.ShapeDtypeStruct((blocks, HEAD, BLOCK), jnp.float32),
            jax.ShapeDtypeStruct((blocks, 1, BLOCK), jnp.float32),
        ),
        in_specs=[SCALAR] + [WHOLE] * 3 + [UNREAD] * len(work),
        scratch_shapes=[
            pltpu.VMEM((full, HEAD), jnp.bfloat16),
            pltpu.VMEM((HEAD, full), jnp.bfloat16),
        ],
        compiler_params=pltpu.CompilerParams(vmem_limit_bytes=VMEM_BYTES),
        cost_estimate=pl.CostEstimate(
            flops=4 * full * full * HEAD, bytes_accessed=2**21, transcendentals=full * full // 2
        ),
    )(core, packed, table, starts, *work)


def attend_back_kernel(
    core,
    packed,
    table,
    starts,
    wide,
    log_total,
    upper,
    out,
    keys,
    keys_t,
    values,
    grad_k,
    grad_v,
):
    blocks = packed.shape[0]
    half = ROT // 2
    flip = core[0] == 1
    queries = prepare(packed, table, keys, keys_t, values, None, blocks, flip)
    for i in range(blocks):
        length = (i + 1) * BLOCK
        cols = slice(i * BLOCK, length)
        scores = dot(keys[:length], queries[i], ((1,), (0,)))
        probs = jnp.exp(masked(scores, i, starts[:, cols]) - log_total[i])
        above = in_order(upper[i].astype(jnp.float32), flip).astype(jnp.bfloat16)
        grad_probs = dot(values[:length], above, ((1,), (0,)))
        row_dot = jnp.sum(above.astype(jnp.float32) * wide[i], axis=0, keepdims=True)
        grad_scores = (probs * (grad_probs - row_dot)).astype(jnp.bfloat16)
        grad_q = dot(keys_t[:, :length], grad_scores, ((1,), (0,))) * HEAD**-0.5
        cosine, sines = (table[:half, cols], table[half:, cols])
        out[i, 0] = in_order(turned(grad_q, cosine, -sines), flip).astype(jnp.bfloat16)
        probs_low = probs.astype(jnp.bfloat16)
        part_v = dot(above, probs_low, ((1,), (1,)))
        part_k = dot(queries[i], grad_scores, ((1,), (1,)))
        if i > 0:
            grad_v[:, : i * BLOCK] += part_v[:, : i * BLOCK]
            grad_k[:, : i * BLOCK] += part_k[:, : i * BLOCK]
        grad_v[:, cols] = part_v[:, cols]
        grad_k[:, cols] = part_k[:, cols]
    for i in range(blocks):
        cols = slice(i * BLOCK, (i + 1) * BLOCK)
        cosine, sines = (table[:half, cols], table[half:, cols])
        out[i, 1] = in_order(turned(grad_k[:, cols], cosine, -sines), flip).astype(jnp.bfloat16)
        out[i, 2] = in_order(grad_v[:, cols], flip).astype(jnp.bfloat16)


def attend_both_kernel(
    core, packed, table, starts, upper, out, keys, keys_t, values, values_t, grad_k, grad_v
):
    blocks = packed.shape[0]
    half = ROT // 2
    flip = core[0] == 1
    queries = prepare(packed, table, keys, keys_t, values, values_t, blocks, flip)
    for i in range(blocks):
        length = (i + 1) * BLOCK
        cols = slice(i * BLOCK, length)
        scores = dot(keys[:length], queries[i], ((1,), (0,)))
        scores = masked(scores, i, starts[:, cols])
        exponent = jnp.exp(scores - jnp.max(scores, axis=0, keepdims=True))
        share = 1.0 / jnp.sum(exponent, axis=0, keepdims=True)
        probs = exponent * share
        probs_low = probs.astype(jnp.bfloat16)
        result = dot(values_t[:, :length], probs_low, ((1,), (0,)))
        out[i, 3] = in_order(result, flip).astype(jnp.bfloat16)
        above = in_order(upper[i].astype(jnp.float32), flip)
        row_dot = jnp.sum(above * result, axis=0, keepdims=True)
        above = above.astype(jnp.bfloat16)
        grad_probs = dot(values[:length], above, ((1,), (0,)))
        grad_scores = (probs * (grad_probs - row_dot)).astype(jnp.bfloat16)
        grad_q = dot(keys_t[:, :length], grad_scores, ((1,), (0,))) * HEAD**-0.5
        cosine, sines = (table[:half, cols], table[half:, cols])
        out[i, 0] = in_order(turned(grad_q, cosine, -sines), flip).astype(jnp.bfloat16)
        part_v = dot(above, probs_low, ((1,), (1,)))
        part_k = dot(queries[i], grad_scores, ((1,), (1,)))
        if i > 0:
            grad_v[:, : i * BLOCK] += part_v[:, : i * BLOCK]
            grad_k[:, : i * BLOCK] += part_k[:, : i * BLOCK]
        grad_v[:, cols] = part_v[:, cols]
        grad_k[:, cols] = part_k[:, cols]
    for i in range(blocks):
        cols = slice(i * BLOCK, (i + 1) * BLOCK)
        cosine, sines = (table[:half, cols], table[half:, cols])
        out[i, 1] = in_order(turned(grad_k[:, cols], cosine, -sines), flip).astype(jnp.bfloat16)
        out[i, 2] = in_order(grad_v[:, cols], flip).astype(jnp.bfloat16)


def attend_both(core, packed, table, starts, upper):
    blocks = packed.shape[0]
    full = blocks * BLOCK
    return pl.pallas_call(
        attend_both_kernel,
        out_shape=jax.ShapeDtypeStruct((blocks, 4, HEAD, BLOCK), jnp.bfloat16),
        in_specs=[SCALAR] + [WHOLE] * 4,
        scratch_shapes=[
            pltpu.VMEM((full, HEAD), jnp.bfloat16),
            pltpu.VMEM((HEAD, full), jnp.bfloat16),
            pltpu.VMEM((full, HEAD), jnp.bfloat16),
            pltpu.VMEM((HEAD, full), jnp.bfloat16),
            pltpu.VMEM((HEAD, full), jnp.float32),
            pltpu.VMEM((HEAD, full), jnp.float32),
        ],
        compiler_params=pltpu.CompilerParams(vmem_limit_bytes=VMEM_BYTES),
        cost_estimate=pl.CostEstimate(
            flops=12 * full * full * HEAD, bytes_accessed=2**22, transcendentals=full * full // 2
        ),
    )(core, packed, table, starts, upper)


def attend_back(core, packed, table, starts, wide, log_total, upper, work=()):
    blocks = packed.shape[0]
    full = blocks * BLOCK
    return pl.pallas_call(
        skipping(attend_back_kernel, 7, len(work)),
        out_shape=jax.ShapeDtypeStruct((blocks, 3, HEAD, BLOCK), jnp.bfloat16),
        in_specs=[SCALAR] + [WHOLE] * 6 + [UNREAD] * len(work),
        scratch_shapes=[
            pltpu.VMEM((full, HEAD), jnp.bfloat16),
            pltpu.VMEM((HEAD, full), jnp.bfloat16),
            pltpu.VMEM((full, HEAD), jnp.bfloat16),
            pltpu.VMEM((HEAD, full), jnp.float32),
            pltpu.VMEM((HEAD, full), jnp.float32),
        ],
        compiler_params=pltpu.CompilerParams(vmem_limit_bytes=VMEM_BYTES),
        cost_estimate=pl.CostEstimate(
            flops=10 * full * full * HEAD, bytes_accessed=2**22, transcendentals=full * full // 2
        ),
    )(core, packed, table, starts, wide, log_total, upper, *work)


def exchange(blocks, axis, groups=None):
    return lax.all_to_all(blocks, axis, 0, 0, tiled=True, axis_index_groups=groups)


def sent_to_all(shard, axis, groups=None):
    size = lax.axis_size(axis) if groups is None else len(groups[0])
    return exchange(jnp.broadcast_to(shard, (size, *shard.shape)), axis, groups)


UNREAD = pl.BlockSpec(memory_space=pl.ANY)


def skipping(kernel, first, count):
    return lambda *refs: kernel(*refs[:first], *refs[first + count :])


def after(value, *work):
    return pl.pallas_call(
        lambda *refs: None,
        out_shape=jax.ShapeDtypeStruct(value.shape, value.dtype),
        in_specs=[UNREAD] * (1 + len(work)),
        out_specs=UNREAD,
        input_output_aliases={0: 0},
        cost_estimate=pl.CostEstimate(flops=0, bytes_accessed=0, transcendentals=0),
    )(value, *work)


def along(distance):
    return [
        (2 * z + core, 2 * ((z + distance) % 4) + core) for z in range(4) for core in range(2)
    ]


def gathered(own, work=(), late=()):
    pieces = [lax.ppermute(own, "tensor", along(-r)) for r in range(1, 4)]
    if late:
        pieces = [after(piece, *late) for piece in pieces]
    mine = jnp.stack([own, *pieces])
    if work:
        mine = after(mine, *work)
    return mine, lax.ppermute(mine, "tensor", ACROSS)


def half_kernel(mine, got, *outs):
    for r, out in enumerate(outs):
        out[...] = (mine[r].astype(jnp.float32) + got[r].astype(jnp.float32)).astype(jnp.bfloat16)


def half_sum(mine, other):
    got = lax.ppermute(other, "tensor", ACROSS)
    return pl.pallas_call(
        half_kernel,
        out_shape=(jax.ShapeDtypeStruct(mine.shape[1:], jnp.bfloat16),) * 4,
        in_specs=[WHOLE] * 2,
        compiler_params=pltpu.CompilerParams(vmem_limit_bytes=VMEM_BYTES),
        cost_estimate=pl.CostEstimate(flops=2**20, bytes_accessed=2**22, transcendentals=0),
    )(mine, got)


def z_terms(half):
    return [half[0]] + [lax.ppermute(half[r], "tensor", along(r)) for r in range(1, 4)]


def z_sum(half):
    total = 0.0
    for term in z_terms(half):
        total = total + term.astype(jnp.float32)
    return total


def settle_kernel(one, two, three, four, residual, bias, out, hat, scale, hat_low):
    total = one[...].astype(jnp.float32) + two[...].astype(jnp.float32)
    total = total + three[...].astype(jnp.float32) + four[...].astype(jnp.float32)
    total = residual[...] + (total + bias[...])
    out[...] = total
    hat[...], scale[...] = normalised(total)
    hat_low[...] = hat[...].astype(jnp.bfloat16)


def settled(terms, residual, bias):
    wide = jax.ShapeDtypeStruct(residual.shape, jnp.float32)
    return pl.pallas_call(
        settle_kernel,
        out_shape=(
            wide,
            wide,
            jax.ShapeDtypeStruct((residual.shape[0], 1), jnp.float32),
            jax.ShapeDtypeStruct(residual.shape, jnp.bfloat16),
        ),
        in_specs=[WHOLE] * 6,
        compiler_params=pltpu.CompilerParams(vmem_limit_bytes=VMEM_BYTES),
        cost_estimate=pl.CostEstimate(flops=2**21, bytes_accessed=2**22, transcendentals=0),
    )(*terms, residual, bias)


def through_norm_kernel(one, two, three, four, grad, hat, scale, out):
    total = one[...].astype(jnp.float32) + two[...].astype(jnp.float32)
    total = total + three[...].astype(jnp.float32) + four[...].astype(jnp.float32)
    total = grad[...].astype(jnp.float32) + norm_back(total, hat[...], scale[...])
    out[...] = total.astype(jnp.bfloat16)


def through_norm(terms, grad, hat, scale):
    return pl.pallas_call(
        through_norm_kernel,
        out_shape=jax.ShapeDtypeStruct(grad.shape, jnp.bfloat16),
        in_specs=[WHOLE] * 7,
        compiler_params=pltpu.CompilerParams(vmem_limit_bytes=VMEM_BYTES),
        cost_estimate=pl.CostEstimate(flops=2**21, bytes_accessed=2**22, transcendentals=0),
    )(*terms, grad, hat, scale)


def swapped(tokens, core):
    halves = tokens.reshape(4, 2, 128, tokens.shape[-1])
    return jnp.where(core == 0, halves, halves[:, ::-1]).reshape(tokens.shape)


def swapped_rows(block, flip):
    half = block.shape[0] // 2
    other = jnp.concatenate([block[half:], block[:half]], axis=0)
    return jnp.where(flip, other, block)


def own_rows(tokens, along_z, half):
    blocks = tokens.reshape(4, 2, 128, tokens.shape[-1])
    return lax.dynamic_index_in_dim(
        lax.dynamic_index_in_dim(blocks, along_z, 0, False), half, 0, False
    )


def in_steps(
    kernel, out_shape, in_specs, out_specs, operands, flops, work=(), scratch=(), alias=None
):
    return pl.pallas_call(
        skipping(kernel, len(operands), len(work)),
        out_shape=out_shape,
        grid_spec=pltpu.PrefetchScalarGridSpec(
            num_scalar_prefetch=1,
            grid=(4,),
            in_specs=[*in_specs, *([UNREAD] * len(work))],
            out_specs=out_specs,
            scratch_shapes=scratch,
        ),
        input_output_aliases={} if alias is None else alias,
        compiler_params=pltpu.CompilerParams(vmem_limit_bytes=VMEM_BYTES),
        cost_estimate=pl.CostEstimate(
            flops=flops, bytes_accessed=2**23 if flops else 2**10, transcendentals=0
        ),
    )(*operands, *work)


def distance_of(b, spot):
    return lax.rem(b - spot[0] + 4, 4)


def columns_of(weight, width, block):
    return pl.BlockSpec((weight.shape[0], width), lambda b, spot: (0, block))


def rows_of(weight, width, block):
    return pl.BlockSpec((BLOCK, width), lambda i, spot: (i, block))


def whole_of(array):
    return pl.BlockSpec(array.shape, lambda i, spot: (0,) * array.ndim)


PIECE = pl.BlockSpec((1, 128, D), lambda b, spot: (distance_of(b, spot), 0, 0))
TOKENS = pl.BlockSpec((BLOCK, D), lambda b, spot: (b, 0))
ALL_TOKENS = jax.ShapeDtypeStruct((1024, D), jnp.bfloat16)
HALVES = (PIECE, PIECE)
ALL_HALVES = (jax.ShapeDtypeStruct((4, 128, D), jnp.bfloat16),) * 2


def project_block(hat, gain, shift, qkv, bias, one, two, packed):
    first = (hat * gain[0:1] + shift[0:1]).astype(jnp.bfloat16)
    one[...] = first
    two[...] = (hat * gain[1:2] + shift[1:2]).astype(jnp.bfloat16)
    weight = qkv[...].reshape(D, 6 * HEAD)
    flat = (dot(first, weight, ((1,), (0,))) + bias[...]).T.astype(jnp.bfloat16)
    for k in range(3):
        for j in range(2):
            at = (2 * k + j) * HEAD
            packed[j, k] = flat[at : at + HEAD]


def project_input_kernel(spot, start, gain, shift, qkv, bias, one, two, packed):
    block = swapped_rows(start[...].astype(jnp.float32), spot[1] == 1)
    hat, _ = normalised(block)
    project_block(hat, gain, shift, qkv, bias, one, two, packed)


def project_kernel(spot, mine, other, gain, shift, qkv, bias, one, two, packed):
    hat = jnp.concatenate([mine[0], other[0]], axis=0).astype(jnp.float32)
    project_block(hat, gain, shift, qkv, bias, one, two, packed)


def project(spot, tokens, pair, qkv, bias, work):
    qkv, block = qkv
    kernel = project_input_kernel if len(tokens) == 1 else project_kernel
    return in_steps(
        kernel,
        (ALL_TOKENS, ALL_TOKENS, jax.ShapeDtypeStruct((8, 3, HEAD, BLOCK), jnp.bfloat16)),
        [
            *([TOKENS] if len(tokens) == 1 else [PIECE, PIECE]),
            whole_of(pair[0]),
            whole_of(pair[1]),
            columns_of(qkv, 6 * HEAD, block)
            if qkv.ndim == 2
            else pl.BlockSpec((16, 64, 6 * HEAD), lambda b, spot: (0, 0, 0)),
            whole_of(bias),
        ],
        (TOKENS, TOKENS, pl.BlockSpec((2, 3, HEAD, BLOCK), lambda b, spot: (b, 0, 0, 0))),
        (spot, *tokens, *pair, qkv, bias),
        2 * 1024 * 384 * D,
        work,
    )


def last_of(blocks, count, place):
    if blocks.ndim == 3:
        return pl.BlockSpec((count, HEAD, BLOCK), lambda i, spot: (place(i), 0, 0))
    return pl.BlockSpec((count, None, HEAD, BLOCK), lambda i, spot: (place(i), 3, 0, 0))


def out_kernel(spot, hidden, heads, fc2, dense, mine, other):
    result = dot(hidden[...], fc2[...], ((1,), (1,)))
    block = jnp.concatenate([heads[0], heads[1]], axis=0).T
    result = result + dot(block, dense[...], ((1,), (1,)))
    mine[0] = result[:128].astype(jnp.bfloat16)
    other[0] = result[128:].astype(jnp.bfloat16)


def branch_sums(spot, hidden, heads, fc2, dense, work=(), flops=2**31):
    (fc2, fc2_block), (dense, dense_block) = (fc2, dense)
    return in_steps(
        out_kernel,
        ALL_HALVES,
        [
            pl.BlockSpec((BLOCK, hidden.shape[1]), lambda b, spot: (b, 0)),
            last_of(heads, 2, lambda b: b),
            columns_of(fc2, hidden.shape[1], fc2_block),
            columns_of(dense, 2 * HEAD, dense_block),
        ],
        HALVES,
        (spot, hidden, heads, fc2, dense),
        flops,
        work,
    )


def to_norms(grad_heads, grad_pre, qkv, fc1, gain):
    block = jnp.concatenate([grad_heads[j, k] for k in range(3) for j in range(2)], axis=0)
    result = dot(block.T, qkv[...], ((1,), (1,))) * gain[0:1]
    return result + dot(grad_pre[...], fc1[...], ((1,), (1,))) * gain[1:2]


def back_kernel(spot, grad_heads, grad_pre, qkv, fc1, gain, mine, other):
    result = to_norms(grad_heads, grad_pre, qkv, fc1, gain)
    mine[0] = result[:128].astype(jnp.bfloat16)
    other[0] = result[128:].astype(jnp.bfloat16)


def back_input_kernel(
    spot, grad_heads, grad_pre, qkv, fc1, gain, start, out_mine, out_other, change
):
    result = to_norms(grad_heads, grad_pre, qkv, fc1, gain)
    z, core = (spot[0], spot[1])
    hat, scale = normalised(swapped_rows(start[...].astype(jnp.float32), core == 1))
    change[...] = swapped_rows(norm_back(result, hat, scale), core == 1)
    for r in range(4):
        for j, out in enumerate((out_mine, out_other)):
            owner = 2 * lax.rem(z + r, 4) + lax.rem(core + j, 2)
            lanes = pl.ds(pl.multiple_of(owner * 128, 128), 128)
            out[r] = change[:, lanes].astype(jnp.bfloat16)


def norm_gradient(spot, grad_heads, grad_pre, qkv, fc1, gain, start=None, work=()):
    (qkv, qkv_block), (fc1, fc1_block) = (qkv, fc1)
    width = grad_pre.shape[1]
    in_specs = [
        pl.BlockSpec((2, 3, HEAD, BLOCK), lambda b, spot: (b, 0, 0, 0)),
        pl.BlockSpec((BLOCK, width), lambda b, spot: (b, 0)),
        columns_of(qkv, 6 * HEAD, qkv_block),
        columns_of(fc1, width, fc1_block),
        whole_of(gain),
    ]
    flops = 2 * 1024 * 896 * D
    operands = (spot, grad_heads, grad_pre, qkv, fc1, gain)
    if start is None:
        return in_steps(back_kernel, ALL_HALVES, in_specs, HALVES, operands, flops, work)
    return in_steps(
        back_input_kernel,
        (jax.ShapeDtypeStruct((4, 1024, 128), jnp.bfloat16),) * 2,
        [*in_specs, TOKENS],
        (pl.BlockSpec((4, BLOCK, 128), lambda b, spot: (0, b, 0)),) * 2,
        (*operands, start),
        flops,
        work,
        [pltpu.VMEM((BLOCK, D), jnp.float32)],
    )


def join_kernel(spot, mine, other, out):
    core = spot[1]
    out[pl.ds(pl.multiple_of(core * 128, 128), 128), :] = mine[0]
    out[pl.ds(pl.multiple_of((1 - core) * 128, 128), 128), :] = other[0]


def joined(spot, mine, other):
    return in_steps(join_kernel, ALL_TOKENS, [PIECE, PIECE], TOKENS, (spot, mine, other), 0)


def head_gradient(block, dense, upper):
    flat = dot(block, dense[...], ((1,), (0,))).T.astype(jnp.bfloat16)
    upper[0] = flat[:HEAD]
    upper[1] = flat[HEAD:]


def gradient_kernel(spot, mine, other, dense, out, upper):
    block = jnp.concatenate([mine[0], other[0]], axis=0)
    out[...] = block
    head_gradient(block, dense, upper)


def columns_kernel(spot, mine, other, dense, out, upper):
    z, core = (spot[0], spot[1])
    for r in range(4):
        for j, pieces in enumerate((mine, other)):
            owner = 2 * lax.rem(z + r, 4) + lax.rem(core + j, 2)
            piece = swapped_rows(pieces[r].astype(jnp.float32), core == 1)
            lanes = pl.ds(pl.multiple_of(owner * 128, 128), 128)
            out[:, lanes] = piece.astype(jnp.bfloat16)
    head_gradient(out[...], dense, upper)


def top_gradient(spot, pieces, dense, work=()):
    dense, block = dense
    kernel, specs = (gradient_kernel, [PIECE, PIECE])
    if pieces[0].shape[2] < D:
        kernel = columns_kernel
        specs = [pl.BlockSpec((4, BLOCK, 128), lambda b, spot: (0, b, 0))] * 2
    return in_steps(
        kernel,
        (ALL_TOKENS, jax.ShapeDtypeStruct((8, HEAD, BLOCK), jnp.bfloat16)),
        [*specs, columns_of(dense, 2 * HEAD, block)],
        (TOKENS, pl.BlockSpec((2, HEAD, BLOCK), lambda b, spot: (b, 0, 0))),
        (spot, *pieces, dense),
        2 * 1024 * 128 * D,
        work,
    )


def as_row(column):
    return jnp.broadcast_to(column, (column.shape[0], 128)).T[:1]


def norm_sums(weight, grad_weight, sums, product, shift):
    wide = weight.astype(jnp.float32)
    product[...] = as_row(jnp.sum(wide * grad_weight, axis=1, keepdims=True))
    shift[...] = as_row(jnp.sum(wide * sums, axis=1, keepdims=True))


def feed_block(normed, grad_low, grad_pre, hidden, fc1, out, product, shift, sums):
    @pl.when(pl.program_id(0) == 0)
    def _():
        total = jnp.sum(grad_pre[...].astype(jnp.float32), axis=0, keepdims=True)
        sums[...] = total

    width = grad_pre.shape[1]
    grad_fc1 = dot(normed[...], grad_pre[...], ((0,), (0,)))
    out[:, :width] = grad_fc1.astype(jnp.bfloat16)
    grad_fc2 = dot(grad_low[...], hidden[...], ((0,), (0,)))
    out[:, width : 2 * width] = grad_fc2.astype(jnp.bfloat16)
    norm_sums(fc1[...], grad_fc1, sums[...], product, shift)


def dense_block(grad_low, heads):
    total = 0.0
    for b in range(4):
        block = jnp.concatenate([heads[2 * b], heads[2 * b + 1]], axis=0)
        total = total + dot(block, grad_low[b * BLOCK : (b + 1) * BLOCK], ((1,), (0,)))
    return total.T.astype(jnp.bfloat16)


def heads_block(normed, grad_heads, qkv, out, product, shift, sums, columns):
    @pl.when(pl.program_id(0) == 0)
    def _():
        for b in range(4):
            for k in range(3):
                for j in range(2):
                    at = (2 * k + j) * HEAD
                    columns[at : at + HEAD, b * BLOCK : (b + 1) * BLOCK] = grad_heads[2 * b + j, k]
        wide = columns[...].astype(jnp.float32)
        sums[...] = as_row(jnp.sum(wide, axis=1, keepdims=True))

    grad_qkv = dot(columns[...], normed[...], ((1,), (0,))).T
    if len(out.shape) == 2:
        out[:, : 6 * HEAD] = grad_qkv.astype(jnp.bfloat16)
    else:
        out[...] = grad_qkv.astype(jnp.bfloat16).reshape(out.shape)
    norm_sums(qkv[...], grad_qkv, sums[...], product, shift)


def feed_kernel(spot, *refs):
    feed_block(*refs)


def feed_dense_kernel(
    spot, normed, grad_low, grad_pre, hidden, fc1, heads, more, out, product, shift, sums
):
    feed_block(normed, grad_low, grad_pre, hidden, fc1, out, product, shift, sums)
    at = 2 * grad_pre.shape[1]
    out[:, at : at + 2 * HEAD] = dense_block(grad_low, heads)
    out[:, at + 2 * HEAD :] = more[...]


def heads_kernel(spot, *refs):
    heads_block(*refs)


def heads_dense_kernel(
    spot, normed, grad_heads, qkv, grad_low, heads, out, product, shift, sums, columns
):
    heads_block(normed, grad_heads, qkv, out, product, shift, sums, columns)
    out[:, 6 * HEAD :] = dense_block(grad_low, heads)


FEATURES = pl.BlockSpec((1024, BLOCK), lambda i, spot: (0, i))
ROW = pl.BlockSpec((1, BLOCK), lambda i, spot: (0, i))
ROWS = jax.ShapeDtypeStruct((1, D), jnp.float32)


def weight_gradient(
    kernel, spot, operands, in_specs, width, summed_width, scratch, work, tiled=None
):
    shape, block = ((D, width), pl.BlockSpec((BLOCK, width), lambda i, spot: (i, 0)))
    if tiled is not None:
        shape = (16, tiled, width)
        block = pl.BlockSpec((4, 64, width), lambda i, spot: (i, 0, 0))
    return in_steps(
        kernel,
        (
            jax.ShapeDtypeStruct(shape, jnp.bfloat16),
            ROWS,
            ROWS,
            jax.ShapeDtypeStruct((1, summed_width), jnp.float32),
        ),
        in_specs,
        (
            block,
            ROW,
            ROW,
            pl.BlockSpec((1, summed_width), lambda i, spot: (0, 0)),
        ),
        (spot, *operands),
        0,
        work,
        scratch,
    )


def feed_gradient(spot, normed, grad_low, grad_pre, hidden, fc1, heads=None, more=None, work=()):
    width = hidden.shape[1]
    operands = [normed, grad_low, grad_pre, hidden, fc1[0]]
    in_specs = [FEATURES, FEATURES, whole_of(grad_pre), whole_of(hidden)]
    in_specs += [rows_of(fc1[0], width, fc1[1])]
    kernel, total = (feed_kernel, 2 * width)
    if heads is not None:
        operands += [heads, more]
        in_specs += [last_of(heads, 8, lambda i: 0), rows_of(more, more.shape[1], 0)]
        kernel, total = (feed_dense_kernel, total + 2 * HEAD + more.shape[1])
    return weight_gradient(kernel, spot, operands, in_specs, total, width, (), work)


def heads_gradient(
    spot, normed, grad_heads, qkv, grad_low=None, heads=None, work=(), tiled=None
):
    width = 6 * HEAD
    operands = [normed, grad_heads, qkv[0]]
    in_specs = [
        FEATURES,
        pl.BlockSpec((8, 3, HEAD, BLOCK), lambda i, spot: (0, 0, 0, 0)),
        rows_of(qkv[0], width, qkv[1]),
    ]
    kernel, total = (heads_kernel, width)
    if heads is not None:
        operands += [grad_low, heads]
        in_specs += [FEATURES, last_of(heads, 8, lambda i: 0)]
        kernel, total = (heads_dense_kernel, width + 2 * HEAD)
    scratch = [pltpu.VMEM((width, 1024), jnp.bfloat16)]
    return weight_gradient(
        kernel, spot, operands, in_specs, total, width, scratch, work, tiled
    )


def normalised(values):
    centred = values - jnp.mean(values, axis=-1, keepdims=True)
    variance = jnp.mean(centred * centred, axis=-1, keepdims=True)
    scale = lax.rsqrt(variance + epsilon)
    return centred * scale, scale


def norm_back(grad, hat, scale):
    mean = jnp.mean(grad, axis=-1, keepdims=True)
    along = jnp.mean(grad * hat, axis=-1, keepdims=True)
    return scale * (grad - mean - hat * along)


def gelu_and_slope(values):
    share = 0.5 * (1.0 + lax.erf(values * math.sqrt(0.5)))
    slope = share + values * jnp.exp(-0.5 * values * values) * (1.0 / math.sqrt(2.0 * math.pi))
    return (values * share).astype(jnp.bfloat16), slope


def low(values):
    return values.astype(jnp.bfloat16)


def shards(inputs, w_qkv, w_dense, w_fc1, w_fc2, norm_gain, biases, segment_ids, cotangent):
    tensor_rank = lax.axis_index("tensor")
    seq_rank = lax.axis_index("seq")
    along_z, core = (tensor_rank // 2, tensor_rank % 2)
    core_ref = core.astype(jnp.int32).reshape(1)
    spot = jnp.stack([along_z, core]).astype(jnp.int32)
    owners = 16
    full_len = segment_ids.shape[1]
    head_cols = w_qkv.shape[3]
    hidden_cols = w_fc1.shape[2]
    share = w_qkv.shape[1]
    gain_share = norm_gain.shape[1]
    bias_share = biases.shape[1]
    mine = jnp.arange(8) == tensor_rank

    qkv_flat = w_qkv.reshape(LAYERS, share, 3 * head_cols)
    vectors = jnp.concatenate([norm_gain.reshape(-1), biases.reshape(-1)])
    rows = 16
    vectors = jnp.pad(vectors, (0, rows * 3 * head_cols - vectors.size)).reshape(rows, -1)
    first = jnp.concatenate([qkv_flat[0], vectors], axis=0)
    first = jnp.broadcast_to(first, (owners, *first.shape))
    first = exchange(first, OWNERS)
    both_zero = lax.all_gather(
        jnp.concatenate([w_fc1[0], w_fc2[0], w_dense[0]], axis=1), OWNERS, axis=0, tiled=True
    )
    pieces = gathered(cotangent.reshape(-1, cotangent.shape[-1]))
    heads_one = lax.all_gather(
        jnp.concatenate([qkv_flat[1], w_dense[1]], axis=1), OWNERS, axis=0, tiled=True
    )
    feed_one = lax.all_gather(
        jnp.concatenate([w_fc1[1], w_fc2[1]], axis=1), OWNERS, axis=0, tiled=True
    )
    qkv_zero = first[:, :share].reshape(D, 3 * head_cols)
    vectors = first[:, share:].reshape(owners, -1)[:, : LAYERS * (gain_share + bias_share)]
    gain_vecs = vectors[:, : LAYERS * gain_share].reshape(owners, LAYERS, -1).astype(jnp.float32)
    bias_vecs = vectors[:, LAYERS * gain_share :].reshape(owners, LAYERS, -1).astype(jnp.float32)
    qkv_places = [(qkv_zero, 0), (heads_one, 0)]
    dense_places = [(both_zero, 8), (heads_one, 3)]
    fc1_places = [(both_zero, 0), (feed_one, 0)]
    fc2_places = [(both_zero, 1), (feed_one, 1)]
    fc1_weights = [both_zero[:, :hidden_cols], feed_one[:, :hidden_cols]]
    fc2_weights = [both_zero[:, hidden_cols : 2 * hidden_cols], feed_one[:, hidden_cols:]]

    pairs, qkv_biases, fc1_biases, outer_biases = ([], [], [], [])
    for l in range(LAYERS):
        vec = bias_vecs[:, l].reshape(-1)
        pairs.append((gain_vecs[:, l].reshape(2, D), vec[: 2 * D].reshape(2, D)))
        bias = vec[2 * D : 5 * D].reshape(3, 8, head_cols)
        bias = lax.dynamic_index_in_dim(bias, tensor_rank, 1, False)
        qkv_biases.append(bias.reshape(1, 3 * head_cols))
        bias = vec[6 * D : 6 * D + FF].reshape(8, hidden_cols)
        fc1_biases.append(lax.dynamic_index_in_dim(bias, tensor_rank, 0, True))
        outer_biases.append((vec[5 * D : 6 * D] + vec[6 * D + FF :]).reshape(1, D))

    segments = lax.dynamic_index_in_dim(segment_ids, seq_rank // 2, 0, False)
    earlier = jnp.zeros_like(segments)
    for doc in range(1, DOCUMENTS):
        before = jnp.sum((segments < doc).astype(jnp.int32))
        earlier = jnp.where(segments == doc, before, earlier)
    places = jnp.arange(full_len, dtype=jnp.int32) - earlier
    half_rot = ROT // 2
    inverse = 10000.0 ** (-jnp.arange(half_rot, dtype=jnp.float32) * 2.0 / ROT)
    angles = inverse[:, None] * places.astype(jnp.float32)[None, :]
    table = jnp.concatenate([jnp.cos(angles), jnp.sin(angles)], axis=0)
    starts = earlier[None, :]

    def feed_forward(normed_two, l):
        pre_act = dot(normed_two, fc1_weights[l], ((1,), (0,))) + fc1_biases[l]
        return gelu_and_slope(pre_act)

    def pre_gradient(grad_low, slope, l):
        return low(dot(grad_low, fc2_weights[l], ((1,), (0,))) * slope)

    tokens = inputs.reshape(-1, D)
    residual = own_rows(tokens, along_z, core).astype(jnp.float32)

    one_zero, two_zero, payload = project(
        spot, (tokens,), pairs[0], (first, 0), qkv_biases[0], ()
    )
    packed_zero = exchange(payload, "seq")
    prepared = (*pairs[1], qkv_biases[1], fc1_biases[1], outer_biases[0], outer_biases[1])
    prepared = (*prepared, pieces[1])
    result, *kept_zero = attend(core_ref, packed_zero, table, starts, prepared)
    heads_zero = exchange(result, "seq")
    hidden_zero, slope_zero = feed_forward(two_zero, 0)
    partial = branch_sums(spot, hidden_zero, heads_zero, fc2_places[0], dense_places[0])
    terms = z_terms(half_sum(*partial))
    residual, hat, scale, hat_low = settled(terms, residual, outer_biases[0])
    grad_top, upper_payload = top_gradient(spot, pieces, dense_places[1])
    upper = exchange(upper_payload, "seq")
    hat_pieces = gathered(hat_low, (upper,))

    one, two, payload = project(
        spot, hat_pieces, pairs[1], qkv_places[1], qkv_biases[1], ()
    )
    packed = exchange(payload, "seq")

    back = attend_both(core_ref, packed, table, starts, upper)
    grad_heads = exchange(back, "seq")
    two = after(two, back)
    hidden, slope = feed_forward(two, 1)
    grad_pre = pre_gradient(grad_top, slope, 1)
    feed_grads, feed_product, feed_shift, feed_sums = feed_gradient(
        spot, two, grad_top, grad_pre, hidden, fc1_places[1], work=(back,)
    )
    shares_feed = lax.psum_scatter(feed_grads, OWNERS, scatter_dimension=0, tiled=True)
    half = half_sum(
        *norm_gradient(
            spot,
            grad_heads,
            grad_pre,
            qkv_places[1],
            fc1_places[1],
            pairs[1][0],
            work=(feed_sums,),
        )
    )
    terms = z_terms(half)
    weight_grads, heads_product, heads_shift, heads_sums = heads_gradient(
        spot, one, grad_heads, qkv_places[1], grad_top, grad_heads, (half[0],)
    )
    partial = branch_sums(
        spot, hidden, grad_heads, fc2_places[1], dense_places[1], (half[0],), 0
    )
    own_top = own_rows(grad_top, along_z, 0)
    grad_own = through_norm(terms, own_top, hat, scale)
    sums_one = (
        (heads_product, feed_product),
        (heads_shift, feed_shift),
        heads_sums,
        feed_sums,
        jnp.sum(own_top.astype(jnp.float32), axis=0),
    )
    grad_low, upper_payload = top_gradient(
        spot, gathered(after(grad_own, heads_shift, partial[0])), dense_places[0]
    )

    upper = exchange(upper_payload, "seq")
    grad_pre = pre_gradient(grad_low, slope_zero, 0)
    weight_grads, feed_product, feed_shift, feed_sums = feed_gradient(
        spot,
        two_zero,
        grad_low,
        grad_pre,
        hidden_zero,
        fc1_places[0],
        heads_zero,
        weight_grads,
        (upper_payload,),
    )
    shares_more = lax.psum_scatter(weight_grads, OWNERS, scatter_dimension=0, tiled=True)
    back = attend_back(
        core_ref, packed_zero, table, starts, *kept_zero, upper, (feed_sums,)
    )
    grad_heads = exchange(back, "seq")
    half = half_sum(partial[0], after(partial[1], back))
    final = residual + (z_sum(half) + outer_biases[1])
    blocks = norm_gradient(
        spot,
        grad_heads,
        grad_pre,
        qkv_places[0],
        fc1_places[0],
        pairs[0][0],
        tokens,
    )
    qkv_grads, heads_product, heads_shift, heads_sums = heads_gradient(
        spot, one_zero, grad_heads, qkv_places[0], work=(blocks[0], final), tiled=share + rows
    )
    sums_zero = (
        (heads_product, feed_product),
        (heads_shift, feed_shift),
        heads_sums,
        feed_sums,
        jnp.sum(grad_own.astype(jnp.float32), axis=0),
    )

    def small_gradients(l, products, shift_grads, head_sums, pre_sums, own_sums):
        gain, shift = pairs[l]
        shift_grad = jnp.concatenate(shift_grads, axis=1)
        product = jnp.concatenate(products, axis=1)
        gain_grad = (product - shift.reshape(1, -1) * shift_grad) / gain.reshape(1, -1)
        placed_heads = jnp.where(mine[:, None], head_sums.reshape(3, 1, head_cols), 0.0)
        placed_pre = jnp.where(mine[:, None], pre_sums, 0.0)
        own_sums = own_sums.reshape(1, -1)
        bias_grad = jnp.concatenate(
            [
                shift_grad,
                placed_heads.reshape(1, -1),
                own_sums,
                placed_pre.reshape(1, -1),
                own_sums,
            ],
            axis=1,
        )
        return [bias_grad.reshape(owners, bias_share), gain_grad.reshape(owners, gain_share)]

    small = jnp.concatenate(
        [*small_gradients(0, *sums_zero), *small_gradients(1, *sums_one)], axis=1
    )
    small = jnp.pad(small, ((0, 0), (0, rows * 3 * head_cols - small.shape[1])))
    small = low(small).reshape(owners, rows, -1)
    tiles = lax.dynamic_update_slice(qkv_grads, small, (0, share, 0))
    out_pieces = gathered(low(final), late=(tiles,))
    block_out = joined(spot, *out_pieces).reshape(inputs.shape)
    half = half_sum(*blocks)
    change = z_sum((half[0], after(half[1], block_out), *half[2:]))
    columns = lax.dynamic_slice_in_dim(grad_low, tensor_rank * (D // 8), D // 8, 1)
    grad_inputs = swapped(columns, core).astype(jnp.float32) + change
    grad_inputs = grad_inputs.reshape(cotangent.shape)
    tiles = jnp.sum(exchange(tiles, OWNERS).astype(jnp.float32), axis=0)
    small = tiles[share:].reshape(-1)[: LAYERS * (gain_share + bias_share)]
    small = jnp.sum(sent_to_all(small, "tensor"), axis=0).reshape(LAYERS, -1)
    feed = shares_feed.astype(jnp.float32)
    more = shares_more.astype(jnp.float32)
    grad_qkv = jnp.stack([tiles[:share], more[:, 1152:1536]])
    grad_dense = jnp.stack([more[:, 1024:1152], more[:, 1536:]])
    grad_fc1 = jnp.stack([more[:, :hidden_cols], feed[:, :hidden_cols]])
    grad_fc2 = jnp.stack([more[:, hidden_cols : 2 * hidden_cols], feed[:, hidden_cols:]])
    return (
        block_out,
        grad_inputs,
        grad_qkv.reshape(w_qkv.shape),
        grad_dense,
        grad_fc1,
        grad_fc2,
        small[:, bias_share:],
        small[:, :bias_share],
    )


def solution(mesh):
    in_specs = (
        P("dp", "seq", None),
        P(None, ("dp", "seq"), None, "tensor"),
        P(None, ("dp", "seq"), "tensor"),
        P(None, ("dp", "seq"), "tensor"),
        P(None, ("dp", "seq"), "tensor"),
        P(None, ("dp", "seq")),
        P(None, ("dp", "seq")),
        P("dp", None),
        P("dp", "seq", "tensor"),
    )
    out_specs = (
        P("dp", "seq", None),
        P("dp", "seq", "tensor"),
        P(None, ("dp", "seq"), None, "tensor"),
        P(None, ("dp", "seq"), "tensor"),
        P(None, ("dp", "seq"), "tensor"),
        P(None, ("dp", "seq"), "tensor"),
        P(None, ("dp", "seq")),
        P(None, ("dp", "seq")),
    )
    return jax.shard_map(shards, mesh=mesh, in_specs=in_specs, out_specs=out_specs, check_vma=False)
```

```python
import math

import jax
import jax.numpy as jnp
from jax import lax
from jax.experimental import pallas as pl
from jax.experimental.pallas import tpu as pltpu
from jax.sharding import PartitionSpec as P

D = 1024
FF = 4096
HEAD = 64
ROT = 16
LAYERS = 2
DOCUMENTS = 5
BLOCK = 256
VMEM_BYTES = 48 * 1024 * 1024
OWNERS = ("dp", "seq")
ACROSS = [(2 * z + core, 2 * z + 1 - core) for z in range(4) for core in range(2)]

epsilon = 1e-05


def dot(a, b, dims):
    return lax.dot_general(a, b, (dims, ((), ())), preferred_element_type=jnp.float32)


def turned(block, cosine, sines):
    half = ROT // 2
    low, high = (block[:half], block[half:ROT])
    return jnp.concatenate(
        [low * cosine - high * sines, high * cosine + low * sines, block[ROT:]], axis=0
    )


def in_order(block, flip):
    half = block.shape[-1] // 2
    other = jnp.concatenate([block[..., half:], block[..., :half]], axis=-1)
    return jnp.where(flip, other, block)


def prepare(packed, table, keys, keys_t, values, values_t, blocks, flip):
    queries = []
    half = ROT // 2
    for i in range(blocks):
        cols = slice(i * BLOCK, (i + 1) * BLOCK)
        cosine, sines = (table[:half, cols], table[half:, cols])
        query = in_order(packed[i, 0].astype(jnp.float32), flip)
        query = turned(query, cosine, sines).astype(jnp.bfloat16)
        queries.append(query * jnp.bfloat16(HEAD**-0.5))
        key = in_order(packed[i, 1].astype(jnp.float32), flip)
        key = turned(key, cosine, sines).astype(jnp.bfloat16)
        keys[cols, :] = key.T
        value = in_order(packed[i, 2].astype(jnp.float32), flip).astype(jnp.bfloat16)
        if keys_t is not None:
            keys_t[:, cols] = key
        if values is not None:
            values[cols, :] = value.T
        if values_t is not None:
            values_t[:, cols] = value
    return queries


def masked(scores, i, starts):
    row = lax.broadcasted_iota(jnp.int32, scores.shape, 0)
    in_document = jnp.where(row >= starts, scores, -1e30)
    last = in_document[i * BLOCK :]
    row = lax.broadcasted_iota(jnp.int32, last.shape, 0)
    col = lax.broadcasted_iota(jnp.int32, last.shape, 1)
    last = jnp.where(row <= col, last, -1e30)
    return jnp.concatenate([in_document[: i * BLOCK], last], axis=0) if i > 0 else last


def attend_kernel(core, packed, table, starts, out, wide, log_total, keys, values_t):
    blocks = packed.shape[0]
    flip = core[0] == 1
    queries = prepare(packed, table, keys, None, None, values_t, blocks, flip)
    for i in range(blocks):
        length = (i + 1) * BLOCK
        scores = dot(keys[:length], queries[i], ((1,), (0,)))
        scores = masked(scores, i, starts[:, i * BLOCK : length])
        largest = jnp.max(scores, axis=0, keepdims=True)
        exponent = jnp.exp(scores - largest)
        total = jnp.sum(exponent, axis=0, keepdims=True)
        result = dot(values_t[:, :length], exponent.astype(jnp.bfloat16), ((1,), (0,)))
        result = result / total
        wide[i] = result
        out[i] = in_order(result, flip).astype(jnp.bfloat16)
        log_total[i] = largest + jnp.log(total)


SCALAR = pl.BlockSpec(memory_space=pltpu.SMEM)
WHOLE = pl.BlockSpec(memory_space=pltpu.VMEM)


def attend(core, packed, table, starts, work=()):
    blocks = packed.shape[0]
    full = blocks * BLOCK
    return pl.pallas_call(
        skipping(attend_kernel, 4, len(work)),
        out_shape=(
            jax.ShapeDtypeStruct((blocks, HEAD, BLOCK), jnp.bfloat16),
            jax.ShapeDtypeStruct((blocks, HEAD, BLOCK), jnp.float32),
            jax.ShapeDtypeStruct((blocks, 1, BLOCK), jnp.float32),
        ),
        in_specs=[SCALAR] + [WHOLE] * 3 + [UNREAD] * len(work),
        scratch_shapes=[
            pltpu.VMEM((full, HEAD), jnp.bfloat16),
            pltpu.VMEM((HEAD, full), jnp.bfloat16),
        ],
        compiler_params=pltpu.CompilerParams(vmem_limit_bytes=VMEM_BYTES),
        cost_estimate=pl.CostEstimate(
            flops=4 * full * full * HEAD, bytes_accessed=2**21, transcendentals=full * full // 2
        ),
    )(core, packed, table, starts, *work)


def attend_back_kernel(
    core,
    packed,
    table,
    starts,
    wide,
    log_total,
    upper,
    out,
    keys,
    keys_t,
    values,
    grad_k,
    grad_v,
):
    blocks = packed.shape[0]
    half = ROT // 2
    flip = core[0] == 1
    queries = prepare(packed, table, keys, keys_t, values, None, blocks, flip)
    for i in range(blocks):
        length = (i + 1) * BLOCK
        cols = slice(i * BLOCK, length)
        scores = dot(keys[:length], queries[i], ((1,), (0,)))
        probs = jnp.exp(masked(scores, i, starts[:, cols]) - log_total[i])
        above = in_order(upper[i].astype(jnp.float32), flip).astype(jnp.bfloat16)
        grad_probs = dot(values[:length], above, ((1,), (0,)))
        row_dot = jnp.sum(above.astype(jnp.float32) * wide[i], axis=0, keepdims=True)
        grad_scores = (probs * (grad_probs - row_dot)).astype(jnp.bfloat16)
        grad_q = dot(keys_t[:, :length], grad_scores, ((1,), (0,))) * HEAD**-0.5
        cosine, sines = (table[:half, cols], table[half:, cols])
        out[i, 0] = in_order(turned(grad_q, cosine, -sines), flip).astype(jnp.bfloat16)
        probs_low = probs.astype(jnp.bfloat16)
        part_v = dot(above, probs_low, ((1,), (1,)))
        part_k = dot(queries[i], grad_scores, ((1,), (1,)))
        if i > 0:
            grad_v[:, : i * BLOCK] += part_v[:, : i * BLOCK]
            grad_k[:, : i * BLOCK] += part_k[:, : i * BLOCK]
        grad_v[:, cols] = part_v[:, cols]
        grad_k[:, cols] = part_k[:, cols]
    for i in range(blocks):
        cols = slice(i * BLOCK, (i + 1) * BLOCK)
        cosine, sines = (table[:half, cols], table[half:, cols])
        out[i, 1] = in_order(turned(grad_k[:, cols], cosine, -sines), flip).astype(jnp.bfloat16)
        out[i, 2] = in_order(grad_v[:, cols], flip).astype(jnp.bfloat16)


def attend_both_kernel(
    core, packed, table, starts, upper, out, keys, keys_t, values, values_t, grad_k, grad_v
):
    blocks = packed.shape[0]
    half = ROT // 2
    flip = core[0] == 1
    queries = prepare(packed, table, keys, keys_t, values, values_t, blocks, flip)
    for i in range(blocks):
        length = (i + 1) * BLOCK
        cols = slice(i * BLOCK, length)
        scores = dot(keys[:length], queries[i], ((1,), (0,)))
        scores = masked(scores, i, starts[:, cols])
        exponent = jnp.exp(scores - jnp.max(scores, axis=0, keepdims=True))
        share = 1.0 / jnp.sum(exponent, axis=0, keepdims=True)
        probs = exponent * share
        probs_low = probs.astype(jnp.bfloat16)
        result = dot(values_t[:, :length], probs_low, ((1,), (0,)))
        out[i, 3] = in_order(result, flip).astype(jnp.bfloat16)
        above = in_order(upper[i].astype(jnp.float32), flip)
        row_dot = jnp.sum(above * result, axis=0, keepdims=True)
        above = above.astype(jnp.bfloat16)
        grad_probs = dot(values[:length], above, ((1,), (0,)))
        grad_scores = (probs * (grad_probs - row_dot)).astype(jnp.bfloat16)
        grad_q = dot(keys_t[:, :length], grad_scores, ((1,), (0,))) * HEAD**-0.5
        cosine, sines = (table[:half, cols], table[half:, cols])
        out[i, 0] = in_order(turned(grad_q, cosine, -sines), flip).astype(jnp.bfloat16)
        part_v = dot(above, probs_low, ((1,), (1,)))
        part_k = dot(queries[i], grad_scores, ((1,), (1,)))
        if i > 0:
            grad_v[:, : i * BLOCK] += part_v[:, : i * BLOCK]
            grad_k[:, : i * BLOCK] += part_k[:, : i * BLOCK]
        grad_v[:, cols] = part_v[:, cols]
        grad_k[:, cols] = part_k[:, cols]
    for i in range(blocks):
        cols = slice(i * BLOCK, (i + 1) * BLOCK)
        cosine, sines = (table[:half, cols], table[half:, cols])
        out[i, 1] = in_order(turned(grad_k[:, cols], cosine, -sines), flip).astype(jnp.bfloat16)
        out[i, 2] = in_order(grad_v[:, cols], flip).astype(jnp.bfloat16)


def attend_both(core, packed, table, starts, upper):
    blocks = packed.shape[0]
    full = blocks * BLOCK
    return pl.pallas_call(
        attend_both_kernel,
        out_shape=jax.ShapeDtypeStruct((blocks, 4, HEAD, BLOCK), jnp.bfloat16),
        in_specs=[SCALAR] + [WHOLE] * 4,
        scratch_shapes=[
            pltpu.VMEM((full, HEAD), jnp.bfloat16),
            pltpu.VMEM((HEAD, full), jnp.bfloat16),
            pltpu.VMEM((full, HEAD), jnp.bfloat16),
            pltpu.VMEM((HEAD, full), jnp.bfloat16),
            pltpu.VMEM((HEAD, full), jnp.float32),
            pltpu.VMEM((HEAD, full), jnp.float32),
        ],
        compiler_params=pltpu.CompilerParams(vmem_limit_bytes=VMEM_BYTES),
        cost_estimate=pl.CostEstimate(
            flops=12 * full * full * HEAD, bytes_accessed=2**22, transcendentals=full * full // 2
        ),
    )(core, packed, table, starts, upper)


def attend_back(core, packed, table, starts, wide, log_total, upper, work=()):
    blocks = packed.shape[0]
    full = blocks * BLOCK
    return pl.pallas_call(
        skipping(attend_back_kernel, 7, len(work)),
        out_shape=jax.ShapeDtypeStruct((blocks, 3, HEAD, BLOCK), jnp.bfloat16),
        in_specs=[SCALAR] + [WHOLE] * 6 + [UNREAD] * len(work),
        scratch_shapes=[
            pltpu.VMEM((full, HEAD), jnp.bfloat16),
            pltpu.VMEM((HEAD, full), jnp.bfloat16),
            pltpu.VMEM((full, HEAD), jnp.bfloat16),
            pltpu.VMEM((HEAD, full), jnp.float32),
            pltpu.VMEM((HEAD, full), jnp.float32),
        ],
        compiler_params=pltpu.CompilerParams(vmem_limit_bytes=VMEM_BYTES),
        cost_estimate=pl.CostEstimate(
            flops=10 * full * full * HEAD, bytes_accessed=2**22, transcendentals=full * full // 2
        ),
    )(core, packed, table, starts, wide, log_total, upper, *work)


def exchange(blocks, axis, groups=None):
    return lax.all_to_all(blocks, axis, 0, 0, tiled=True, axis_index_groups=groups)


def sent_to_all(shard, axis, groups=None):
    size = lax.axis_size(axis) if groups is None else len(groups[0])
    return exchange(jnp.broadcast_to(shard, (size, *shard.shape)), axis, groups)


UNREAD = pl.BlockSpec(memory_space=pl.ANY)


def skipping(kernel, first, count):
    return lambda *refs: kernel(*refs[:first], *refs[first + count :])


def after(value, *work):
    return pl.pallas_call(
        lambda *refs: None,
        out_shape=jax.ShapeDtypeStruct(value.shape, value.dtype),
        in_specs=[UNREAD] * (1 + len(work)),
        out_specs=UNREAD,
        input_output_aliases={0: 0},
        cost_estimate=pl.CostEstimate(flops=0, bytes_accessed=0, transcendentals=0),
    )(value, *work)


def along(distance):
    return [
        (2 * z + core, 2 * ((z + distance) % 4) + core) for z in range(4) for core in range(2)
    ]


def gathered(own, work=(), late=()):
    pieces = [lax.ppermute(own, "tensor", along(-r)) for r in range(1, 4)]
    if late:
        pieces = [after(piece, *late) for piece in pieces]
    mine = jnp.stack([own, *pieces])
    if work:
        mine = after(mine, *work)
    return mine, lax.ppermute(mine, "tensor", ACROSS)


def half_kernel(mine, got, *outs):
    for r, out in enumerate(outs):
        out[...] = (mine[r].astype(jnp.float32) + got[r].astype(jnp.float32)).astype(jnp.bfloat16)


def half_sum(mine, other):
    got = lax.ppermute(other, "tensor", ACROSS)
    return pl.pallas_call(
        half_kernel,
        out_shape=(jax.ShapeDtypeStruct(mine.shape[1:], jnp.bfloat16),) * 4,
        in_specs=[WHOLE] * 2,
        compiler_params=pltpu.CompilerParams(vmem_limit_bytes=VMEM_BYTES),
        cost_estimate=pl.CostEstimate(flops=2**20, bytes_accessed=2**22, transcendentals=0),
    )(mine, got)


def z_terms(half):
    return [half[0]] + [lax.ppermute(half[r], "tensor", along(r)) for r in range(1, 4)]


def z_sum(half):
    total = 0.0
    for term in z_terms(half):
        total = total + term.astype(jnp.float32)
    return total


def settle_kernel(one, two, three, four, residual, bias, out, hat, scale, hat_low):
    total = one[...].astype(jnp.float32) + two[...].astype(jnp.float32)
    total = total + three[...].astype(jnp.float32) + four[...].astype(jnp.float32)
    total = residual[...] + (total + bias[...])
    out[...] = total
    hat[...], scale[...] = normalised(total)
    hat_low[...] = hat[...].astype(jnp.bfloat16)


def settled(terms, residual, bias):
    wide = jax.ShapeDtypeStruct(residual.shape, jnp.float32)
    return pl.pallas_call(
        settle_kernel,
        out_shape=(
            wide,
            wide,
            jax.ShapeDtypeStruct((residual.shape[0], 1), jnp.float32),
            jax.ShapeDtypeStruct(residual.shape, jnp.bfloat16),
        ),
        in_specs=[WHOLE] * 6,
        compiler_params=pltpu.CompilerParams(vmem_limit_bytes=VMEM_BYTES),
        cost_estimate=pl.CostEstimate(flops=2**21, bytes_accessed=2**22, transcendentals=0),
    )(*terms, residual, bias)


def through_norm_kernel(one, two, three, four, grad, hat, scale, out):
    total = one[...].astype(jnp.float32) + two[...].astype(jnp.float32)
    total = total + three[...].astype(jnp.float32) + four[...].astype(jnp.float32)
    total = grad[...].astype(jnp.float32) + norm_back(total, hat[...], scale[...])
    out[...] = total.astype(jnp.bfloat16)


def through_norm(terms, grad, hat, scale):
    return pl.pallas_call(
        through_norm_kernel,
        out_shape=jax.ShapeDtypeStruct(grad.shape, jnp.bfloat16),
        in_specs=[WHOLE] * 7,
        compiler_params=pltpu.CompilerParams(vmem_limit_bytes=VMEM_BYTES),
        cost_estimate=pl.CostEstimate(flops=2**21, bytes_accessed=2**22, transcendentals=0),
    )(*terms, grad, hat, scale)


def swapped(tokens, core):
    halves = tokens.reshape(4, 2, 128, tokens.shape[-1])
    return jnp.where(core == 0, halves, halves[:, ::-1]).reshape(tokens.shape)


def swapped_rows(block, flip):
    half = block.shape[0] // 2
    other = jnp.concatenate([block[half:], block[:half]], axis=0)
    return jnp.where(flip, other, block)


def own_rows(tokens, along_z, half):
    blocks = tokens.reshape(4, 2, 128, tokens.shape[-1])
    return lax.dynamic_index_in_dim(
        lax.dynamic_index_in_dim(blocks, along_z, 0, False), half, 0, False
    )


def in_steps(
    kernel, out_shape, in_specs, out_specs, operands, flops, work=(), scratch=(), alias=None
):
    return pl.pallas_call(
        skipping(kernel, len(operands), len(work)),
        out_shape=out_shape,
        grid_spec=pltpu.PrefetchScalarGridSpec(
            num_scalar_prefetch=1,
            grid=(4,),
            in_specs=[*in_specs, *([UNREAD] * len(work))],
            out_specs=out_specs,
            scratch_shapes=scratch,
        ),
        input_output_aliases={} if alias is None else alias,
        compiler_params=pltpu.CompilerParams(vmem_limit_bytes=VMEM_BYTES),
        cost_estimate=pl.CostEstimate(
            flops=flops, bytes_accessed=2**23 if flops else 2**10, transcendentals=0
        ),
    )(*operands, *work)


def distance_of(b, spot):
    return lax.rem(b - spot[0] + 4, 4)


def columns_of(weight, width, block):
    return pl.BlockSpec((weight.shape[0], width), lambda b, spot: (0, block))


def rows_of(weight, width, block):
    return pl.BlockSpec((BLOCK, width), lambda i, spot: (i, block))


def whole_of(array):
    return pl.BlockSpec(array.shape, lambda i, spot: (0,) * array.ndim)


PIECE = pl.BlockSpec((1, 128, D), lambda b, spot: (distance_of(b, spot), 0, 0))
TOKENS = pl.BlockSpec((BLOCK, D), lambda b, spot: (b, 0))
ALL_TOKENS = jax.ShapeDtypeStruct((1024, D), jnp.bfloat16)
HALVES = (PIECE, PIECE)
ALL_HALVES = (jax.ShapeDtypeStruct((4, 128, D), jnp.bfloat16),) * 2


def project_block(hat, gain, shift, qkv, bias, one, two, packed):
    first = (hat * gain[0:1] + shift[0:1]).astype(jnp.bfloat16)
    one[...] = first
    two[...] = (hat * gain[1:2] + shift[1:2]).astype(jnp.bfloat16)
    weight = qkv[...].reshape(D, 6 * HEAD)
    flat = (dot(first, weight, ((1,), (0,))) + bias[...]).T.astype(jnp.bfloat16)
    for k in range(3):
        for j in range(2):
            at = (2 * k + j) * HEAD
            packed[j, k] = flat[at : at + HEAD]


def project_input_kernel(spot, start, gain, shift, qkv, bias, one, two, packed):
    block = swapped_rows(start[...].astype(jnp.float32), spot[1] == 1)
    hat, _ = normalised(block)
    project_block(hat, gain, shift, qkv, bias, one, two, packed)


def project_kernel(spot, mine, other, gain, shift, qkv, bias, one, two, packed):
    hat = jnp.concatenate([mine[0], other[0]], axis=0).astype(jnp.float32)
    project_block(hat, gain, shift, qkv, bias, one, two, packed)


def project(spot, tokens, pair, qkv, bias, work):
    qkv, block = qkv
    kernel = project_input_kernel if len(tokens) == 1 else project_kernel
    return in_steps(
        kernel,
        (ALL_TOKENS, ALL_TOKENS, jax.ShapeDtypeStruct((8, 3, HEAD, BLOCK), jnp.bfloat16)),
        [
            *([TOKENS] if len(tokens) == 1 else [PIECE, PIECE]),
            whole_of(pair[0]),
            whole_of(pair[1]),
            columns_of(qkv, 6 * HEAD, block)
            if qkv.ndim == 2
            else pl.BlockSpec((16, 64, 6 * HEAD), lambda b, spot: (0, 0, 0)),
            whole_of(bias),
        ],
        (TOKENS, TOKENS, pl.BlockSpec((2, 3, HEAD, BLOCK), lambda b, spot: (b, 0, 0, 0))),
        (spot, *tokens, *pair, qkv, bias),
        2 * 1024 * 384 * D,
        work,
    )


def last_of(blocks, count, place):
    if blocks.ndim == 3:
        return pl.BlockSpec((count, HEAD, BLOCK), lambda i, spot: (place(i), 0, 0))
    return pl.BlockSpec((count, None, HEAD, BLOCK), lambda i, spot: (place(i), 3, 0, 0))


def out_kernel(spot, hidden, heads, fc2, dense, mine, other):
    result = dot(hidden[...], fc2[...], ((1,), (1,)))
    block = jnp.concatenate([heads[0], heads[1]], axis=0).T
    result = result + dot(block, dense[...], ((1,), (1,)))
    mine[0] = result[:128].astype(jnp.bfloat16)
    other[0] = result[128:].astype(jnp.bfloat16)


def branch_sums(spot, hidden, heads, fc2, dense, work=(), flops=2**31):
    (fc2, fc2_block), (dense, dense_block) = (fc2, dense)
    return in_steps(
        out_kernel,
        ALL_HALVES,
        [
            pl.BlockSpec((BLOCK, hidden.shape[1]), lambda b, spot: (b, 0)),
            last_of(heads, 2, lambda b: b),
            columns_of(fc2, hidden.shape[1], fc2_block),
            columns_of(dense, 2 * HEAD, dense_block),
        ],
        HALVES,
        (spot, hidden, heads, fc2, dense),
        flops,
        work,
    )


def to_norms(grad_heads, grad_pre, qkv, fc1, gain):
    block = jnp.concatenate([grad_heads[j, k] for k in range(3) for j in range(2)], axis=0)
    result = dot(block.T, qkv[...], ((1,), (1,))) * gain[0:1]
    return result + dot(grad_pre[...], fc1[...], ((1,), (1,))) * gain[1:2]


def back_kernel(spot, grad_heads, grad_pre, qkv, fc1, gain, mine, other):
    result = to_norms(grad_heads, grad_pre, qkv, fc1, gain)
    mine[0] = result[:128].astype(jnp.bfloat16)
    other[0] = result[128:].astype(jnp.bfloat16)


def back_input_kernel(
    spot, grad_heads, grad_pre, qkv, fc1, gain, start, out_mine, out_other, change
):
    result = to_norms(grad_heads, grad_pre, qkv, fc1, gain)
    z, core = (spot[0], spot[1])
    hat, scale = normalised(swapped_rows(start[...].astype(jnp.float32), core == 1))
    change[...] = swapped_rows(norm_back(result, hat, scale), core == 1)
    for r in range(4):
        for j, out in enumerate((out_mine, out_other)):
            owner = 2 * lax.rem(z + r, 4) + lax.rem(core + j, 2)
            lanes = pl.ds(pl.multiple_of(owner * 128, 128), 128)
            out[r] = change[:, lanes].astype(jnp.bfloat16)


def norm_gradient(spot, grad_heads, grad_pre, qkv, fc1, gain, start=None, work=()):
    (qkv, qkv_block), (fc1, fc1_block) = (qkv, fc1)
    width = grad_pre.shape[1]
    in_specs = [
        pl.BlockSpec((2, 3, HEAD, BLOCK), lambda b, spot: (b, 0, 0, 0)),
        pl.BlockSpec((BLOCK, width), lambda b, spot: (b, 0)),
        columns_of(qkv, 6 * HEAD, qkv_block),
        columns_of(fc1, width, fc1_block),
        whole_of(gain),
    ]
    flops = 2 * 1024 * 896 * D
    operands = (spot, grad_heads, grad_pre, qkv, fc1, gain)
    if start is None:
        return in_steps(back_kernel, ALL_HALVES, in_specs, HALVES, operands, flops, work)
    return in_steps(
        back_input_kernel,
        (jax.ShapeDtypeStruct((4, 1024, 128), jnp.bfloat16),) * 2,
        [*in_specs, TOKENS],
        (pl.BlockSpec((4, BLOCK, 128), lambda b, spot: (0, b, 0)),) * 2,
        (*operands, start),
        flops,
        work,
        [pltpu.VMEM((BLOCK, D), jnp.float32)],
    )


def join_kernel(spot, mine, other, out):
    core = spot[1]
    out[pl.ds(pl.multiple_of(core * 128, 128), 128), :] = mine[0]
    out[pl.ds(pl.multiple_of((1 - core) * 128, 128), 128), :] = other[0]


def joined(spot, mine, other):
    return in_steps(join_kernel, ALL_TOKENS, [PIECE, PIECE], TOKENS, (spot, mine, other), 0)


def head_gradient(block, dense, upper):
    flat = dot(block, dense[...], ((1,), (0,))).T.astype(jnp.bfloat16)
    upper[0] = flat[:HEAD]
    upper[1] = flat[HEAD:]


def gradient_kernel(spot, mine, other, dense, out, upper):
    block = jnp.concatenate([mine[0], other[0]], axis=0)
    out[...] = block
    head_gradient(block, dense, upper)


def columns_kernel(spot, mine, other, dense, out, upper):
    z, core = (spot[0], spot[1])
    for r in range(4):
        for j, pieces in enumerate((mine, other)):
            owner = 2 * lax.rem(z + r, 4) + lax.rem(core + j, 2)
            piece = swapped_rows(pieces[r].astype(jnp.float32), core == 1)
            lanes = pl.ds(pl.multiple_of(owner * 128, 128), 128)
            out[:, lanes] = piece.astype(jnp.bfloat16)
    head_gradient(out[...], dense, upper)


def top_gradient(spot, pieces, dense, work=()):
    dense, block = dense
    kernel, specs = (gradient_kernel, [PIECE, PIECE])
    if pieces[0].shape[2] < D:
        kernel = columns_kernel
        specs = [pl.BlockSpec((4, BLOCK, 128), lambda b, spot: (0, b, 0))] * 2
    return in_steps(
        kernel,
        (ALL_TOKENS, jax.ShapeDtypeStruct((8, HEAD, BLOCK), jnp.bfloat16)),
        [*specs, columns_of(dense, 2 * HEAD, block)],
        (TOKENS, pl.BlockSpec((2, HEAD, BLOCK), lambda b, spot: (b, 0, 0))),
        (spot, *pieces, dense),
        2 * 1024 * 128 * D,
        work,
    )


def as_row(column):
    return jnp.broadcast_to(column, (column.shape[0], 128)).T[:1]


def norm_sums(weight, grad_weight, sums, product, shift):
    wide = weight.astype(jnp.float32)
    product[...] = as_row(jnp.sum(wide * grad_weight, axis=1, keepdims=True))
    shift[...] = as_row(jnp.sum(wide * sums, axis=1, keepdims=True))


def feed_block(normed, grad_low, grad_pre, hidden, fc1, out, product, shift, sums):
    @pl.when(pl.program_id(0) == 0)
    def _():
        total = jnp.sum(grad_pre[...].astype(jnp.float32), axis=0, keepdims=True)
        sums[...] = total

    width = grad_pre.shape[1]
    grad_fc1 = dot(normed[...], grad_pre[...], ((0,), (0,)))
    out[:, :width] = grad_fc1.astype(jnp.bfloat16)
    grad_fc2 = dot(grad_low[...], hidden[...], ((0,), (0,)))
    out[:, width : 2 * width] = grad_fc2.astype(jnp.bfloat16)
    norm_sums(fc1[...], grad_fc1, sums[...], product, shift)


def dense_block(grad_low, heads):
    total = 0.0
    for b in range(4):
        block = jnp.concatenate([heads[2 * b], heads[2 * b + 1]], axis=0)
        total = total + dot(block, grad_low[b * BLOCK : (b + 1) * BLOCK], ((1,), (0,)))
    return total.T.astype(jnp.bfloat16)


def heads_block(normed, grad_heads, qkv, out, product, shift, sums, columns):
    @pl.when(pl.program_id(0) == 0)
    def _():
        for b in range(4):
            for k in range(3):
                for j in range(2):
                    at = (2 * k + j) * HEAD
                    columns[at : at + HEAD, b * BLOCK : (b + 1) * BLOCK] = grad_heads[2 * b + j, k]
        wide = columns[...].astype(jnp.float32)
        sums[...] = as_row(jnp.sum(wide, axis=1, keepdims=True))

    grad_qkv = dot(columns[...], normed[...], ((1,), (0,))).T
    if len(out.shape) == 2:
        out[:, : 6 * HEAD] = grad_qkv.astype(jnp.bfloat16)
    else:
        out[...] = grad_qkv.astype(jnp.bfloat16).reshape(out.shape)
    norm_sums(qkv[...], grad_qkv, sums[...], product, shift)


def feed_kernel(spot, *refs):
    feed_block(*refs)


def feed_dense_kernel(
    spot, normed, grad_low, grad_pre, hidden, fc1, heads, more, out, product, shift, sums
):
    feed_block(normed, grad_low, grad_pre, hidden, fc1, out, product, shift, sums)
    at = 2 * grad_pre.shape[1]
    out[:, at : at + 2 * HEAD] = dense_block(grad_low, heads)
    out[:, at + 2 * HEAD :] = more[...]


def heads_kernel(spot, *refs):
    heads_block(*refs)


def heads_dense_kernel(
    spot, normed, grad_heads, qkv, grad_low, heads, out, product, shift, sums, columns
):
    heads_block(normed, grad_heads, qkv, out, product, shift, sums, columns)
    out[:, 6 * HEAD :] = dense_block(grad_low, heads)


FEATURES = pl.BlockSpec((1024, BLOCK), lambda i, spot: (0, i))
ROW = pl.BlockSpec((1, BLOCK), lambda i, spot: (0, i))
ROWS = jax.ShapeDtypeStruct((1, D), jnp.float32)


def weight_gradient(
    kernel, spot, operands, in_specs, width, summed_width, scratch, work, tiled=None
):
    shape, block = ((D, width), pl.BlockSpec((BLOCK, width), lambda i, spot: (i, 0)))
    if tiled is not None:
        shape = (16, tiled, width)
        block = pl.BlockSpec((4, 64, width), lambda i, spot: (i, 0, 0))
    return in_steps(
        kernel,
        (
            jax.ShapeDtypeStruct(shape, jnp.bfloat16),
            ROWS,
            ROWS,
            jax.ShapeDtypeStruct((1, summed_width), jnp.float32),
        ),
        in_specs,
        (
            block,
            ROW,
            ROW,
            pl.BlockSpec((1, summed_width), lambda i, spot: (0, 0)),
        ),
        (spot, *operands),
        0,
        work,
        scratch,
    )


def feed_gradient(spot, normed, grad_low, grad_pre, hidden, fc1, heads=None, more=None, work=()):
    width = hidden.shape[1]
    operands = [normed, grad_low, grad_pre, hidden, fc1[0]]
    in_specs = [FEATURES, FEATURES, whole_of(grad_pre), whole_of(hidden)]
    in_specs += [rows_of(fc1[0], width, fc1[1])]
    kernel, total = (feed_kernel, 2 * width)
    if heads is not None:
        operands += [heads, more]
        in_specs += [last_of(heads, 8, lambda i: 0), rows_of(more, more.shape[1], 0)]
        kernel, total = (feed_dense_kernel, total + 2 * HEAD + more.shape[1])
    return weight_gradient(kernel, spot, operands, in_specs, total, width, (), work)


def heads_gradient(
    spot, normed, grad_heads, qkv, grad_low=None, heads=None, work=(), tiled=None
):
    width = 6 * HEAD
    operands = [normed, grad_heads, qkv[0]]
    in_specs = [
        FEATURES,
        pl.BlockSpec((8, 3, HEAD, BLOCK), lambda i, spot: (0, 0, 0, 0)),
        rows_of(qkv[0], width, qkv[1]),
    ]
    kernel, total = (heads_kernel, width)
    if heads is not None:
        operands += [grad_low, heads]
        in_specs += [FEATURES, last_of(heads, 8, lambda i: 0)]
        kernel, total = (heads_dense_kernel, width + 2 * HEAD)
    scratch = [pltpu.VMEM((width, 1024), jnp.bfloat16)]
    return weight_gradient(
        kernel, spot, operands, in_specs, total, width, scratch, work, tiled
    )


def normalised(values):
    centred = values - jnp.mean(values, axis=-1, keepdims=True)
    variance = jnp.mean(centred * centred, axis=-1, keepdims=True)
    scale = lax.rsqrt(variance + epsilon)
    return centred * scale, scale


def norm_back(grad, hat, scale):
    mean = jnp.mean(grad, axis=-1, keepdims=True)
    along = jnp.mean(grad * hat, axis=-1, keepdims=True)
    return scale * (grad - mean - hat * along)


def gelu_and_slope(values):
    share = 0.5 * (1.0 + lax.erf(values * math.sqrt(0.5)))
    slope = share + values * jnp.exp(-0.5 * values * values) * (1.0 / math.sqrt(2.0 * math.pi))
    return (values * share).astype(jnp.bfloat16), slope


def low(values):
    return values.astype(jnp.bfloat16)


def shards(inputs, w_qkv, w_dense, w_fc1, w_fc2, norm_gain, biases, segment_ids, cotangent):
    tensor_rank = lax.axis_index("tensor")
    seq_rank = lax.axis_index("seq")
    along_z, core = (tensor_rank // 2, tensor_rank % 2)
    core_ref = core.astype(jnp.int32).reshape(1)
    spot = jnp.stack([along_z, core]).astype(jnp.int32)
    owners = 16
    full_len = segment_ids.shape[1]
    head_cols = w_qkv.shape[3]
    hidden_cols = w_fc1.shape[2]
    share = w_qkv.shape[1]
    gain_share = norm_gain.shape[1]
    bias_share = biases.shape[1]
    mine = jnp.arange(8) == tensor_rank

    qkv_flat = w_qkv.reshape(LAYERS, share, 3 * head_cols)
    vectors = jnp.concatenate([norm_gain.reshape(-1), biases.reshape(-1)])
    rows = 16
    vectors = jnp.pad(vectors, (0, rows * 3 * head_cols - vectors.size)).reshape(rows, -1)
    first = jnp.concatenate([qkv_flat[0], vectors], axis=0)
    first = jnp.broadcast_to(first, (owners, *first.shape))
    columns = after(cotangent.reshape(-1, cotangent.shape[-1]), first)
    first = exchange(first, OWNERS)
    both_zero = lax.all_gather(
        jnp.concatenate([w_fc1[0], w_fc2[0], w_dense[0]], axis=1), OWNERS, axis=0, tiled=True
    )
    pieces = gathered(columns)
    heads_one = lax.all_gather(
        jnp.concatenate([qkv_flat[1], w_dense[1]], axis=1), OWNERS, axis=0, tiled=True
    )
    feed_one = lax.all_gather(
        jnp.concatenate([w_fc1[1], w_fc2[1]], axis=1), OWNERS, axis=0, tiled=True
    )
    qkv_zero = first[:, :share].reshape(D, 3 * head_cols)
    vectors = first[:, share:].reshape(owners, -1)[:, : LAYERS * (gain_share + bias_share)]
    gain_vecs = vectors[:, : LAYERS * gain_share].reshape(owners, LAYERS, -1).astype(jnp.float32)
    bias_vecs = vectors[:, LAYERS * gain_share :].reshape(owners, LAYERS, -1).astype(jnp.float32)
    qkv_places = [(qkv_zero, 0), (heads_one, 0)]
    dense_places = [(both_zero, 8), (heads_one, 3)]
    fc1_places = [(both_zero, 0), (feed_one, 0)]
    fc2_places = [(both_zero, 1), (feed_one, 1)]
    fc1_weights = [both_zero[:, :hidden_cols], feed_one[:, :hidden_cols]]
    fc2_weights = [both_zero[:, hidden_cols : 2 * hidden_cols], feed_one[:, hidden_cols:]]

    pairs, qkv_biases, fc1_biases, outer_biases = ([], [], [], [])
    for l in range(LAYERS):
        vec = bias_vecs[:, l].reshape(-1)
        pairs.append((gain_vecs[:, l].reshape(2, D), vec[: 2 * D].reshape(2, D)))
        bias = vec[2 * D : 5 * D].reshape(3, 8, head_cols)
        bias = lax.dynamic_index_in_dim(bias, tensor_rank, 1, False)
        qkv_biases.append(bias.reshape(1, 3 * head_cols))
        bias = vec[6 * D : 6 * D + FF].reshape(8, hidden_cols)
        fc1_biases.append(lax.dynamic_index_in_dim(bias, tensor_rank, 0, True))
        outer_biases.append((vec[5 * D : 6 * D] + vec[6 * D + FF :]).reshape(1, D))

    segments = lax.dynamic_index_in_dim(segment_ids, seq_rank // 2, 0, False)
    earlier = jnp.zeros_like(segments)
    for doc in range(1, DOCUMENTS):
        before = jnp.sum((segments < doc).astype(jnp.int32))
        earlier = jnp.where(segments == doc, before, earlier)
    places = jnp.arange(full_len, dtype=jnp.int32) - earlier
    half_rot = ROT // 2
    inverse = 10000.0 ** (-jnp.arange(half_rot, dtype=jnp.float32) * 2.0 / ROT)
    angles = inverse[:, None] * places.astype(jnp.float32)[None, :]
    table = jnp.concatenate([jnp.cos(angles), jnp.sin(angles)], axis=0)
    starts = earlier[None, :]

    def feed_forward(normed_two, l):
        pre_act = dot(normed_two, fc1_weights[l], ((1,), (0,))) + fc1_biases[l]
        return gelu_and_slope(pre_act)

    def pre_gradient(grad_low, slope, l):
        return low(dot(grad_low, fc2_weights[l], ((1,), (0,))) * slope)

    tokens = inputs.reshape(-1, D)
    residual = own_rows(tokens, along_z, core).astype(jnp.float32)

    one_zero, two_zero, payload = project(
        spot, (tokens,), pairs[0], (first, 0), qkv_biases[0], (pieces[1],)
    )
    packed_zero = exchange(payload, "seq")
    prepared = (*pairs[1], qkv_biases[1], fc1_biases[1], outer_biases[0], outer_biases[1])
    result, *kept_zero = attend(core_ref, packed_zero, table, starts, prepared)
    heads_zero = exchange(result, "seq")
    hidden_zero, slope_zero = feed_forward(two_zero, 0)
    partial = branch_sums(spot, hidden_zero, heads_zero, fc2_places[0], dense_places[0])
    terms = z_terms(half_sum(*partial))
    residual, hat, scale, hat_low = settled(terms, residual, outer_biases[0])
    grad_top, upper_payload = top_gradient(spot, pieces, dense_places[1])
    upper = exchange(upper_payload, "seq")
    hat_pieces = gathered(hat_low, (upper,))

    one, two, payload = project(
        spot, hat_pieces, pairs[1], qkv_places[1], qkv_biases[1], ()
    )
    packed = exchange(payload, "seq")

    back = attend_both(core_ref, packed, table, starts, upper)
    grad_heads = exchange(back, "seq")
    two = after(two, back)
    hidden, slope = feed_forward(two, 1)
    grad_pre = pre_gradient(grad_top, slope, 1)
    feed_grads, feed_product, feed_shift, feed_sums = feed_gradient(
        spot, two, grad_top, grad_pre, hidden, fc1_places[1], work=(back,)
    )
    shares_feed = lax.psum_scatter(feed_grads, OWNERS, scatter_dimension=0, tiled=True)
    half = half_sum(
        *norm_gradient(
            spot,
            grad_heads,
            grad_pre,
            qkv_places[1],
            fc1_places[1],
            pairs[1][0],
            work=(feed_sums,),
        )
    )
    terms = z_terms(half)
    weight_grads, heads_product, heads_shift, heads_sums = heads_gradient(
        spot, one, grad_heads, qkv_places[1], grad_top, grad_heads, (half[0],)
    )
    partial = branch_sums(
        spot, hidden, grad_heads, fc2_places[1], dense_places[1], (half[0],), 0
    )
    own_top = own_rows(grad_top, along_z, 0)
    grad_own = through_norm(terms, own_top, hat, scale)
    sums_one = (
        (heads_product, feed_product),
        (heads_shift, feed_shift),
        heads_sums,
        feed_sums,
        jnp.sum(own_top.astype(jnp.float32), axis=0),
    )
    grad_low, upper_payload = top_gradient(
        spot, gathered(after(grad_own, heads_shift, partial[0])), dense_places[0]
    )

    upper = exchange(upper_payload, "seq")
    grad_pre = pre_gradient(grad_low, slope_zero, 0)
    weight_grads, feed_product, feed_shift, feed_sums = feed_gradient(
        spot,
        two_zero,
        grad_low,
        grad_pre,
        hidden_zero,
        fc1_places[0],
        heads_zero,
        weight_grads,
        (upper_payload,),
    )
    shares_more = lax.psum_scatter(weight_grads, OWNERS, scatter_dimension=0, tiled=True)
    back = attend_back(
        core_ref, packed_zero, table, starts, *kept_zero, upper, (feed_sums,)
    )
    grad_heads = exchange(back, "seq")
    half = half_sum(partial[0], after(partial[1], back))
    final = residual + (z_sum(half) + outer_biases[1])
    blocks = norm_gradient(
        spot,
        grad_heads,
        grad_pre,
        qkv_places[0],
        fc1_places[0],
        pairs[0][0],
        tokens,
    )
    qkv_grads, heads_product, heads_shift, heads_sums = heads_gradient(
        spot, one_zero, grad_heads, qkv_places[0], work=(blocks[0], final), tiled=share + rows
    )
    sums_zero = (
        (heads_product, feed_product),
        (heads_shift, feed_shift),
        heads_sums,
        feed_sums,
        jnp.sum(grad_own.astype(jnp.float32), axis=0),
    )

    def small_gradients(l, products, shift_grads, head_sums, pre_sums, own_sums):
        gain, shift = pairs[l]
        shift_grad = jnp.concatenate(shift_grads, axis=1)
        product = jnp.concatenate(products, axis=1)
        gain_grad = (product - shift.reshape(1, -1) * shift_grad) / gain.reshape(1, -1)
        placed_heads = jnp.where(mine[:, None], head_sums.reshape(3, 1, head_cols), 0.0)
        placed_pre = jnp.where(mine[:, None], pre_sums, 0.0)
        own_sums = own_sums.reshape(1, -1)
        bias_grad = jnp.concatenate(
            [
                shift_grad,
                placed_heads.reshape(1, -1),
                own_sums,
                placed_pre.reshape(1, -1),
                own_sums,
            ],
            axis=1,
        )
        return [bias_grad.reshape(owners, bias_share), gain_grad.reshape(owners, gain_share)]

    small = jnp.concatenate(
        [*small_gradients(0, *sums_zero), *small_gradients(1, *sums_one)], axis=1
    )
    small = jnp.pad(small, ((0, 0), (0, rows * 3 * head_cols - small.shape[1])))
    small = low(small).reshape(owners, rows, -1)
    tiles = lax.dynamic_update_slice(qkv_grads, small, (0, share, 0))
    out_pieces = gathered(low(final), late=(tiles,))
    block_out = joined(spot, *out_pieces).reshape(inputs.shape)
    half = half_sum(*blocks)
    change = z_sum((half[0], after(half[1], block_out), *half[2:]))
    columns = lax.dynamic_slice_in_dim(grad_low, tensor_rank * (D // 8), D // 8, 1)
    grad_inputs = swapped(columns, core).astype(jnp.float32) + change
    grad_inputs = grad_inputs.reshape(cotangent.shape)
    tiles = jnp.sum(exchange(tiles, OWNERS).astype(jnp.float32), axis=0)
    small = tiles[share:].reshape(-1)[: LAYERS * (gain_share + bias_share)]
    small = jnp.sum(sent_to_all(small, "tensor"), axis=0).reshape(LAYERS, -1)
    feed = shares_feed.astype(jnp.float32)
    more = shares_more.astype(jnp.float32)
    grad_qkv = jnp.stack([tiles[:share], more[:, 1152:1536]])
    grad_dense = jnp.stack([more[:, 1024:1152], more[:, 1536:]])
    grad_fc1 = jnp.stack([more[:, :hidden_cols], feed[:, :hidden_cols]])
    grad_fc2 = jnp.stack([more[:, hidden_cols : 2 * hidden_cols], feed[:, hidden_cols:]])
    return (
        block_out,
        grad_inputs,
        grad_qkv.reshape(w_qkv.shape),
        grad_dense,
        grad_fc1,
        grad_fc2,
        small[:, bias_share:],
        small[:, :bias_share],
    )


def solution(mesh):
    in_specs = (
        P("dp", "seq", None),
        P(None, ("dp", "seq"), None, "tensor"),
        P(None, ("dp", "seq"), "tensor"),
        P(None, ("dp", "seq"), "tensor"),
        P(None, ("dp", "seq"), "tensor"),
        P(None, ("dp", "seq")),
        P(None, ("dp", "seq")),
        P("dp", None),
        P("dp", "seq", "tensor"),
    )
    out_specs = (
        P("dp", "seq", None),
        P("dp", "seq", "tensor"),
        P(None, ("dp", "seq"), None, "tensor"),
        P(None, ("dp", "seq"), "tensor"),
        P(None, ("dp", "seq"), "tensor"),
        P(None, ("dp", "seq"), "tensor"),
        P(None, ("dp", "seq")),
        P(None, ("dp", "seq")),
    )
    return jax.shard_map(shards, mesh=mesh, in_specs=in_specs, out_specs=out_specs, check_vma=False)
```
